128 devices in a mesh: seg: 16 (over y, z), head: 8 (over x, core).
Axes of the slice: x: 4, y: 4, z: 4, core: 2. Of those that a mesh axis runs over, the one named last changes fastest.
Arguments:
- ssm_input: bfloat16 [3, 16, 1536, 3072], P(None, 'seg', None, 'head'), may hold values from -6 to 6
- gate_input: bfloat16 [3, 16, 1536, 3072], P(None, 'seg', None, 'head'), may hold values from -300 to 300
- b_input: bfloat16 [3, 16, 1536, 256], P(None, 'seg'), may hold values from -0.375 to 0.375
- c_output: bfloat16 [3, 16, 1536, 256], P(None, 'seg'), may hold values from -0.375 to 0.375
- log_decay: float32 [3, 16, 24, 1536], P(None, 'seg', 'head'), may hold values from 0 to 1, as said below
- root_state: float32 [16, 24, 128, 256], P('seg', 'head'), may hold values from -12 to 12
- norm_gain: float32 [3072], P('head'), may hold values from 0.1 to 1.9
- out_grad: bfloat16 [3, 16, 1536, 3072], P(None, 'seg', None, 'head'), may hold values from -6 to 6
- parent_ids: int32 [2, 16], replicated, may hold values from 0 to 15
Outputs:
- input_grad: bfloat16 [3, 16, 1536, 3072], P(None, 'seg', None, 'head')
- state_grad: float32 [3, 16, 24, 128, 256], P(None, 'seg', 'head')
The draws below stay inside these ranges and needn't reach their ends.
Inputs may be any that keep to these rules, and one draw needn't show every extreme that they name: parent_ids[0, j] is the level-0 parent of level-1 segment j and parent_ids[1, j] the level-1 parent of level-2 segment j; a segment may have any number of children. `log_decay`: positive decay rates.
All inputs are finite; a program needn't handle non-finite values.
Results may differ from the reference program's by a relative error of at most 0.0062.
Values sent between devices are 32-bit elements; how exact they have to be, the bound alone decides.
No kernel may reach another device: no remote copies, remote signals or barrier semaphores. Data moves between devices by JAX's collectives and lax.ppermute only.
A program may use at most 192 MiB of HBM per device.

```python
import math
import jax
import jax.numpy as jnp
import numpy as np
from jax import lax

LEVELS = 3
PIECE_POSITIONS = 1536
BLOCK = 256
HEADS = 24
HDIM = 128
STATE = 256
SEGS = 16


def draw_gate_input(key, part):
    key = jax.random.fold_in(key, 11)
    key_base, key_column, key_token = jax.random.split(key, 3)
    columns = HEADS * HDIM
    tensor_extent = (LEVELS, SEGS, PIECE_POSITIONS, columns)
    center_level = jax.random.normal(key_base, tensor_extent, jnp.float32)
    ramp = 3.0 ** (jnp.arange(columns, dtype=jnp.float32) / columns)
    jitter = jnp.exp(jax.random.uniform(key_column, (columns,), jnp.float32, -0.35, 0.35))
    tokenwise = jnp.exp(jax.random.uniform(key_token, (LEVELS, SEGS, PIECE_POSITIONS, 1), jnp.float32, 0.0, math.log(10.0)))
    return (center_level * ramp * jitter * tokenwise).astype(jnp.bfloat16)


def draw_log_decay(key, part):
    key = jax.random.fold_in(key, 23)
    sampler_seeds = jax.random.split(key, 7)
    tensor_extent = (LEVELS, SEGS, HEADS, PIECE_POSITIONS)
    keep_share = 0.5
    jagged_multiplier = jnp.exp(jax.random.uniform(sampler_seeds[4], tensor_extent, jnp.float32, math.log(0.5), math.log(2.0)))
    slow = jax.random.uniform(sampler_seeds[0], (HEADS,), jnp.float32) < keep_share
    fast_rate = jnp.exp(jax.random.uniform(sampler_seeds[1], (HEADS,), jnp.float32, math.log(1.0 / 50.0), math.log(1.0 / 30.0)))
    slow_rate = jnp.exp(jax.random.uniform(sampler_seeds[2], (HEADS,), jnp.float32, math.log(0.02), math.log(0.2))) / (LEVELS * PIECE_POSITIONS)
    center_level = jnp.where(slow, slow_rate, fast_rate)
    dispersion_multiplier = jnp.exp(jax.random.uniform(sampler_seeds[3], (LEVELS, SEGS, 1, 1), jnp.float32, math.log(0.5), math.log(2.0)))
    spike_multiplier = jax.random.uniform(sampler_seeds[5], tensor_extent, jnp.float32) < 1.0 / PIECE_POSITIONS
    objective_scalar = jax.random.uniform(sampler_seeds[6], tensor_extent, jnp.float32, 0.22, 0.7)
    return center_level[None, None, :, None] * dispersion_multiplier * jagged_multiplier + jnp.where(spike_multiplier, objective_scalar, 0.0)


def plant(result, rng, low, high):
    longest = result.shape.index(max(result.shape))
    spots = []
    for shift in (0, 1):
        where = [jax.random.randint(jax.random.fold_in(rng, axis), (), 0, length) for axis, length in enumerate(result.shape)]
        where[longest] = (where[longest] + shift) % result.shape[longest]
        spots.append(tuple(where))
    return result.at[spots[0]].set(low).at[spots[1]].set(high)


def block_scale(stream_key, shape, cuts, least, high):
    level = 1.0
    for dim, blocks in cuts:
        heights = jax.random.uniform(jax.random.fold_in(jax.random.fold_in(stream_key, 6), dim), (blocks,), jnp.float32, least / len(cuts), high / len(cuts))
        level = level * jnp.repeat(jnp.exp(heights), shape[dim] // blocks).reshape((-1,) + (1,) * (len(shape) - 1 - dim))
    return level


def cumulative_ranks(count, lean):
    portions = [(1 << 20) // math.isqrt(grade ** lean) + 1 for grade in range(1, count + 1)]
    spread = 1 + sum(portions) // (1 << 30)
    return np.cumsum(np.array([max(1, weight // spread) for weight in portions]))


def ranked_ids(own_key, shape, count, lean):
    listing = cumulative_ranks(count, lean)
    ticket = jax.random.randint(jax.random.fold_in(own_key, 1), shape, 0, int(listing[count - 1]))
    rank = jnp.searchsorted(jnp.asarray(listing, jnp.int32), ticket, side="right")
    return jax.random.permutation(jax.random.fold_in(own_key, 2), count)[rank].astype(jnp.int32)


def gaussian(key, dims, scale, limit, cuts=(), kind=jnp.bfloat16):
    array = scale * jax.random.normal(key, dims, jnp.float32)
    if cuts:
        array = array * block_scale(key, dims, cuts, -0.22, 0.18)
    return jnp.clip(array, -limit, limit).astype(kind)


def setup_inputs(seed: int = 0) -> dict:
    arg_keys = jax.random.split(jax.random.key(seed), 10)
    ssm_input = gaussian(arg_keys[0], (LEVELS, SEGS, PIECE_POSITIONS, HEADS * HDIM), 1.0, 6.0, ((1, 16), (3, 8)))
    gate_input = draw_gate_input(jax.random.fold_in(arg_keys[9], 71), 0)
    b_input = gaussian(arg_keys[2], (LEVELS, SEGS, PIECE_POSITIONS, STATE), 0.0625, 0.375, ((1, 16),))
    c_output = gaussian(arg_keys[3], (LEVELS, SEGS, PIECE_POSITIONS, STATE), 0.0625, 0.375, ((1, 16),))
    log_decay = draw_log_decay(jax.random.fold_in(arg_keys[9], 71), 0)
    root_state = gaussian(arg_keys[5], (SEGS, HEADS, HDIM, STATE), 2.0, 12.0, ((0, 16), (1, 8)), jnp.float32)
    norm_gain = jnp.clip(1.0 + 0.18 * jax.random.normal(arg_keys[6], (HEADS * HDIM,), jnp.float32), 0.1, 1.9)
    out_grad = gaussian(arg_keys[7], (LEVELS, SEGS, PIECE_POSITIONS, HEADS * HDIM), 1.0, 6.0, ((1, 16), (3, 8)))
    parent_ids = plant(ranked_ids(arg_keys[8], (LEVELS - 1, SEGS), SEGS, 2), jax.random.fold_in(arg_keys[8], 3), 0, SEGS - 1).astype(jnp.int32)
    return dict(ssm_input=ssm_input, gate_input=gate_input, b_input=b_input, c_output=c_output, log_decay=log_decay, root_state=root_state, norm_gain=norm_gain, out_grad=out_grad, parent_ids=parent_ids)


EPSILON = 1e-05

def rounded(values):
    return lax.optimization_barrier(values.astype(jnp.bfloat16)).astype(jnp.float32)

def prep_segment(ssm_input, b_input, c_output, log_decay):
    length, columns = ssm_input.shape
    head_count = log_decay.shape[0]
    head_size = columns // head_count
    blocks = length // BLOCK
    cumulative = -jnp.cumsum(log_decay.reshape(head_count, blocks, BLOCK), axis=2)
    b_blocks = b_input.astype(jnp.float32).reshape(blocks, BLOCK, STATE)
    c_blocks = c_output.astype(jnp.float32).reshape(blocks, BLOCK, STATE)
    scores = jnp.einsum('ktn,kun->ktu', c_blocks, b_blocks)
    causal = jnp.arange(BLOCK)[:, None] >= jnp.arange(BLOCK)[None, :]
    exponent = jnp.where(causal, cumulative[..., :, None] - cumulative[..., None, :], 0.0)
    weights = rounded(jnp.where(causal, scores[None] * jnp.exp(exponent), 0.0))
    to_end = jnp.transpose(jnp.exp(cumulative[..., -1:] - cumulative), (1, 2, 0))[..., None]
    from_start = jnp.transpose(jnp.exp(cumulative), (1, 2, 0))[..., None]
    x_blocks = ssm_input.astype(jnp.float32).reshape(blocks, BLOCK, head_count, head_size)
    block_state = jnp.einsum('kuhp,kun->khpn', rounded(x_blocks * to_end), b_blocks)
    return (cumulative, weights, block_state, b_blocks, c_blocks, x_blocks, to_end, from_start)

def run_blocks(block_state, cumulative, start_state):
    factor = jnp.exp(cumulative[..., -1])
    entries = []
    current = start_state
    for number in range(block_state.shape[0]):
        entries.append(current)
        current = factor[:, number, None, None] * current + block_state[number]
    return (jnp.stack(entries), current)

def run_back(block_grad, cumulative, end_grad):
    factor = jnp.exp(cumulative[..., -1])
    exit_grads = []
    current = end_grad
    for number in range(block_grad.shape[0] - 1, -1, -1):
        exit_grads.insert(0, current)
        current = block_grad[number] + factor[:, number, None, None] * current
    return (jnp.stack(exit_grads), current)

def forward_segment(ssm_input, gate_input, b_input, c_output, log_decay, norm_gain, out_grad, start_state):
    cumulative, weights, block_state, b_blocks, c_blocks, x_blocks, to_end, from_start = prep_segment(ssm_input, b_input, c_output, log_decay)
    entries, end_state = run_blocks(block_state, cumulative, start_state)
    within = jnp.einsum('hktu,kuhp->kthp', weights, x_blocks)
    carried = jnp.einsum('ktn,khpn->kthp', c_blocks, rounded(entries)) * from_start
    ssm_out = (within + carried).reshape(ssm_input.shape)
    gate_act = jax.nn.silu(gate_input.astype(jnp.float32))
    gated_out = ssm_out * gate_act
    scaled = out_grad.astype(jnp.float32) * norm_gain
    inv_rms = lax.rsqrt(lax.optimization_barrier(jnp.mean(gated_out * gated_out, axis=-1, keepdims=True)) + EPSILON)
    dot_term = lax.optimization_barrier(jnp.mean(scaled * gated_out, axis=-1, keepdims=True))
    ssm_grad = ((inv_rms * scaled - gated_out * inv_rms * inv_rms * inv_rms * dot_term) * gate_act).astype(jnp.bfloat16)
    return (ssm_grad, end_state)

def backward_segment(ssm_input, b_input, c_output, log_decay, ssm_grad, end_grad):
    cumulative, weights, block_state, b_blocks, c_blocks, x_blocks, to_end, from_start = prep_segment(ssm_input, b_input, c_output, log_decay)
    grad_blocks = ssm_grad.astype(jnp.float32).reshape(x_blocks.shape)
    block_grad = jnp.einsum('kthp,ktn->khpn', rounded(grad_blocks * from_start), c_blocks)
    exit_grads, state_grad = run_back(block_grad, cumulative, end_grad)
    within = jnp.einsum('hktu,kthp->kuhp', weights, grad_blocks)
    carried = jnp.einsum('khpn,kun->kuhp', rounded(exit_grads), b_blocks) * to_end
    return ((within + carried).reshape(ssm_input.shape).astype(jnp.bfloat16), state_grad)

def reference(ssm_input, gate_input, b_input, c_output, log_decay, root_state, norm_gain, out_grad, parent_ids):
    start_state = root_state
    ssm_grads = []
    for depth in range(LEVELS):

        def per_segment(items):
            return forward_segment(items[0], items[1], items[2], items[3], items[4], norm_gain, items[5], items[6])
        ssm_grad, end_state = lax.map(per_segment, (ssm_input[depth], gate_input[depth], b_input[depth], c_output[depth], log_decay[depth], out_grad[depth], start_state))
        ssm_grads.append(ssm_grad)
        if depth + 1 < LEVELS:
            start_state = jnp.take(end_state, parent_ids[depth], axis=0)
    input_grads = [None] * LEVELS
    state_grads = [None] * LEVELS
    end_grad = jnp.zeros_like(root_state)
    for depth in range(LEVELS - 1, -1, -1):

        def per_back(items):
            return backward_segment(items[0], items[1], items[2], items[3], items[4], items[5])
        input_grads[depth], state_grads[depth] = lax.map(per_back, (ssm_input[depth], b_input[depth], c_output[depth], log_decay[depth], ssm_grads[depth], end_grad))
        if depth > 0:
            end_grad = jax.ops.segment_sum(state_grads[depth], parent_ids[depth - 1], num_segments=SEGS)
    return (jnp.stack(input_grads), jnp.stack(state_grads))
```

```python
import functools
import math

import jax
import jax.numpy as jnp
from jax import lax
from jax.experimental import pallas as pl
from jax.experimental.pallas import tpu as pltpu
from jax.sharding import PartitionSpec as P

BLOCK = 256
HALF = BLOCK // 2
HEADS = 24
HDIM = 128
STATE = 256
CHUNK = 3
SPAN = CHUNK * BLOCK
FOLD = SPAN // 2
EPSILON = 1e-05
VMEM_LIMIT = 24 * 1024 * 1024
LOG2E = math.log2(math.e)

WIDTH = 8 * CHUNK
CUM = 0
FROM_BLOCK = WIDTH
TO_BLOCK = 2 * WIDTH
FROM_LEVEL = 3 * WIDTH
TO_LEVEL = 4 * WIDTH

F32 = jnp.float32
BF16 = jnp.bfloat16
shaped = jax.ShapeDtypeStruct
pin = pltpu.with_memory_space_constraint


def call(body, name, micros, **kwargs):
    return pl.pallas_call(
        body,
        name=name,
        compiler_params=pltpu.CompilerParams(vmem_limit_bytes=VMEM_LIMIT),
        cost_estimate=pl.CostEstimate(
            flops=int(micros * 1e9), bytes_accessed=int(micros * 3e6), transcendentals=0
        ),
        **kwargs,
    )


def whole(array):
    rank = len(array.shape)
    return pl.BlockSpec(array.shape, lambda *_: (0,) * rank)


def dot(left, right, left_dim, right_dim, precision=None):
    return lax.dot_general(
        left,
        right,
        (((left_dim,), (right_dim,)), ((), ())),
        precision=precision,
        preferred_element_type=F32,
    )


def spread(packed, group, j, heads):
    at = group + 8 * j
    return jnp.concatenate(
        [
            jnp.broadcast_to(packed[:, at + h : at + h + 1], (packed.shape[0], HDIM))
            for h in range(heads)
        ],
        axis=1,
    )


def block(j):
    return slice(j * BLOCK, (j + 1) * BLOCK)


def head(h):
    return slice(h * HDIM, (h + 1) * HDIM)


def turn(values):
    size = values.shape[0]
    unit = lax.broadcasted_iota(jnp.int32, (size, size), 0) == lax.broadcasted_iota(
        jnp.int32, (size, size), 1
    )
    return dot(jnp.where(unit, 1.0, 0.0).astype(BF16), values, 1, 1).astype(BF16)


def silu(values):
    half = 0.5 * values
    return half + half * jnp.tanh(half)


def scatter_pieces(send, number, state, heads):
    rows = STATE // send.shape[0]
    for piece in range(send.shape[0]):
        for h in range(heads):
            at = (number * heads + h) * rows
            send[piece, at : at + rows] = state[piece * rows : (piece + 1) * rows, head(h)]


def gather_pieces(got, number, h, heads):
    rows = STATE // got.shape[0]
    at = (number * heads + h) * rows
    return got[:, at : at + rows].reshape(STATE, HDIM)


def start_all(copies):
    for copy in copies:
        copy.start()


def wait_all(copies):
    for copy in copies:
        copy.wait()


def piece_copies(sources, targets, sems, pieces):
    result = []
    for i, (at, first, count) in enumerate(pieces):
        rows = pl.ds(first * BLOCK, count * BLOCK)
        result.append(
            [
                pltpu.make_async_copy(source(at, rows), target.at[at, rows], sems.at[i, a])
                for a, (source, target) in enumerate(zip(sources, targets))
            ]
        )
    return result


def block_ends(parts):
    lasts = [part[:, BLOCK - 1 :] for part in parts]
    before = [jnp.zeros((8, 1), F32)]
    for last in lasts[:-1]:
        before.append(before[-1] + last)
    after = [jnp.zeros((8, 1), F32)]
    for last in lasts[:0:-1]:
        after.insert(0, after[0] + last)
    return lasts, before, after


def states_body(heads, steps, decay_hbm, root_hbm, x_hbm, b_hbm, send_out, rows_ref, rates, decay,
                send, root, x, b, decay_sem, root_sem, sems, out_sems):
    chunks = rows_ref.shape[0]
    blocks = steps * CHUNK
    decay_copy = pltpu.make_async_copy(decay_hbm, decay, decay_sem)
    decay_copy.start()
    pieces = [(0, 0, CHUNK), (0, CHUNK, CHUNK), (1, 0, CHUNK), (1, CHUNK, CHUNK)]
    copies = piece_copies(
        [lambda at, span: x_hbm.at[at, 0, span], lambda at, span: b_hbm.at[at, 0, span]],
        [x, b],
        sems,
        pieces,
    )
    root_copy = pltpu.make_async_copy(root_hbm.at[0], root, root_sem)
    start_all(copies[0])
    root_copy.start()
    for some in copies[1:]:
        start_all(some)

    rates[...] = jnp.zeros_like(rates)
    decay_copy.wait()
    for level in range(decay.shape[0]):
        for number in range(blocks):
            for h in range(heads):
                row = 8 * (level * blocks + number) + h
                rates[row : row + 1] = decay[level, h, :, block(number)]
    upper = (
        lax.broadcasted_iota(jnp.int32, (BLOCK, BLOCK), 0)
        <= lax.broadcasted_iota(jnp.int32, (BLOCK, BLOCK), 1)
    )
    upper = jnp.where(upper, 1.0, 0.0).astype(BF16)
    rest = rates[...]
    sums = jnp.zeros_like(rest)
    for _ in range(3):
        part = rest.astype(BF16)
        rest = rest - part.astype(F32)
        sums = sums + dot(part, upper, 1, 0)
    sums = sums * -LOG2E
    for chunk in range(chunks):
        rows_ref[chunk] = sums[WIDTH * chunk : WIDTH * (chunk + 1)]

    lines = []
    totals = []
    for level in range(2):
        numbers = range(level * blocks, (level + 1) * blocks)
        parts = [sums[8 * number : 8 * number + 8] for number in numbers]
        lasts, _, after = block_ends(parts)
        for part, last, suffix in zip(parts, lasts, after):
            lines.append(jnp.exp2(last - part + suffix))
        totals.append(jnp.exp2(after[0] + lasts[0]))
    lines.append(jnp.zeros((128 - 16 * blocks, BLOCK), F32))
    to_level = jnp.concatenate(lines, axis=0).T

    root_copy.wait()
    state = jnp.concatenate([(root[h] * totals[0][h : h + 1]).T for h in range(heads)], axis=1)
    half = heads * STATE // send.shape[0]
    outs = []
    for i, (level, first, count) in enumerate(pieces):
        if (level, first) == (1, 0):
            scatter_pieces(send, 0, state, heads)
            part = pl.ds(0, half)
            outs.append(
                pltpu.make_async_copy(send.at[:, part], send_out.at[:, part], out_sems.at[0])
            )
            outs[0].start()
            state = jnp.zeros((STATE, heads * HDIM), F32)
        wait_all(copies[i])
        for number in range(first, first + count):
            at = 8 * (level * blocks + number)
            scale = jnp.concatenate(
                [
                    jnp.broadcast_to(to_level[:, at + h : at + h + 1], (BLOCK, HDIM))
                    for h in range(heads)
                ],
                axis=1,
            )
            decayed = (x[level, block(number)].astype(F32) * scale).astype(BF16)
            state = state + dot(turn(b[level, block(number)]), decayed, 1, 0)
    scatter_pieces(send, 1, state, heads)
    decays = jnp.broadcast_to(totals[1], (8, HDIM))
    for piece in range(send.shape[0]):
        send[piece, send.shape[1] - 8 :] = decays
    part = pl.ds(half, send.shape[1] - half)
    outs.append(pltpu.make_async_copy(send.at[:, part], send_out.at[:, part], out_sems.at[1]))
    outs[1].start()
    wait_all(outs)


def pack(rows, packed):
    steps = packed.shape[0]
    parts = [rows[step, 8 * j : 8 * j + 8] for step in range(steps) for j in range(CHUNK)]
    lasts, before, after = block_ends(parts)
    for step in range(steps):
        mine = slice(step * CHUNK, (step + 1) * CHUNK)
        part = rows[step]
        last = jnp.concatenate(lasts[mine], axis=0)
        packed[step] = jnp.concatenate(
            [
                part,
                jnp.exp2(part),
                jnp.exp2(last - part),
                jnp.exp2(jnp.concatenate(before[mine], axis=0) + part),
                jnp.exp2(last - part + jnp.concatenate(after[mine], axis=0)),
                jnp.zeros((128 - 5 * WIDTH, BLOCK), F32),
            ],
            axis=0,
        ).T


def pick_body(heads, parent_ref, got_ref, send_out, send, sems):
    segments = got_ref.shape[0]
    rows = STATE // segments
    pair = send.shape[1]
    half = pair // 2
    quarter = segments // 4
    copies = []
    for seg in range(segments):
        first = parent_ref[0, seg]
        second = parent_ref[1, seg]
        root = parent_ref[0, second]
        send[seg, :half] = got_ref[first, :half]
        decay = got_ref[second, pair : pair + 8]
        for h in range(heads):
            a = slice(h * rows, (h + 1) * rows)
            b = slice(half + h * rows, half + (h + 1) * rows)
            send[seg, b] = decay[h : h + 1] * got_ref[root, a] + got_ref[second, b]
        if (seg + 1) % quarter == 0:
            part = pl.ds(seg + 1 - quarter, quarter)
            copies.append(
                pltpu.make_async_copy(send.at[part], send_out.at[part], sems.at[len(copies)])
            )
            copies[-1].start()
    wait_all(copies)


def fold_body(heads, parent_ref, decay_ref, got_ref, send_out, send, sems):
    rows = STATE // got_ref.shape[0]
    half = send.shape[1] // 2
    send[...] = jnp.zeros_like(send)
    copies = [
        pltpu.make_async_copy(send.at[:, part], send_out.at[:, part], sems.at[i])
        for i, part in enumerate([pl.ds(0, half), pl.ds(half, half)])
    ]
    for seg in range(got_ref.shape[0]):
        second = parent_ref[1, seg]
        send[second, :half] += got_ref[seg, :half]
    copies[0].start()
    for seg in range(got_ref.shape[0]):
        first = parent_ref[0, seg]
        decay = decay_ref[seg]
        for h in range(heads):
            a = slice(h * rows, (h + 1) * rows)
            b = slice(half + h * rows, half + (h + 1) * rows)
            send[first, b] += decay[h : h + 1] * send[seg, a] + got_ref[seg, b]
    copies[1].start()
    wait_all(copies)


def causal_mask(transposed):
    first = lax.broadcasted_iota(jnp.int32, (HALF, HALF), 0)
    second = lax.broadcasted_iota(jnp.int32, (HALF, HALF), 1)
    return first <= second if transposed else first >= second


def weighted(heads, j, rows, packed, x, b, c):
    scores = dot(c, b, 1, 1)
    causal = causal_mask(False)
    results = []
    for h in range(heads):
        row = rows[8 * j + h : 8 * j + h + 1]
        col = packed[:, CUM + 8 * j + h : CUM + 8 * j + h + 1]
        first = jnp.where(causal, col[:HALF] - row[:, :HALF], -jnp.inf)
        last = jnp.where(causal, col[HALF:] - row[:, HALF:], -jnp.inf)
        across = col[HALF:] - row[:, :HALF]
        top = jnp.concatenate(
            [(scores[:HALF, :HALF] * jnp.exp2(first)).astype(BF16), jnp.zeros((HALF, HALF), BF16)],
            axis=1,
        )
        bottom = jnp.concatenate(
            [
                (scores[HALF:, :HALF] * jnp.exp2(across)).astype(BF16),
                (scores[HALF:, HALF:] * jnp.exp2(last)).astype(BF16),
            ],
            axis=1,
        )
        results.append(dot(jnp.concatenate([top, bottom], axis=0), x[:, head(h)], 1, 0))
    return jnp.concatenate(results, axis=1)


def weighted_back(heads, j, rows, packed, grad, b, c):
    scores = dot(b, c, 1, 1)
    causal = causal_mask(True)
    results = []
    for h in range(heads):
        row = rows[8 * j + h : 8 * j + h + 1]
        col = packed[:, CUM + 8 * j + h : CUM + 8 * j + h + 1]
        first = jnp.where(causal, row[:, :HALF] - col[:HALF], -jnp.inf)
        last = jnp.where(causal, row[:, HALF:] - col[HALF:], -jnp.inf)
        across = row[:, HALF:] - col[:HALF]
        top = jnp.concatenate(
            [
                (scores[:HALF, :HALF] * jnp.exp2(first)).astype(BF16),
                (scores[:HALF, HALF:] * jnp.exp2(across)).astype(BF16),
            ],
            axis=1,
        )
        bottom = jnp.concatenate(
            [jnp.zeros((HALF, HALF), BF16), (scores[HALF:, HALF:] * jnp.exp2(last)).astype(BF16)],
            axis=1,
        )
        results.append(dot(jnp.concatenate([top, bottom], axis=0), grad[:, head(h)], 1, 0))
    return jnp.concatenate(results, axis=1)


def gated_sums(ssm_out, gate, out_grad, gain):
    gated = ssm_out * silu(gate.astype(F32))
    scaled = out_grad.astype(F32) * gain
    squares = jnp.sum(gated * gated, axis=1, keepdims=True)
    products = jnp.sum(scaled * gated, axis=1, keepdims=True)
    return gated, jnp.concatenate([squares, products, jnp.zeros((BLOCK, 6), F32)], axis=1).T


def store_sums(sums, step, at, pairs):
    both = jnp.concatenate(pairs, axis=1)
    for q in range(2):
        for half in range(2):
            sums[4 * step + 2 * q + half : 4 * step + 2 * q + half + 1, at : at + FOLD] = both[
                q : q + 1, half * FOLD : (half + 1) * FOLD
            ]


def norm_columns(total, step, at, features):
    lines = [total[4 * step + i : 4 * step + i + 1, at : at + FOLD] for i in range(4)]
    squares = jnp.concatenate(lines[:2], axis=1) / features
    dots = jnp.concatenate(lines[2:], axis=1) / features
    inv_rms = lax.rsqrt(squares + EPSILON)
    back = inv_rms * inv_rms * inv_rms * dots
    return jnp.concatenate([inv_rms, back, jnp.zeros((6, SPAN), F32)], axis=0).T


def ssm_gradient(j, norm, gain, gate, out_grad, gated):
    inv_rms, back = norm[block(j), 0:1], norm[block(j), 1:2]
    grad = inv_rms * (out_grad.astype(F32) * gain) - gated.astype(F32) * back
    return (grad * silu(gate.astype(F32))).astype(BF16)


def forward0_body(heads, steps, rows_ref, root_ref, gain_ref, x_ref, gate_ref, b_ref, c_ref,
                  out_grad_ref, gated_ref, sums_ref, state, packs):
    step = pl.program_id(0)

    @pl.when(step == 0)
    def _():
        pack(rows_ref, packs)
        for h in range(heads):
            state[:, head(h)] = root_ref[0, h].T

    rows, packed = rows_ref[step], packs[step]
    current = state[...]
    pairs = []
    for j in range(CHUNK):
        x, b, c = x_ref[0, 0, block(j)], b_ref[0, 0, block(j)], c_ref[0, 0, block(j)]
        within = weighted(heads, j, rows, packed, x, b, c)
        carried = dot(c, current.astype(BF16), 1, 0) * spread(packed, FROM_BLOCK, j, heads)
        gated, pair = gated_sums(
            within + carried, gate_ref[0, 0, block(j)], out_grad_ref[0, 0, block(j)], gain_ref[...]
        )
        gated_ref[0, block(j)] = gated.astype(BF16)
        pairs.append(pair)
        decayed = (x.astype(F32) * spread(packed, TO_BLOCK, j, heads)).astype(BF16)
        factor = spread(packed[BLOCK - 1 :], FROM_BLOCK, j, heads)
        current = current * factor + dot(turn(b), decayed, 1, 0)
    state[...] = current
    for part in range(steps):

        @pl.when(step == part)
        def _():
            store_sums(sums_ref, part, 0, pairs)


def local_body(heads, steps, rows_ref, x_ref, b_ref, c_ref, out_ref, turned_ref, state, packs):
    step = pl.program_id(1)

    @pl.when(step == 0)
    def _():
        pack(rows_ref, packs)
        state[...] = jnp.zeros_like(state)

    rows, packed = rows_ref[step], packs[step]
    current = state[...]
    for j in range(CHUNK):
        x, b, c = x_ref[0, 0, block(j)], b_ref[0, 0, block(j)], c_ref[0, 0, block(j)]
        within = weighted(heads, j, rows, packed, x, b, c)
        carried = dot(c, current.astype(BF16), 1, 0) * spread(packed, FROM_BLOCK, j, heads)
        out_ref[0, block(j)] = (within + carried).astype(BF16)
        turned_ref[0, block(j)] = turn(c)
        decayed = (x.astype(F32) * spread(packed, TO_BLOCK, j, heads)).astype(BF16)
        factor = spread(packed[BLOCK - 1 :], FROM_BLOCK, j, heads)
        current = current * factor + dot(turn(b), decayed, 1, 0)
    state[...] = current


def readout_body(heads, steps, local_hbm, gate_hbm, c_hbm, out_grad_hbm, turned_hbm, rows_hbm,
                 start_ref, gain_ref, first_sums_ref, gated_ref, gate, out_grad, turned, packed,
                 sums_out, local, c, rows, sums, sems, rows_sem, turned_sem, out_sem):
    rows_copy = pltpu.make_async_copy(rows_hbm.at[pl.ds(steps, 2 * steps)], rows, rows_sem)
    rows_copy.start()
    half = CHUNK * steps // 2
    pieces = [(0, 0, 1), (0, 1, 2), (0, half, half), (1, 0, half), (1, half, half)]
    copies = piece_copies(
        [
            lambda at, span: c_hbm.at[at + 1, 0, span],
            lambda at, span: local_hbm.at[at, span],
            lambda at, span: gate_hbm.at[at + 1, 0, span],
            lambda at, span: out_grad_hbm.at[at + 1, 0, span],
        ],
        [c, local, gate, out_grad],
        sems,
        pieces,
    )
    for some in copies:
        start_all(some)
    turned_copy = pltpu.make_async_copy(turned_hbm, turned, turned_sem)
    turned_copy.start()
    sums[0, :, :FOLD] = first_sums_ref[...]
    rows_copy.wait()
    for at in range(2):
        pack(rows.at[pl.ds(at * steps, steps)], packed.at[pl.ds(at * steps, steps)])
    pairs = []
    for i, (at, first, count) in enumerate(pieces):
        if first == 0:
            start = jnp.concatenate(
                [gather_pieces(start_ref, at, h, heads) for h in range(heads)], axis=1
            ).astype(BF16)
        wait_all(copies[i])
        for number in range(first, first + count):
            step, j = number // CHUNK, number % CHUNK
            place = block(number)
            carried = dot(c[at, place], start, 1, 0)
            carried = carried * spread(packed[at * steps + step], FROM_LEVEL, j, heads)
            gated, pair = gated_sums(
                carried + local[at, place].astype(F32),
                gate[at, place],
                out_grad[at, place],
                gain_ref[...],
            )
            gated_ref[at, place] = gated.astype(BF16)
            pairs.append(pair)
            if j == CHUNK - 1:
                store_sums(sums.at[0], step, (at + 1) * FOLD, pairs)
                pairs = []
    for copy in range(1, sums.shape[0]):
        sums[copy] = sums[0]
    out = pltpu.make_async_copy(sums, sums_out, out_sem)
    out.start()
    turned_copy.wait()
    out.wait()


def grads_body(heads, steps, features, packed_ref, turned_ref, gate_ref, out_grad_ref, gated_ref,
               total_ref, gain_ref, grad_out, send_out, grads, send, grad_sems, sems):
    total = jnp.sum(total_ref[...], axis=0)
    half = send.shape[1] // 2
    outs = []
    for at in (1, 0):
        state = jnp.zeros((STATE, heads * HDIM), F32)
        for step in range(steps):
            packed = packed_ref[at * steps + step]
            norm = norm_columns(total, step, (at + 1) * FOLD, features)
            for j in range(CHUNK):
                place = block(step * CHUNK + j)
                grad = ssm_gradient(
                    j,
                    norm,
                    gain_ref[...],
                    gate_ref[at, place],
                    out_grad_ref[at, place],
                    gated_ref[at, place],
                )
                grads[at, place] = grad
                decayed = (grad.astype(F32) * spread(packed, FROM_LEVEL, j, heads)).astype(BF16)
                state = state + dot(turned_ref[at, place], decayed, 1, 0)
            span = pl.ds(step * SPAN, SPAN)
            outs.append(
                pltpu.make_async_copy(
                    grads.at[at, span], grad_out.at[at, span], grad_sems.at[at * steps + step]
                )
            )
            outs[-1].start()
        scatter_pieces(send, 1 - at, state, heads)
        part = pl.ds((1 - at) * half, half)
        outs.append(pltpu.make_async_copy(send.at[:, part], send_out.at[:, part], sems.at[at]))
        outs[-1].start()
    wait_all(outs)


def back_chunk(heads, rows, packed, grad_of, b_ref, c_ref, state):
    current = state[...]
    for j in reversed(range(CHUNK)):
        b, c = b_ref[0, 0, block(j)], c_ref[0, 0, block(j)]
        grad = grad_of(j)
        within = weighted_back(heads, j, rows, packed, grad, b, c)
        carried = dot(b, current.astype(BF16), 1, 0) * spread(packed, TO_BLOCK, j, heads)
        yield j, (within + carried).astype(BF16)
        decayed = (grad.astype(F32) * spread(packed, FROM_BLOCK, j, heads)).astype(BF16)
        factor = spread(packed[BLOCK - 1 :], FROM_BLOCK, j, heads)
        current = current * factor + dot(turn(c), decayed, 1, 0)
    state[...] = current


def back0_body(heads, steps, features, rows_ref, gain_ref, total_ref, gate_ref, b_ref, c_ref,
               out_grad_ref, gated_ref, partial_ref, state_grad_ref, state, packs, norms):
    step = steps - 1 - pl.program_id(0)

    @pl.when(step == steps - 1)
    def _():
        pack(rows_ref, packs)
        total = jnp.sum(total_ref[...], axis=0)
        for part in range(steps):
            norms[part] = norm_columns(total, part, 0, features)
        state[...] = jnp.zeros_like(state)

    norm = norms[step]

    def grad_of(j):
        return ssm_gradient(
            j,
            norm,
            gain_ref[...],
            gate_ref[0, 0, block(j)],
            out_grad_ref[0, 0, block(j)],
            gated_ref[0, block(j)],
        )

    for j, part in back_chunk(heads, rows_ref[step], packs[step], grad_of, b_ref, c_ref, state):
        partial_ref[0, 0, block(j)] = part

    @pl.when(step == 0)
    def _():
        for h in range(heads):
            state_grad_ref[0, 0, h] = state[:, head(h)].T


def back_body(heads, steps, rows_ref, grad_ref, b_ref, c_ref, given_in, given_state, partial_ref,
              state_grad_ref, state, packs):
    step = steps - 1 - pl.program_id(1)

    @pl.when(step == steps - 1)
    def _():
        pack(rows_ref, packs)
        state[...] = jnp.zeros_like(state)

    def grad_of(j):
        return grad_ref[0, block(j)]

    for j, part in back_chunk(heads, rows_ref[step], packs[step], grad_of, b_ref, c_ref, state):
        partial_ref[0, 0, block(j)] = part

    @pl.when(step == 0)
    def _():
        for h in range(heads):
            state_grad_ref[0, 0, h] = state[:, head(h)].T


def inputs_body(heads, steps, b_hbm, partial_hbm, local_hbm, rows_hbm, end_ref, input_grad_out,
                state_grad_out, b, partial, grads, states, rows, packed, sems, local_sems,
                rows_sem, out_sems, state_sems):
    rows_copy = pltpu.make_async_copy(rows_hbm.at[pl.ds(0, 2 * steps)], rows, rows_sem)
    rows_copy.start()
    half = CHUNK * steps // 2
    pieces = [(1, 0, 1), (1, 1, 2), (1, half, half), (0, 0, half), (0, half, 2), (0, half + 2, 1)]
    copies = piece_copies(
        [lambda at, span: b_hbm.at[at, 0, span], lambda at, span: partial_hbm.at[at, 0, span]],
        [b, partial],
        sems,
        pieces,
    )
    locals_in = [
        pltpu.make_async_copy(local_hbm.at[level, 0], states.at[level], local_sems.at[level])
        for level in range(2)
    ]
    for i, (level, first, _) in enumerate(pieces):
        start_all(copies[i])
        if first == half:
            locals_in[level].start()
    rows_copy.wait()
    for level in range(2):
        pack(rows.at[pl.ds(level * steps, steps)], packed.at[pl.ds(level * steps, steps)])
    outs = []
    for i, (level, first, count) in enumerate(pieces):
        if first == 0:
            end = jnp.concatenate(
                [gather_pieces(end_ref, 1 - level, h, heads) for h in range(heads)], axis=1
            )
            rounded = end.astype(BF16)
        wait_all(copies[i])
        for number in range(first, first + count):
            place = block(number)
            extra = dot(b[level, place], rounded, 1, 0) * spread(
                packed[level * steps + number // CHUNK], TO_LEVEL, number % CHUNK, heads
            )
            grads[level, place] = (partial[level, place].astype(F32) + extra).astype(BF16)
        span = pl.ds(first * BLOCK, count * BLOCK)
        outs.append(
            pltpu.make_async_copy(
                grads.at[level, span], input_grad_out.at[level, 0, span], out_sems.at[i]
            )
        )
        outs[-1].start()
        if first == half:
            last = packed[(level + 1) * steps - 1, BLOCK - 1 :]
            total = spread(last, FROM_LEVEL, CHUNK - 1, heads)
            locals_in[level].wait()
            for h in range(heads):
                states[level, h] += (end[:, head(h)] * total[:, head(h)]).T
            outs.append(
                pltpu.make_async_copy(
                    states.at[level], state_grad_out.at[level, 0], state_sems.at[level]
                )
            )
            outs[-1].start()
    wait_all(outs)


def shards(features, head_devices, ssm_input, gate_input, b_input, c_output, log_decay,
           root_state, norm_gain, out_grad, parent_ids):
    levels, _, length, columns = ssm_input.shape
    heads = columns // HDIM
    blocks = length // BLOCK
    steps = blocks // CHUNK
    segments = parent_ids.shape[1]
    rows = STATE // segments
    gain = norm_gain.reshape(1, columns)
    decay = jnp.transpose(log_decay, (0, 2, 1, 3))

    smem = pl.BlockSpec(memory_space=pltpu.SMEM)
    vmem = pl.BlockSpec(memory_space=pltpu.VMEM)
    anywhere = pl.BlockSpec(memory_space=pl.ANY)
    rows_shape = (levels * steps, WIDTH, BLOCK)
    two_levels = (2 * steps, BLOCK, 128)
    pair_shape = (segments, 2 * heads * rows, HDIM)
    first_shape = (segments, 2 * heads * rows + 8, HDIM)
    sums_shape = (head_devices, 8, levels * FOLD)
    state_shape = (levels, 1, heads, HDIM, STATE)
    state_scratch = pltpu.VMEM((STATE, columns), F32)
    packs_scratch = pltpu.VMEM((steps, BLOCK, 128), F32)
    pair_scratch = pltpu.VMEM(pair_shape, F32)
    dma = pltpu.SemaphoreType.DMA

    far = lambda array: pin(array, pltpu.HBM)
    near = lambda array: pin(array, pltpu.VMEM)
    decay, x, gate, out_grad = far(decay), far(ssm_input), far(gate_input), far(out_grad)
    b, c, root = far(b_input), far(c_output), far(root_state)

    def pair_of_levels(width):
        return pltpu.VMEM((2, length, width), BF16)

    def tokens(width, place):
        return pl.BlockSpec((1, 1, SPAN, width), lambda *g: (place(*g)[0], 0, place(*g)[1], 0))

    def flat(width, place):
        return pl.BlockSpec((1, SPAN, width), lambda *g: (*place(*g), 0))

    def level_rows(place):
        return pl.BlockSpec((steps,) + rows_shape[1:], lambda *g: (place(*g)[0], 0, 0))

    def state_grads(place):
        return pl.BlockSpec((1, 1, heads, HDIM, STATE), lambda *g: (place(*g)[0], 0, 0, 0, 0))

    exchange = functools.partial(
        lax.all_to_all, axis_name="seg", split_axis=0, concat_axis=0, tiled=True
    )

    send, cum_rows = call(
        functools.partial(states_body, heads, steps),
        "states",
        6,
        in_specs=[anywhere] * 4,
        out_specs=[anywhere, vmem],
        out_shape=[pltpu.HBM(first_shape, F32), pltpu.HBM(rows_shape, F32)],
        scratch_shapes=[
            pltpu.VMEM((levels * blocks * 8, BLOCK), F32),
            pltpu.VMEM(decay.shape, F32),
            pltpu.VMEM(first_shape, F32),
            pltpu.VMEM(root_state.shape[1:], F32),
            pair_of_levels(columns),
            pair_of_levels(STATE),
            dma,
            dma,
            dma((4, 2)),
            dma((2,)),
        ],
    )(decay, root, x, b)
    got = exchange(send)

    own = lambda k: (0, k)
    gated0, sums0 = call(
        functools.partial(forward0_body, heads, steps),
        "forward0",
        6,
        grid=(steps,),
        in_specs=[
            level_rows(own),
            whole(root_state),
            whole(gain),
            tokens(columns, own),
            tokens(columns, own),
            tokens(STATE, own),
            tokens(STATE, own),
            tokens(columns, own),
        ],
        out_specs=[flat(columns, own), pl.BlockSpec((8, FOLD), lambda _: (0, 0))],
        out_shape=[pltpu.HBM((1, length, columns), BF16), pltpu.HBM((8, FOLD), F32)],
        scratch_shapes=[state_scratch, packs_scratch],
    )(far(cum_rows), root, gain, x, gate, b, c, out_grad)

    got, sums0 = lax.optimization_barrier((got, sums0))
    picked = call(
        functools.partial(pick_body, heads),
        "pick",
        1,
        in_specs=[smem, vmem],
        out_specs=anywhere,
        out_shape=pltpu.HBM(pair_shape, F32),
        scratch_shapes=[pair_scratch, dma((4,))],
    )(parent_ids, near(got))

    picked, late_rows = lax.optimization_barrier((picked, cum_rows))
    starts = exchange(picked)
    both = lambda l, k: (l, k)
    later = lambda l, k: (l + 1, k)
    local, turned = call(
        functools.partial(local_body, heads, steps),
        "local",
        7,
        grid=(2, steps),
        in_specs=[
            level_rows(later),
            tokens(columns, later),
            tokens(STATE, later),
            tokens(STATE, later),
        ],
        out_specs=[flat(columns, both), flat(BLOCK, both)],
        out_shape=[
            pltpu.HBM((2, length, columns), BF16),
            pltpu.HBM((2, blocks * STATE, BLOCK), BF16),
        ],
        scratch_shapes=[state_scratch, packs_scratch],
    )(far(late_rows), x, b, c)

    gated, gate_near, out_grad_near, turned_near, packed, sums = call(
        functools.partial(readout_body, heads, steps),
        "readout",
        5,
        in_specs=[anywhere] * 6 + [vmem] * 3,
        out_specs=[vmem] * 5 + [anywhere],
        out_shape=[
            pair_of_levels(columns),
            pair_of_levels(columns),
            pair_of_levels(columns),
            pair_of_levels(BLOCK),
            pltpu.VMEM(two_levels, F32),
            pltpu.HBM(sums_shape, F32),
        ],
        scratch_shapes=[
            pair_of_levels(columns),
            pair_of_levels(STATE),
            pltpu.VMEM((2 * steps,) + rows_shape[1:], F32),
            pltpu.VMEM(sums_shape, F32),
            dma((5, 4)),
            dma,
            dma,
            dma,
        ],
    )(
        far(local),
        gate,
        c,
        out_grad,
        far(turned),
        far(late_rows),
        near(starts),
        gain,
        sums0,
    )
    totals = lax.all_to_all(sums, "head", split_axis=0, concat_axis=0, tiled=True)

    grads, send_back = call(
        functools.partial(grads_body, heads, steps, features),
        "grads",
        5,
        in_specs=[vmem] * 7,
        out_specs=[anywhere, anywhere],
        out_shape=[pltpu.HBM((2, length, columns), BF16), pltpu.HBM(pair_shape, F32)],
        scratch_shapes=[pair_of_levels(columns), pair_scratch, dma((2 * steps,)), dma((2,))],
    )(
        near(packed),
        near(turned_near),
        near(gate_near),
        near(out_grad_near),
        near(gated),
        near(totals),
        gain,
    )
    got_back = exchange(send_back)

    own_back = lambda k: (0, steps - 1 - k)
    given = call(
        functools.partial(back0_body, heads, steps, features),
        "back0",
        6,
        grid=(steps,),
        in_specs=[
            level_rows(own_back),
            whole(gain),
            pl.BlockSpec(sums_shape, lambda _: (0, 0, 0)),
            tokens(columns, own_back),
            tokens(STATE, own_back),
            tokens(STATE, own_back),
            tokens(columns, own_back),
            flat(columns, own_back),
        ],
        out_specs=[tokens(columns, own_back), state_grads(own_back)],
        out_shape=[pltpu.HBM(ssm_input.shape, BF16), pltpu.HBM(state_shape, F32)],
        scratch_shapes=[state_scratch, packs_scratch, pltpu.VMEM((steps, SPAN, 8), F32)],
    )(far(cum_rows), gain, totals, gate, b, c, out_grad, far(gated0))

    got_back, *given = lax.optimization_barrier((got_back, *given))
    folded = call(
        functools.partial(fold_body, heads),
        "fold",
        1,
        in_specs=[smem, vmem, vmem],
        out_specs=anywhere,
        out_shape=pltpu.HBM(pair_shape, F32),
        scratch_shapes=[pair_scratch, dma((2,))],
    )(parent_ids, got[:, pair_shape[1] :], near(got_back))

    folded, late_rows = lax.optimization_barrier((folded, cum_rows))
    ends = exchange(folded)
    down_back = lambda l, k: (2 - l, steps - 1 - k)
    both_down_back = lambda l, k: (1 - l, steps - 1 - k)
    given = call(
        functools.partial(back_body, heads, steps),
        "back",
        8,
        grid=(2, steps),
        in_specs=[
            level_rows(down_back),
            flat(columns, both_down_back),
            tokens(STATE, down_back),
            tokens(STATE, down_back),
            anywhere,
            anywhere,
        ],
        out_specs=[tokens(columns, down_back), state_grads(down_back)],
        out_shape=[pltpu.HBM(ssm_input.shape, BF16), pltpu.HBM(state_shape, F32)],
        input_output_aliases={4: 0, 5: 1},
        scratch_shapes=[state_scratch, packs_scratch],
    )(far(late_rows), far(grads), b, c, *given)

    return call(
        functools.partial(inputs_body, heads, steps),
        "inputs",
        4,
        in_specs=[anywhere] * 4 + [vmem],
        out_specs=[anywhere, anywhere],
        out_shape=[pltpu.HBM(ssm_input.shape, BF16), pltpu.HBM(state_shape, F32)],
        input_output_aliases={1: 0, 2: 1},
        scratch_shapes=[
            pair_of_levels(STATE),
            pair_of_levels(columns),
            pair_of_levels(columns),
            pltpu.VMEM((2,) + state_shape[2:], F32),
            pltpu.VMEM((2 * steps,) + rows_shape[1:], F32),
            pltpu.VMEM(two_levels, F32),
            dma((6, 2)),
            dma((2,)),
            dma,
            dma((6,)),
            dma((2,)),
        ],
    )(b, *given, far(late_rows), near(ends))


def solution(mesh):
    in_specs = (
        P(None, "seg", None, "head"),
        P(None, "seg", None, "head"),
        P(None, "seg", None, None),
        P(None, "seg", None, None),
        P(None, "seg", "head", None),
        P("seg", "head", None, None),
        P("head"),
        P(None, "seg", None, "head"),
        P(),
    )
    out_specs = (P(None, "seg", None, "head"), P(None, "seg", "head", None, None))

    def run(*arrays):
        body = functools.partial(shards, arrays[0].shape[3], mesh.shape["head"])
        return tuple(
            jax.shard_map(
                body, mesh=mesh, in_specs=in_specs, out_specs=out_specs, check_vma=False
            )(*arrays)
        )

    return run
```

```python
import functools
import math

import jax
import jax.numpy as jnp
from jax import lax
from jax.experimental import pallas as pl
from jax.experimental.pallas import tpu as pltpu
from jax.sharding import PartitionSpec as P

BLOCK = 256
HALF = BLOCK // 2
HEADS = 24
HDIM = 128
STATE = 256
CHUNK = 3
SPAN = CHUNK * BLOCK
FOLD = SPAN // 2
EPSILON = 1e-05
VMEM_LIMIT = 24 * 1024 * 1024
LOG2E = math.log2(math.e)

WIDTH = 8 * CHUNK
CUM = 0
FROM_BLOCK = WIDTH
TO_BLOCK = 2 * WIDTH
FROM_LEVEL = 3 * WIDTH
TO_LEVEL = 4 * WIDTH

F32 = jnp.float32
BF16 = jnp.bfloat16
shaped = jax.ShapeDtypeStruct
pin = pltpu.with_memory_space_constraint


def call(body, name, micros, **kwargs):
    return pl.pallas_call(
        body,
        name=name,
        compiler_params=pltpu.CompilerParams(vmem_limit_bytes=VMEM_LIMIT),
        cost_estimate=pl.CostEstimate(
            flops=int(micros * 1e9), bytes_accessed=int(micros * 3e6), transcendentals=0
        ),
        **kwargs,
    )


def whole(array):
    rank = len(array.shape)
    return pl.BlockSpec(array.shape, lambda *_: (0,) * rank)


def dot(left, right, left_dim, right_dim, precision=None):
    return lax.dot_general(
        left,
        right,
        (((left_dim,), (right_dim,)), ((), ())),
        precision=precision,
        preferred_element_type=F32,
    )


def spread(packed, group, j, heads):
    at = group + 8 * j
    return jnp.concatenate(
        [
            jnp.broadcast_to(packed[:, at + h : at + h + 1], (packed.shape[0], HDIM))
            for h in range(heads)
        ],
        axis=1,
    )


def block(j):
    return slice(j * BLOCK, (j + 1) * BLOCK)


def head(h):
    return slice(h * HDIM, (h + 1) * HDIM)


def turn(values):
    size = values.shape[0]
    unit = lax.broadcasted_iota(jnp.int32, (size, size), 0) == lax.broadcasted_iota(
        jnp.int32, (size, size), 1
    )
    return dot(jnp.where(unit, 1.0, 0.0).astype(BF16), values, 1, 1).astype(BF16)


def silu(values):
    half = 0.5 * values
    return half + half * jnp.tanh(half)


def scatter_pieces(send, number, state, heads):
    rows = STATE // send.shape[0]
    for piece in range(send.shape[0]):
        for h in range(heads):
            at = (number * heads + h) * rows
            send[piece, at : at + rows] = state[piece * rows : (piece + 1) * rows, head(h)]


def gather_pieces(got, number, h, heads):
    rows = STATE // got.shape[0]
    at = (number * heads + h) * rows
    return got[:, at : at + rows].reshape(STATE, HDIM)


def start_all(copies):
    for copy in copies:
        copy.start()


def wait_all(copies):
    for copy in copies:
        copy.wait()


def piece_copies(sources, targets, sems, pieces):
    result = []
    for i, (at, first, count) in enumerate(pieces):
        rows = pl.ds(first * BLOCK, count * BLOCK)
        result.append(
            [
                pltpu.make_async_copy(source(at, rows), target.at[at, rows], sems.at[i, a])
                for a, (source, target) in enumerate(zip(sources, targets))
            ]
        )
    return result


def block_ends(parts):
    lasts = [part[:, BLOCK - 1 :] for part in parts]
    before = [jnp.zeros((8, 1), F32)]
    for last in lasts[:-1]:
        before.append(before[-1] + last)
    after = [jnp.zeros((8, 1), F32)]
    for last in lasts[:0:-1]:
        after.insert(0, after[0] + last)
    return lasts, before, after


def states_body(heads, steps, decay, root_hbm, x_hbm, b_hbm, send_out, rows_out, rates, rows, send,
                root, x, b, root_sem, sems, out_sems):
    chunks = rows.shape[0]
    blocks = steps * CHUNK
    pieces = [(0, 0, CHUNK), (0, CHUNK, CHUNK), (1, 0, CHUNK), (1, CHUNK, CHUNK)]
    copies = piece_copies(
        [lambda at, span: x_hbm.at[at, 0, span], lambda at, span: b_hbm.at[at, 0, span]],
        [x, b],
        sems,
        pieces,
    )
    root_copy = pltpu.make_async_copy(root_hbm.at[0], root, root_sem)
    root_copy.start()
    start_all(copies[0])

    rates[...] = jnp.zeros_like(rates)
    for level in range(decay.shape[0]):
        for number in range(blocks):
            for h in range(heads):
                row = 8 * (level * blocks + number) + h
                rates[row : row + 1] = decay[level, h, :, block(number)]
    upper = (
        lax.broadcasted_iota(jnp.int32, (BLOCK, BLOCK), 0)
        <= lax.broadcasted_iota(jnp.int32, (BLOCK, BLOCK), 1)
    )
    upper = jnp.where(upper, 1.0, 0.0).astype(BF16)
    rest = rates[...]
    sums = jnp.zeros_like(rest)
    for _ in range(3):
        part = rest.astype(BF16)
        rest = rest - part.astype(F32)
        sums = sums + dot(part, upper, 1, 0)
    sums = sums * -LOG2E
    for chunk in range(chunks):
        rows[chunk] = sums[WIDTH * chunk : WIDTH * (chunk + 1)]
    outs = [pltpu.make_async_copy(rows, rows_out, out_sems.at[2])]
    outs[0].start()

    lines = []
    totals = []
    for level in range(2):
        numbers = range(level * blocks, (level + 1) * blocks)
        parts = [sums[8 * number : 8 * number + 8] for number in numbers]
        lasts, _, after = block_ends(parts)
        for part, last, suffix in zip(parts, lasts, after):
            lines.append(jnp.exp2(last - part + suffix))
        totals.append(jnp.exp2(after[0] + lasts[0]))
    lines.append(jnp.zeros((128 - 16 * blocks, BLOCK), F32))
    to_level = jnp.concatenate(lines, axis=0).T

    root_copy.wait()
    start_all(copies[1])
    state = jnp.concatenate([(root[h] * totals[0][h : h + 1]).T for h in range(heads)], axis=1)
    half = heads * STATE // send.shape[0]
    for i, (level, first, count) in enumerate(pieces):
        if (level, first) == (1, 0):
            scatter_pieces(send, 0, state, heads)
            part = pl.ds(0, half)
            outs.append(
                pltpu.make_async_copy(send.at[:, part], send_out.at[:, part], out_sems.at[0])
            )
            outs[-1].start()
            state = jnp.zeros((STATE, heads * HDIM), F32)
        wait_all(copies[i])
        if i > 0:
            start_all(sum(copies[i + 1 : i + 2], []))
        turned, decayed = [], []
        for number in range(first, first + count):
            at = 8 * (level * blocks + number)
            scale = jnp.concatenate(
                [
                    jnp.broadcast_to(to_level[:, at + h : at + h + 1], (BLOCK, HDIM))
                    for h in range(heads)
                ],
                axis=1,
            )
            decayed.append((x[level, block(number)].astype(F32) * scale).astype(BF16))
            turned.append(turn(b[level, block(number)]))
        state = state + dot(
            jnp.concatenate(turned, axis=1), jnp.concatenate(decayed, axis=0), 1, 0
        )
    scatter_pieces(send, 1, state, heads)
    decays = jnp.broadcast_to(totals[1], (8, HDIM))
    for piece in range(send.shape[0]):
        send[piece, send.shape[1] - 8 :] = decays
    part = pl.ds(half, send.shape[1] - half)
    outs.append(pltpu.make_async_copy(send.at[:, part], send_out.at[:, part], out_sems.at[1]))
    outs[-1].start()
    wait_all(outs)


def pack(rows, packed):
    steps = packed.shape[0]
    parts = [rows[step, 8 * j : 8 * j + 8] for step in range(steps) for j in range(CHUNK)]
    lasts, before, after = block_ends(parts)
    for step in range(steps):
        mine = slice(step * CHUNK, (step + 1) * CHUNK)
        part = rows[step]
        last = jnp.concatenate(lasts[mine], axis=0)
        packed[step] = jnp.concatenate(
            [
                part,
                jnp.exp2(part),
                jnp.exp2(last - part),
                jnp.exp2(jnp.concatenate(before[mine], axis=0) + part),
                jnp.exp2(last - part + jnp.concatenate(after[mine], axis=0)),
                jnp.zeros((128 - 5 * WIDTH, BLOCK), F32),
            ],
            axis=0,
        ).T


def pick_body(heads, parent_ref, got_ref, send_out, send, sems):
    segments = got_ref.shape[0]
    rows = STATE // segments
    pair = send.shape[1]
    half = pair // 2
    quarter = segments // 4
    copies = []
    for seg in range(segments):
        first = parent_ref[0, seg]
        second = parent_ref[1, seg]
        root = parent_ref[0, second]
        send[seg, :half] = got_ref[first, :half]
        decay = got_ref[second, pair : pair + 8]
        for h in range(heads):
            a = slice(h * rows, (h + 1) * rows)
            b = slice(half + h * rows, half + (h + 1) * rows)
            send[seg, b] = decay[h : h + 1] * got_ref[root, a] + got_ref[second, b]
        if (seg + 1) % quarter == 0:
            part = pl.ds(seg + 1 - quarter, quarter)
            copies.append(
                pltpu.make_async_copy(send.at[part], send_out.at[part], sems.at[len(copies)])
            )
            copies[-1].start()
    wait_all(copies)


def fold_body(heads, parent_ref, decay_ref, got_ref, send_out, send, sems):
    rows = STATE // got_ref.shape[0]
    half = send.shape[1] // 2
    send[...] = jnp.zeros_like(send)
    copies = [
        pltpu.make_async_copy(send.at[:, part], send_out.at[:, part], sems.at[i])
        for i, part in enumerate([pl.ds(0, half), pl.ds(half, half)])
    ]
    for seg in range(got_ref.shape[0]):
        second = parent_ref[1, seg]
        send[second, :half] += got_ref[seg, :half]
    copies[0].start()
    for seg in range(got_ref.shape[0]):
        first = parent_ref[0, seg]
        decay = decay_ref[seg]
        for h in range(heads):
            a = slice(h * rows, (h + 1) * rows)
            b = slice(half + h * rows, half + (h + 1) * rows)
            send[first, b] += decay[h : h + 1] * send[seg, a] + got_ref[seg, b]
    copies[1].start()
    wait_all(copies)


def causal_mask(transposed):
    first = lax.broadcasted_iota(jnp.int32, (HALF, HALF), 0)
    second = lax.broadcasted_iota(jnp.int32, (HALF, HALF), 1)
    return first <= second if transposed else first >= second


def weighted(heads, j, rows, packed, x, b, c):
    scores = dot(c, b, 1, 1)
    causal = causal_mask(False)
    results = []
    for h in range(heads):
        row = rows[8 * j + h : 8 * j + h + 1]
        col = packed[:, CUM + 8 * j + h : CUM + 8 * j + h + 1]
        first = jnp.where(causal, col[:HALF] - row[:, :HALF], -jnp.inf)
        last = jnp.where(causal, col[HALF:] - row[:, HALF:], -jnp.inf)
        across = col[HALF:] - row[:, :HALF]
        top = jnp.concatenate(
            [(scores[:HALF, :HALF] * jnp.exp2(first)).astype(BF16), jnp.zeros((HALF, HALF), BF16)],
            axis=1,
        )
        bottom = jnp.concatenate(
            [
                (scores[HALF:, :HALF] * jnp.exp2(across)).astype(BF16),
                (scores[HALF:, HALF:] * jnp.exp2(last)).astype(BF16),
            ],
            axis=1,
        )
        results.append(dot(jnp.concatenate([top, bottom], axis=0), x[:, head(h)], 1, 0))
    return jnp.concatenate(results, axis=1)


def weighted_back(heads, j, rows, packed, grad, b, c):
    scores = dot(b, c, 1, 1)
    causal = causal_mask(True)
    results = []
    for h in range(heads):
        row = rows[8 * j + h : 8 * j + h + 1]
        col = packed[:, CUM + 8 * j + h : CUM + 8 * j + h + 1]
        first = jnp.where(causal, row[:, :HALF] - col[:HALF], -jnp.inf)
        last = jnp.where(causal, row[:, HALF:] - col[HALF:], -jnp.inf)
        across = row[:, HALF:] - col[:HALF]
        top = jnp.concatenate(
            [
                (scores[:HALF, :HALF] * jnp.exp2(first)).astype(BF16),
                (scores[:HALF, HALF:] * jnp.exp2(across)).astype(BF16),
            ],
            axis=1,
        )
        bottom = jnp.concatenate(
            [jnp.zeros((HALF, HALF), BF16), (scores[HALF:, HALF:] * jnp.exp2(last)).astype(BF16)],
            axis=1,
        )
        results.append(dot(jnp.concatenate([top, bottom], axis=0), grad[:, head(h)], 1, 0))
    return jnp.concatenate(results, axis=1)


def gated_sums(ssm_out, gate, out_grad, gain):
    act = silu(gate.astype(F32))
    gated = ssm_out * act
    scaled = out_grad.astype(F32) * gain
    squares = jnp.sum(gated * gated, axis=1, keepdims=True)
    products = jnp.sum(scaled * gated, axis=1, keepdims=True)
    pair = jnp.concatenate([squares, products, jnp.zeros((BLOCK, 6), F32)], axis=1).T
    return gated, scaled * act, gated * act, pair


def store_sums(sums, step, at, pairs):
    both = jnp.concatenate(pairs, axis=1)
    for q in range(2):
        for half in range(2):
            sums[4 * step + 2 * q + half : 4 * step + 2 * q + half + 1, at : at + FOLD] = both[
                q : q + 1, half * FOLD : (half + 1) * FOLD
            ]


def norm_columns(total, step, at, features):
    lines = [total[4 * step + i : 4 * step + i + 1, at : at + FOLD] for i in range(4)]
    squares = jnp.concatenate(lines[:2], axis=1) / features
    dots = jnp.concatenate(lines[2:], axis=1) / features
    inv_rms = lax.rsqrt(squares + EPSILON)
    back = inv_rms * inv_rms * inv_rms * dots
    return jnp.concatenate([inv_rms, back, jnp.zeros((6, SPAN), F32)], axis=0).T


def ssm_gradient(j, norm, gain, gate, out_grad, gated):
    inv_rms, back = norm[block(j), 0:1], norm[block(j), 1:2]
    grad = inv_rms * (out_grad.astype(F32) * gain) - gated.astype(F32) * back
    return (grad * silu(gate.astype(F32))).astype(BF16)


def forward0_body(heads, steps, rows_ref, root_ref, gain_ref, x_ref, gate_ref, b_ref, c_ref,
                  out_grad_ref, gated_ref, sums_ref, state, packs):
    step = pl.program_id(0)

    @pl.when(step == 0)
    def _():
        pack(rows_ref, packs)
        for h in range(heads):
            state[:, head(h)] = root_ref[0, h].T

    rows, packed = rows_ref[step], packs[step]
    current = state[...]
    pairs = []
    for j in range(CHUNK):
        x, b, c = x_ref[0, 0, block(j)], b_ref[0, 0, block(j)], c_ref[0, 0, block(j)]
        within = weighted(heads, j, rows, packed, x, b, c)
        carried = dot(c, current.astype(BF16), 1, 0) * spread(packed, FROM_BLOCK, j, heads)
        gated, _, _, pair = gated_sums(
            within + carried, gate_ref[0, 0, block(j)], out_grad_ref[0, 0, block(j)], gain_ref[...]
        )
        gated_ref[0, block(j)] = gated.astype(BF16)
        pairs.append(pair)
        decayed = (x.astype(F32) * spread(packed, TO_BLOCK, j, heads)).astype(BF16)
        factor = spread(packed[BLOCK - 1 :], FROM_BLOCK, j, heads)
        current = current * factor + dot(b, decayed, 0, 0)
    state[...] = current
    for part in range(steps):

        @pl.when(step == part)
        def _():
            store_sums(sums_ref, part, 0, pairs)


def local_body(heads, steps, rows_ref, x_ref, b_ref, c_ref, out_ref, turned_ref, state, packs):
    step = pl.program_id(1)

    @pl.when(step == 0)
    def _():
        pack(rows_ref, packs)
        state[...] = jnp.zeros_like(state)

    rows, packed = rows_ref[step], packs[step]
    current = state[...]
    for j in range(CHUNK):
        x, b, c = x_ref[0, 0, block(j)], b_ref[0, 0, block(j)], c_ref[0, 0, block(j)]
        within = weighted(heads, j, rows, packed, x, b, c)
        carried = dot(c, current.astype(BF16), 1, 0) * spread(packed, FROM_BLOCK, j, heads)
        out_ref[0, block(j)] = (within + carried).astype(BF16)
        turned_ref[0, :, block(j)] = turn(c)
        decayed = (x.astype(F32) * spread(packed, TO_BLOCK, j, heads)).astype(BF16)
        factor = spread(packed[BLOCK - 1 :], FROM_BLOCK, j, heads)
        current = current * factor + dot(b, decayed, 0, 0)
    state[...] = current


def readout_body(heads, steps, local_hbm, gate_hbm, c_hbm, out_grad_hbm, turned_hbm, rows_hbm,
                 start_ref, gain_ref, first_sums_ref, scaled_act, gated_act, turned, packed,
                 sums_out, local, gate, out_grad, c, rows, sums, sems, rows_sem, turned_sem, out_sem):
    rows_copy = pltpu.make_async_copy(rows_hbm.at[pl.ds(steps, 2 * steps)], rows, rows_sem)
    rows_copy.start()
    half = CHUNK * steps // 2
    pieces = [(0, 0, 1), (0, 1, 2), (0, half, half), (1, 0, half), (1, half, half)]
    copies = piece_copies(
        [
            lambda at, span: c_hbm.at[at + 1, 0, span],
            lambda at, span: local_hbm.at[at, span],
            lambda at, span: gate_hbm.at[at + 1, 0, span],
            lambda at, span: out_grad_hbm.at[at + 1, 0, span],
        ],
        [c, local, gate, out_grad],
        sems,
        pieces,
    )
    turned_copy = pltpu.make_async_copy(turned_hbm, turned, turned_sem)
    copies.append([turned_copy])
    start_all(copies[0] + copies[1])
    sums[0, :, :FOLD] = first_sums_ref[...]
    rows_copy.wait()
    for at in range(2):
        pack(rows.at[pl.ds(at * steps, steps)], packed.at[pl.ds(at * steps, steps)])
    start_all(copies[2])
    pairs = []
    for i, (at, first, count) in enumerate(pieces):
        if first == 0:
            start = jnp.concatenate(
                [gather_pieces(start_ref, at, h, heads) for h in range(heads)], axis=1
            ).astype(BF16)
        wait_all(copies[i])
        start_all(sum(copies[i + 3 : i + 4], []))
        piece = dot(c[at, first * BLOCK : (first + count) * BLOCK], start, 1, 0)
        for number in range(first, first + count):
            step, j = number // CHUNK, number % CHUNK
            place = block(number)
            carried = piece[block(number - first)]
            carried = carried * spread(packed[at * steps + step], FROM_LEVEL, j, heads)
            _, scaled_act[at, place], gated_act[at, place], pair = gated_sums(
                carried + local[at, place].astype(F32),
                gate[at, place],
                out_grad[at, place],
                gain_ref[...],
            )
            pairs.append(pair)
            if j == CHUNK - 1:
                store_sums(sums.at[0], step, (at + 1) * FOLD, pairs)
                pairs = []
    for copy in range(1, sums.shape[0]):
        sums[copy] = sums[0]
    out = pltpu.make_async_copy(sums, sums_out, out_sem)
    out.start()
    turned_copy.wait()
    out.wait()


def grads_body(heads, steps, features, packed_ref, turned_ref, scaled_act_ref, gated_act_ref,
               total_ref, grad_out, send_out, grads, send, grad_sems, sems):
    total = jnp.sum(total_ref[...], axis=0)
    half = send.shape[1] // 2
    outs = []
    for at in (1, 0):
        state = jnp.zeros((STATE, heads * HDIM), F32)
        for step in range(steps):
            packed = packed_ref[at * steps + step]
            norm = norm_columns(total, step, (at + 1) * FOLD, features)
            decayed = []
            for j in range(CHUNK):
                place = block(step * CHUNK + j)
                inv_rms, back = norm[block(j), 0:1], norm[block(j), 1:2]
                grad = inv_rms * scaled_act_ref[at, place] - back * gated_act_ref[at, place]
                grad = grad.astype(BF16)
                grads[at, place] = grad
                decayed.append(
                    (grad.astype(F32) * spread(packed, FROM_LEVEL, j, heads)).astype(BF16)
                )
            span = slice(step * SPAN, (step + 1) * SPAN)
            state = state + dot(
                turned_ref[at, :, span], jnp.concatenate(decayed, axis=0), 1, 0
            )
            span = pl.ds(step * SPAN, SPAN)
            outs.append(
                pltpu.make_async_copy(
                    grads.at[at, span], grad_out.at[at, span], grad_sems.at[at * steps + step]
                )
            )
            outs[-1].start()
        scatter_pieces(send, 1 - at, state, heads)
        part = pl.ds((1 - at) * half, half)
        outs.append(pltpu.make_async_copy(send.at[:, part], send_out.at[:, part], sems.at[at]))
        outs[-1].start()
    wait_all(outs)


def back_chunk(heads, rows, packed, grad_of, b_ref, c_ref, state):
    current = state[...]
    for j in reversed(range(CHUNK)):
        b, c = b_ref[0, 0, block(j)], c_ref[0, 0, block(j)]
        grad = grad_of(j)
        within = weighted_back(heads, j, rows, packed, grad, b, c)
        carried = dot(b, current.astype(BF16), 1, 0) * spread(packed, TO_BLOCK, j, heads)
        yield j, (within + carried).astype(BF16)
        decayed = (grad.astype(F32) * spread(packed, FROM_BLOCK, j, heads)).astype(BF16)
        factor = spread(packed[BLOCK - 1 :], FROM_BLOCK, j, heads)
        current = current * factor + dot(c, decayed, 0, 0)
    state[...] = current


def back0_body(heads, steps, features, rows_ref, gain_ref, total_ref, gate_ref, b_ref, c_ref,
               out_grad_ref, gated_ref, partial_ref, state_grad_ref, state, packs, norms):
    step = steps - 1 - pl.program_id(0)

    @pl.when(step == steps - 1)
    def _():
        pack(rows_ref, packs)
        total = jnp.sum(total_ref[...], axis=0)
        for part in range(steps):
            norms[part] = norm_columns(total, part, 0, features)
        state[...] = jnp.zeros_like(state)

    norm = norms[step]

    def grad_of(j):
        return ssm_gradient(
            j,
            norm,
            gain_ref[...],
            gate_ref[0, 0, block(j)],
            out_grad_ref[0, 0, block(j)],
            gated_ref[0, block(j)],
        )

    for j, part in back_chunk(heads, rows_ref[step], packs[step], grad_of, b_ref, c_ref, state):
        partial_ref[0, 0, block(j)] = part

    @pl.when(step == 0)
    def _():
        for h in range(heads):
            state_grad_ref[0, 0, h] = state[:, head(h)].T


def back_body(heads, steps, rows_ref, grad_ref, b_ref, c_ref, given_in, given_state, partial_ref,
              state_grad_ref, state, packs):
    step = steps - 1 - pl.program_id(1)

    @pl.when(step == steps - 1)
    def _():
        pack(rows_ref, packs)
        state[...] = jnp.zeros_like(state)

    def grad_of(j):
        return grad_ref[0, block(j)]

    for j, part in back_chunk(heads, rows_ref[step], packs[step], grad_of, b_ref, c_ref, state):
        partial_ref[0, 0, block(j)] = part

    @pl.when(step == 0)
    def _():
        for h in range(heads):
            state_grad_ref[0, 0, h] = state[:, head(h)].T


def inputs_body(heads, steps, b_hbm, partial_hbm, local_hbm, rows_hbm, end_ref, input_grad_out,
                state_grad_out, b, partial, grads, states, rows, packed, sems, local_sems,
                rows_sem, out_sems, state_sems):
    rows_copy = pltpu.make_async_copy(rows_hbm.at[pl.ds(0, 2 * steps)], rows, rows_sem)
    rows_copy.start()
    half = CHUNK * steps // 2
    pieces = [(1, 0, 1), (1, 1, 2), (1, half, half), (0, 0, half), (0, half, 2), (0, half + 2, 1)]
    copies = piece_copies(
        [lambda at, span: b_hbm.at[at, 0, span], lambda at, span: partial_hbm.at[at, 0, span]],
        [b, partial],
        sems,
        pieces,
    )
    locals_in = [
        pltpu.make_async_copy(local_hbm.at[level, 0], states.at[level], local_sems.at[level])
        for level in range(2)
    ]
    for i, (level, first, _) in enumerate(pieces):
        if first == half:
            copies[i].append(locals_in[level])
    start_all(copies[0] + copies[1] + copies[2])
    rows_copy.wait()
    for level in range(2):
        pack(rows.at[pl.ds(level * steps, steps)], packed.at[pl.ds(level * steps, steps)])
    outs = []
    for i, (level, first, count) in enumerate(pieces):
        if first == 0:
            end = jnp.concatenate(
                [gather_pieces(end_ref, 1 - level, h, heads) for h in range(heads)], axis=1
            )
            rounded = end.astype(BF16)
        wait_all(copies[i])
        start_all(sum(copies[i + 3 : i + 4], []))
        piece = dot(b[level, first * BLOCK : (first + count) * BLOCK], rounded, 1, 0)
        for number in range(first, first + count):
            place = block(number)
            extra = piece[block(number - first)] * spread(
                packed[level * steps + number // CHUNK], TO_LEVEL, number % CHUNK, heads
            )
            grads[level, place] = (partial[level, place].astype(F32) + extra).astype(BF16)
        span = pl.ds(first * BLOCK, count * BLOCK)
        outs.append(
            pltpu.make_async_copy(
                grads.at[level, span], input_grad_out.at[level, 0, span], out_sems.at[i]
            )
        )
        outs[-1].start()
        if first == half:
            last = packed[(level + 1) * steps - 1, BLOCK - 1 :]
            total = spread(last, FROM_LEVEL, CHUNK - 1, heads)
            for h in range(heads):
                states[level, h] += (end[:, head(h)] * total[:, head(h)]).T
            outs.append(
                pltpu.make_async_copy(
                    states.at[level], state_grad_out.at[level, 0], state_sems.at[level]
                )
            )
            outs[-1].start()
    wait_all(outs)


def shards(features, head_devices, ssm_input, gate_input, b_input, c_output, log_decay,
           root_state, norm_gain, out_grad, parent_ids):
    levels, _, length, columns = ssm_input.shape
    heads = columns // HDIM
    blocks = length // BLOCK
    steps = blocks // CHUNK
    segments = parent_ids.shape[1]
    rows = STATE // segments
    gain = norm_gain.reshape(1, columns)
    decay = jnp.transpose(log_decay, (0, 2, 1, 3))

    smem = pl.BlockSpec(memory_space=pltpu.SMEM)
    vmem = pl.BlockSpec(memory_space=pltpu.VMEM)
    anywhere = pl.BlockSpec(memory_space=pl.ANY)
    rows_shape = (levels * steps, WIDTH, BLOCK)
    two_levels = (2 * steps, BLOCK, 128)
    pair_shape = (segments, 2 * heads * rows, HDIM)
    first_shape = (segments, 2 * heads * rows + 8, HDIM)
    sums_shape = (head_devices, 8, levels * FOLD)
    state_shape = (levels, 1, heads, HDIM, STATE)
    state_scratch = pltpu.VMEM((STATE, columns), F32)
    packs_scratch = pltpu.VMEM((steps, BLOCK, 128), F32)
    pair_scratch = pltpu.VMEM(pair_shape, F32)
    dma = pltpu.SemaphoreType.DMA

    far = lambda array: pin(array, pltpu.HBM)
    near = lambda array: pin(array, pltpu.VMEM)
    x, gate, out_grad = far(ssm_input), far(gate_input), far(out_grad)
    decay = near(decay)
    b, c, root = far(b_input), far(c_output), far(root_state)

    def pair_of_levels(width):
        return pltpu.VMEM((2, length, width), BF16)

    def tokens(width, place):
        return pl.BlockSpec((1, 1, SPAN, width), lambda *g: (place(*g)[0], 0, place(*g)[1], 0))

    def flat(width, place):
        return pl.BlockSpec((1, SPAN, width), lambda *g: (*place(*g), 0))

    def level_rows(place):
        return pl.BlockSpec((steps,) + rows_shape[1:], lambda *g: (place(*g)[0], 0, 0))

    def state_grads(place):
        return pl.BlockSpec((1, 1, heads, HDIM, STATE), lambda *g: (place(*g)[0], 0, 0, 0, 0))

    exchange = functools.partial(
        lax.all_to_all, axis_name="seg", split_axis=0, concat_axis=0, tiled=True
    )

    send, cum_rows = call(
        functools.partial(states_body, heads, steps),
        "states",
        6,
        in_specs=[vmem] + [anywhere] * 3,
        out_specs=[anywhere, anywhere],
        out_shape=[pltpu.HBM(first_shape, F32), pltpu.HBM(rows_shape, F32)],
        scratch_shapes=[
            pltpu.VMEM((levels * blocks * 8, BLOCK), F32),
            pltpu.VMEM(rows_shape, F32),
            pltpu.VMEM(first_shape, F32),
            pltpu.VMEM(root_state.shape[1:], F32),
            pair_of_levels(columns),
            pair_of_levels(STATE),
            dma,
            dma((4, 2)),
            dma((3,)),
        ],
    )(decay, root, x, b)
    got = exchange(send)

    own = lambda k: (0, k)
    gated0, sums0 = call(
        functools.partial(forward0_body, heads, steps),
        "forward0",
        6,
        grid=(steps,),
        in_specs=[
            level_rows(own),
            whole(root_state),
            whole(gain),
            tokens(columns, own),
            tokens(columns, own),
            tokens(STATE, own),
            tokens(STATE, own),
            tokens(columns, own),
        ],
        out_specs=[flat(columns, own), pl.BlockSpec((8, FOLD), lambda _: (0, 0))],
        out_shape=[pltpu.HBM((1, length, columns), BF16), pltpu.HBM((8, FOLD), F32)],
        scratch_shapes=[state_scratch, packs_scratch],
    )(far(cum_rows), root, gain, x, gate, b, c, out_grad)

    got, sums0 = lax.optimization_barrier((got, sums0))
    picked = call(
        functools.partial(pick_body, heads),
        "pick",
        1,
        in_specs=[smem, vmem],
        out_specs=anywhere,
        out_shape=pltpu.HBM(pair_shape, F32),
        scratch_shapes=[pair_scratch, dma((4,))],
    )(parent_ids, near(got))

    picked, late_rows = lax.optimization_barrier((picked, cum_rows))
    starts = exchange(picked)
    both = lambda l, k: (l, k)
    later = lambda l, k: (l + 1, k)
    local, turned = call(
        functools.partial(local_body, heads, steps),
        "local",
        7,
        grid=(2, steps),
        in_specs=[
            level_rows(later),
            tokens(columns, later),
            tokens(STATE, later),
            tokens(STATE, later),
        ],
        out_specs=[
            flat(columns, both),
            pl.BlockSpec((1, STATE, SPAN), lambda l, k: (l, 0, k)),
        ],
        out_shape=[
            pltpu.HBM((2, length, columns), BF16),
            pltpu.HBM((2, STATE, length), BF16),
        ],
        scratch_shapes=[state_scratch, packs_scratch],
    )(far(late_rows), x, b, c)

    scaled_act, gated_act, turned, packed, sums = call(
        functools.partial(readout_body, heads, steps),
        "readout",
        5,
        in_specs=[anywhere] * 6 + [vmem] * 3,
        out_specs=[vmem] * 4 + [anywhere],
        out_shape=[
            pltpu.VMEM((2, length, columns), F32),
            pltpu.VMEM((2, length, columns), F32),
            pltpu.VMEM((2, STATE, length), BF16),
            pltpu.VMEM(two_levels, F32),
            pltpu.HBM(sums_shape, F32),
        ],
        scratch_shapes=[
            pair_of_levels(columns),
            pair_of_levels(columns),
            pair_of_levels(columns),
            pair_of_levels(STATE),
            pltpu.VMEM((2 * steps,) + rows_shape[1:], F32),
            pltpu.VMEM(sums_shape, F32),
            dma((5, 4)),
            dma,
            dma,
            dma,
        ],
    )(
        far(local),
        gate,
        c,
        out_grad,
        far(turned),
        far(late_rows),
        near(starts),
        gain,
        sums0,
    )
    totals = lax.all_to_all(sums, "head", split_axis=0, concat_axis=0, tiled=True)

    grads, send_back = call(
        functools.partial(grads_body, heads, steps, features),
        "grads",
        4,
        in_specs=[vmem] * 5,
        out_specs=[anywhere, anywhere],
        out_shape=[pltpu.HBM((2, length, columns), BF16), pltpu.HBM(pair_shape, F32)],
        scratch_shapes=[pair_of_levels(columns), pair_scratch, dma((2 * steps,)), dma((2,))],
    )(near(packed), near(turned), near(scaled_act), near(gated_act), near(totals))
    got_back = exchange(send_back)

    own_back = lambda k: (0, steps - 1 - k)
    given = call(
        functools.partial(back0_body, heads, steps, features),
        "back0",
        6,
        grid=(steps,),
        in_specs=[
            level_rows(own_back),
            whole(gain),
            pl.BlockSpec(sums_shape, lambda _: (0, 0, 0)),
            tokens(columns, own_back),
            tokens(STATE, own_back),
            tokens(STATE, own_back),
            tokens(columns, own_back),
            flat(columns, own_back),
        ],
        out_specs=[tokens(columns, own_back), state_grads(own_back)],
        out_shape=[pltpu.HBM(ssm_input.shape, BF16), pltpu.HBM(state_shape, F32)],
        scratch_shapes=[state_scratch, packs_scratch, pltpu.VMEM((steps, SPAN, 8), F32)],
    )(far(cum_rows), gain, totals, gate, b, c, out_grad, far(gated0))

    got_back, *given = lax.optimization_barrier((got_back, *given))
    folded = call(
        functools.partial(fold_body, heads),
        "fold",
        1,
        in_specs=[smem, vmem, vmem],
        out_specs=anywhere,
        out_shape=pltpu.HBM(pair_shape, F32),
        scratch_shapes=[pair_scratch, dma((2,))],
    )(parent_ids, got[:, pair_shape[1] :], near(got_back))

    folded, late_rows = lax.optimization_barrier((folded, cum_rows))
    ends = exchange(folded)
    down_back = lambda l, k: (2 - l, steps - 1 - k)
    both_down_back = lambda l, k: (1 - l, steps - 1 - k)
    given = call(
        functools.partial(back_body, heads, steps),
        "back",
        8,
        grid=(2, steps),
        in_specs=[
            level_rows(down_back),
            flat(columns, both_down_back),
            tokens(STATE, down_back),
            tokens(STATE, down_back),
            anywhere,
            anywhere,
        ],
        out_specs=[tokens(columns, down_back), state_grads(down_back)],
        out_shape=[pltpu.HBM(ssm_input.shape, BF16), pltpu.HBM(state_shape, F32)],
        input_output_aliases={4: 0, 5: 1},
        scratch_shapes=[state_scratch, packs_scratch],
    )(far(late_rows), far(grads), b, c, *given)

    return call(
        functools.partial(inputs_body, heads, steps),
        "inputs",
        4,
        in_specs=[anywhere] * 4 + [vmem],
        out_specs=[anywhere, anywhere],
        out_shape=[pltpu.HBM(ssm_input.shape, BF16), pltpu.HBM(state_shape, F32)],
        input_output_aliases={1: 0, 2: 1},
        scratch_shapes=[
            pair_of_levels(STATE),
            pair_of_levels(columns),
            pair_of_levels(columns),
            pltpu.VMEM((2,) + state_shape[2:], F32),
            pltpu.VMEM((2 * steps,) + rows_shape[1:], F32),
            pltpu.VMEM(two_levels, F32),
            dma((6, 2)),
            dma((2,)),
            dma,
            dma((6,)),
            dma((2,)),
        ],
    )(b, *given, far(late_rows), near(ends))


def solution(mesh):
    in_specs = (
        P(None, "seg", None, "head"),
        P(None, "seg", None, "head"),
        P(None, "seg", None, None),
        P(None, "seg", None, None),
        P(None, "seg", "head", None),
        P("seg", "head", None, None),
        P("head"),
        P(None, "seg", None, "head"),
        P(),
    )
    out_specs = (P(None, "seg", None, "head"), P(None, "seg", "head", None, None))

    def run(*arrays):
        body = functools.partial(shards, arrays[0].shape[3], mesh.shape["head"])
        return tuple(
            jax.shard_map(
                body, mesh=mesh, in_specs=in_specs, out_specs=out_specs, check_vma=False
            )(*arrays)
        )

    return run
```

```python
import functools
import math

import jax
import jax.numpy as jnp
from jax import lax
from jax.experimental import pallas as pl
from jax.experimental.pallas import tpu as pltpu
from jax.sharding import PartitionSpec as P

BLOCK = 256
HALF = BLOCK // 2
HEADS = 24
HDIM = 128
STATE = 256
CHUNK = 3
SPAN = CHUNK * BLOCK
FOLD = SPAN // 2
EPSILON = 1e-05
VMEM_LIMIT = 24 * 1024 * 1024
LOG2E = math.log2(math.e)

WIDTH = 8 * CHUNK
CUM = 0
FROM_BLOCK = WIDTH
TO_BLOCK = 2 * WIDTH

F32 = jnp.float32
BF16 = jnp.bfloat16
shaped = jax.ShapeDtypeStruct
pin = pltpu.with_memory_space_constraint


def call(body, name, micros, **kwargs):
    return pl.pallas_call(
        body,
        name=name,
        compiler_params=pltpu.CompilerParams(vmem_limit_bytes=VMEM_LIMIT),
        cost_estimate=pl.CostEstimate(
            flops=int(micros * 1e9), bytes_accessed=int(micros * 3e6), transcendentals=0
        ),
        **kwargs,
    )


def whole(array):
    rank = len(array.shape)
    return pl.BlockSpec(array.shape, lambda *_: (0,) * rank)


def dot(left, right, left_dim, right_dim, precision=None):
    return lax.dot_general(
        left,
        right,
        (((left_dim,), (right_dim,)), ((), ())),
        precision=precision,
        preferred_element_type=F32,
    )


def spread(packed, group, j, heads):
    at = group + 8 * j
    return jnp.concatenate(
        [
            jnp.broadcast_to(packed[:, at + h : at + h + 1], (packed.shape[0], HDIM))
            for h in range(heads)
        ],
        axis=1,
    )


def block(j):
    return slice(j * BLOCK, (j + 1) * BLOCK)


def head(h):
    return slice(h * HDIM, (h + 1) * HDIM)


def turn(values):
    size = values.shape[0]
    unit = lax.broadcasted_iota(jnp.int32, (size, size), 0) == lax.broadcasted_iota(
        jnp.int32, (size, size), 1
    )
    return dot(jnp.where(unit, 1.0, 0.0).astype(BF16), values, 1, 1)


def silu(values):
    half = 0.5 * values
    return half + half * jnp.tanh(half)


def scatter_pieces(send, number, states):
    rows = STATE // send.shape[0]
    for piece in range(send.shape[0]):
        for h, state in enumerate(states):
            at = (number * len(states) + h) * rows
            send[piece, at : at + rows] = state[piece * rows : (piece + 1) * rows]


def gather_pieces(got, number, h, heads):
    rows = STATE // got.shape[0]
    at = (number * heads + h) * rows
    return got[:, at : at + rows].reshape(STATE, HDIM)


def start_all(copies):
    for copy in copies:
        copy.start()


def wait_all(copies):
    for copy in copies:
        copy.wait()


def piece_copies(sources, targets, sems, pieces):
    result = []
    for i, (at, first, count) in enumerate(pieces):
        rows = pl.ds(first * BLOCK, count * BLOCK)
        result.append(
            [
                pltpu.make_async_copy(source(at, rows), target.at[at, rows], sems.at[i, a])
                for a, (source, target) in enumerate(zip(sources, targets))
            ]
        )
    return result


def block_ends(parts):
    lasts = [part[:, BLOCK - 1 :] for part in parts]
    before = [jnp.zeros((8, 1), F32)]
    for last in lasts[:-1]:
        before.append(before[-1] + last)
    after = [jnp.zeros((8, 1), F32)]
    for last in lasts[:0:-1]:
        after.insert(0, after[0] + last)
    return lasts, before, after


def states_body(heads, steps, decay_hbm, root_hbm, x_hbm, b_hbm, send_out, rows_out, rates, rows,
                decay, send, root, x, b, decay_sem, root_sem, sems, out_sems):
    blocks = steps * CHUNK
    decay_copy = pltpu.make_async_copy(decay_hbm, decay, decay_sem)
    decay_copy.start()
    pieces = [(0, 0, CHUNK), (0, CHUNK, CHUNK), (1, 0, CHUNK), (1, CHUNK, CHUNK)]
    copies = piece_copies(
        [lambda at, span: x_hbm.at[at, 0, span], lambda at, span: b_hbm.at[at, 0, span]],
        [x, b],
        sems,
        pieces,
    )
    root_copy = pltpu.make_async_copy(root_hbm.at[0], root, root_sem)
    start_all(copies[0])
    root_copy.start()

    rates[...] = jnp.zeros_like(rates)
    upper = (
        lax.broadcasted_iota(jnp.int32, (BLOCK, BLOCK), 0)
        <= lax.broadcasted_iota(jnp.int32, (BLOCK, BLOCK), 1)
    )
    upper = jnp.where(upper, 1.0, 0.0).astype(BF16)
    decay_copy.wait()
    start_all(copies[1])
    for level in range(decay.shape[0]):
        for number in range(blocks):
            for h in range(heads):
                row = 8 * (level * blocks + number) + h
                rates[row : row + 1] = decay[level, h, :, block(number)]
    rest = rates[...]
    sums = jnp.zeros_like(rest)
    for _ in range(3):
        part = rest.astype(BF16)
        rest = rest - part.astype(F32)
        sums = sums + dot(part, upper, 1, 0)
    sums = sums * -LOG2E
    for chunk in range(rows.shape[0]):
        rows[chunk] = sums[WIDTH * chunk : WIDTH * (chunk + 1)]
    outs = [pltpu.make_async_copy(rows, rows_out, out_sems.at[2])]
    outs[0].start()

    to_level = []
    totals = []
    for level in range(2):
        numbers = range(level * blocks, (level + 1) * blocks)
        parts = [sums[8 * number : 8 * number + 8] for number in numbers]
        lasts, _, after = block_ends(parts)
        for part, last, suffix in zip(parts, lasts, after):
            to_level.append(jnp.exp2(last - part + suffix))
        totals.append(jnp.exp2(after[0] + lasts[0]))

    root_copy.wait()
    states = [(root[h] * totals[0][h : h + 1]).T for h in range(heads)]
    half = heads * STATE // send.shape[0]
    for i, (level, first, count) in enumerate(pieces):
        if (level, first) == (1, 0):
            scatter_pieces(send, 0, states)
            part = pl.ds(0, half)
            outs.append(
                pltpu.make_async_copy(send.at[:, part], send_out.at[:, part], out_sems.at[0])
            )
            outs[-1].start()
            states = [jnp.zeros((STATE, HDIM), F32)] * heads
        wait_all(copies[i])
        if i > 0:
            start_all(sum(copies[i + 1 : i + 2], []))
        numbers = range(first, first + count)
        turned = [turn(b[level, block(number)]) for number in numbers]
        span = slice(first * BLOCK, (first + count) * BLOCK)
        for h in range(heads):
            decayed = [
                (values * to_level[level * blocks + number][h : h + 1]).astype(BF16)
                for number, values in zip(numbers, turned)
            ]
            states[h] = states[h] + dot(
                jnp.concatenate(decayed, axis=1), x[level, span, head(h)], 1, 0
            )
    scatter_pieces(send, 1, states)
    decays = jnp.broadcast_to(totals[1], (8, HDIM))
    for piece in range(send.shape[0]):
        send[piece, send.shape[1] - 8 :] = decays
    part = pl.ds(half, send.shape[1] - half)
    outs.append(pltpu.make_async_copy(send.at[:, part], send_out.at[:, part], out_sems.at[1]))
    outs[-1].start()
    wait_all(outs)


def level_decays(rows, to_end):
    steps = rows.shape[0]
    parts = [rows[step, 8 * j : 8 * j + 8] for step in range(steps) for j in range(CHUNK)]
    lasts, before, after = block_ends(parts)
    if to_end:
        lines = [last - part + end for part, last, end in zip(parts, lasts, after)]
    else:
        lines = [start + part for part, start in zip(parts, before)]
    return [
        jnp.exp2(jnp.concatenate(lines[step * CHUNK : (step + 1) * CHUNK], axis=0))
        for step in range(steps)
    ]


def pack(rows, packed):
    for step in range(packed.shape[0]):
        part = rows[step]
        last = jnp.concatenate(
            [
                jnp.broadcast_to(part[8 * j : 8 * j + 8, BLOCK - 1 :], (8, BLOCK))
                for j in range(CHUNK)
            ],
            axis=0,
        )
        packed[step] = jnp.concatenate(
            [
                part,
                jnp.exp2(part),
                jnp.exp2(last - part),
                jnp.zeros((128 - 3 * WIDTH, BLOCK), F32),
            ],
            axis=0,
        ).T


def pick_body(heads, parent_ref, got_ref, send_out, send, sems):
    segments = got_ref.shape[0]
    rows = STATE // segments
    pair = send.shape[1]
    half = pair // 2
    quarter = segments // 4
    copies = []
    for seg in range(segments):
        first = parent_ref[0, seg]
        second = parent_ref[1, seg]
        root = parent_ref[0, second]
        send[seg, :half] = got_ref[first, :half]
        decay = got_ref[second, pair : pair + 8]
        for h in range(heads):
            a = slice(h * rows, (h + 1) * rows)
            b = slice(half + h * rows, half + (h + 1) * rows)
            send[seg, b] = decay[h : h + 1] * got_ref[root, a] + got_ref[second, b]
        if (seg + 1) % quarter == 0:
            part = pl.ds(seg + 1 - quarter, quarter)
            copies.append(
                pltpu.make_async_copy(send.at[part], send_out.at[part], sems.at[len(copies)])
            )
            copies[-1].start()
    wait_all(copies)


def fold_body(heads, parent_ref, decay_ref, got_ref, send_out, send, sems):
    rows = STATE // got_ref.shape[0]
    half = send.shape[1] // 2
    send[...] = jnp.zeros_like(send)
    copies = [
        pltpu.make_async_copy(send.at[:, part], send_out.at[:, part], sems.at[i])
        for i, part in enumerate([pl.ds(0, half), pl.ds(half, half)])
    ]
    for seg in range(got_ref.shape[0]):
        second = parent_ref[1, seg]
        send[second, :half] += got_ref[seg, :half]
    copies[0].start()
    for seg in range(got_ref.shape[0]):
        first = parent_ref[0, seg]
        decay = decay_ref[seg]
        for h in range(heads):
            a = slice(h * rows, (h + 1) * rows)
            b = slice(half + h * rows, half + (h + 1) * rows)
            send[first, b] += decay[h : h + 1] * send[seg, a] + got_ref[seg, b]
    copies[1].start()
    wait_all(copies)


def causal_mask(transposed):
    first = lax.broadcasted_iota(jnp.int32, (HALF, HALF), 0)
    second = lax.broadcasted_iota(jnp.int32, (HALF, HALF), 1)
    return first <= second if transposed else first >= second


def weighted(heads, j, rows, packed, x, b, c):
    scores = dot(c, b, 1, 1)
    causal = causal_mask(False)
    results = []
    for h in range(heads):
        row = rows[8 * j + h : 8 * j + h + 1]
        col = packed[:, CUM + 8 * j + h : CUM + 8 * j + h + 1]
        first = jnp.where(causal, col[:HALF] - row[:, :HALF], -jnp.inf)
        last = jnp.where(causal, col[HALF:] - row[:, HALF:], -jnp.inf)
        across = col[HALF:] - row[:, :HALF]
        top = jnp.concatenate(
            [(scores[:HALF, :HALF] * jnp.exp2(first)).astype(BF16), jnp.zeros((HALF, HALF), BF16)],
            axis=1,
        )
        bottom = jnp.concatenate(
            [
                (scores[HALF:, :HALF] * jnp.exp2(across)).astype(BF16),
                (scores[HALF:, HALF:] * jnp.exp2(last)).astype(BF16),
            ],
            axis=1,
        )
        results.append(dot(jnp.concatenate([top, bottom], axis=0), x[:, head(h)], 1, 0))
    return jnp.concatenate(results, axis=1)


def weighted_back(heads, j, rows, packed, grad, b, c):
    scores = dot(b, c, 1, 1)
    causal = causal_mask(True)
    results = []
    for h in range(heads):
        row = rows[8 * j + h : 8 * j + h + 1]
        col = packed[:, CUM + 8 * j + h : CUM + 8 * j + h + 1]
        first = jnp.where(causal, row[:, :HALF] - col[:HALF], -jnp.inf)
        last = jnp.where(causal, row[:, HALF:] - col[HALF:], -jnp.inf)
        across = row[:, HALF:] - col[:HALF]
        top = jnp.concatenate(
            [
                (scores[:HALF, :HALF] * jnp.exp2(first)).astype(BF16),
                (scores[:HALF, HALF:] * jnp.exp2(across)).astype(BF16),
            ],
            axis=1,
        )
        bottom = jnp.concatenate(
            [jnp.zeros((HALF, HALF), BF16), (scores[HALF:, HALF:] * jnp.exp2(last)).astype(BF16)],
            axis=1,
        )
        results.append(dot(jnp.concatenate([top, bottom], axis=0), grad[:, head(h)], 1, 0))
    return jnp.concatenate(results, axis=1)


def gated_sums(ssm_out, gate, out_grad, gain):
    act = silu(gate.astype(F32))
    gated = ssm_out * act
    scaled = out_grad.astype(F32) * gain
    squares = jnp.sum(gated * gated, axis=1, keepdims=True)
    products = jnp.sum(scaled * gated, axis=1, keepdims=True)
    pair = jnp.concatenate([squares, products, jnp.zeros((BLOCK, 6), F32)], axis=1).T
    return gated, scaled * act, gated * act, pair


def store_sums(sums, step, at, pairs):
    both = jnp.concatenate(pairs, axis=1)
    for q in range(2):
        for half in range(2):
            sums[4 * step + 2 * q + half : 4 * step + 2 * q + half + 1, at : at + FOLD] = both[
                q : q + 1, half * FOLD : (half + 1) * FOLD
            ]


def norm_columns(total, step, at, features):
    lines = [total[4 * step + i : 4 * step + i + 1, at : at + FOLD] for i in range(4)]
    squares = jnp.concatenate(lines[:2], axis=1) / features
    dots = jnp.concatenate(lines[2:], axis=1) / features
    inv_rms = lax.rsqrt(squares + EPSILON)
    back = inv_rms * inv_rms * inv_rms * dots
    return jnp.concatenate([inv_rms, back, jnp.zeros((6, SPAN), F32)], axis=0).T


def ssm_gradient(j, norm, gain, gate, out_grad, gated):
    inv_rms, back = norm[block(j), 0:1], norm[block(j), 1:2]
    grad = inv_rms * (out_grad.astype(F32) * gain) - gated.astype(F32) * back
    return (grad * silu(gate.astype(F32))).astype(BF16)


def forward0_body(heads, steps, rows_ref, root_ref, gain_ref, x_ref, gate_ref, b_ref, c_ref,
                  out_grad_ref, gated_ref, sums_ref, state, packs):
    step = pl.program_id(0)

    @pl.when(step == 0)
    def _():
        pack(rows_ref, packs)
        for h in range(heads):
            state[:, head(h)] = root_ref[0, h].T

    rows, packed = rows_ref[step], packs[step]
    current = state[...]
    pairs = []
    for j in range(CHUNK):
        x, b, c = x_ref[0, 0, block(j)], b_ref[0, 0, block(j)], c_ref[0, 0, block(j)]
        within = weighted(heads, j, rows, packed, x, b, c)
        carried = dot(c, current.astype(BF16), 1, 0) * spread(packed, FROM_BLOCK, j, heads)
        gated, _, _, pair = gated_sums(
            within + carried, gate_ref[0, 0, block(j)], out_grad_ref[0, 0, block(j)], gain_ref[...]
        )
        gated_ref[0, block(j)] = gated.astype(BF16)
        pairs.append(pair)
        decayed = (x.astype(F32) * spread(packed, TO_BLOCK, j, heads)).astype(BF16)
        factor = spread(packed[BLOCK - 1 :], FROM_BLOCK, j, heads)
        current = current * factor + dot(b, decayed, 0, 0)
    state[...] = current
    for part in range(steps):

        @pl.when(step == part)
        def _():
            store_sums(sums_ref, part, 0, pairs)


def local_body(heads, steps, rows_ref, x_ref, b_ref, c_ref, gate_hbm, c_hbm, out_grad_hbm,
               rows_hbm, out_ref, turned_ref, first_ref, gate_out, c_out, out_grad_out, rows_out,
               state, packs, sems):
    level, step = pl.program_id(0), pl.program_id(1)
    span = pl.ds(0, SPAN)
    copies = [
        pltpu.make_async_copy(source, target, sems.at[i])
        for i, (source, target) in enumerate(
            [
                (gate_hbm.at[1, 0, span], gate_out),
                (c_hbm.at[1, 0, span], c_out),
                (out_grad_hbm.at[1, 0, span], out_grad_out),
                (rows_hbm.at[pl.ds(steps, 2 * steps)], rows_out),
            ]
        )
    ]

    @pl.when((level == 0) & (step == 0))
    def _():
        start_all(copies)

    @pl.when(step == 0)
    def _():
        pack(rows_ref, packs)
        state[...] = jnp.zeros_like(state)

    rows, packed = rows_ref[step], packs[step]
    current = state[...]
    for j in range(CHUNK):
        x, b, c = x_ref[0, 0, block(j)], b_ref[0, 0, block(j)], c_ref[0, 0, block(j)]
        within = weighted(heads, j, rows, packed, x, b, c)
        carried = dot(c, current.astype(BF16), 1, 0) * spread(packed, FROM_BLOCK, j, heads)
        out_ref[0, block(j)] = (within + carried).astype(BF16)
        turned_ref[0, :, block(j)] = turn(c).astype(BF16)
        decayed = (x.astype(F32) * spread(packed, TO_BLOCK, j, heads)).astype(BF16)
        factor = spread(packed[BLOCK - 1 :], FROM_BLOCK, j, heads)
        current = current * factor + dot(b, decayed, 0, 0)
    state[...] = current

    @pl.when((level == 0) & (step == 0))
    def _():
        first_ref[...] = out_ref[0]

    @pl.when((level == 1) & (step == steps - 1))
    def _():
        wait_all(copies)


def readout_body(heads, steps, local_hbm, gate_hbm, c_hbm, out_grad_hbm, turned_hbm, local_ref,
                 gate_ref, c_ref, out_grad_ref, rows_ref, start_ref, gain_ref, first_sums_ref,
                 scaled_act, gated_act, turned, lines, sums_out, local, gate, out_grad, c, sums,
                 sems, turned_sem, out_sem):
    chunks = [(at, step) for at in range(2) for step in range(steps)]
    pieces = [(at, step * CHUNK, CHUNK) for at, step in chunks[1:]]
    copies = piece_copies(
        [
            lambda at, span: c_hbm.at[at + 1, 0, span],
            lambda at, span: local_hbm.at[at, span],
            lambda at, span: gate_hbm.at[at + 1, 0, span],
            lambda at, span: out_grad_hbm.at[at + 1, 0, span],
        ],
        [c, local, gate, out_grad],
        sems,
        pieces,
    )
    turned_copy = pltpu.make_async_copy(turned_hbm, turned, turned_sem)
    copies.append([turned_copy])
    start_all(copies[0] + copies[1])
    sums[0, :, :FOLD] = first_sums_ref[...]
    columns = []
    for at in range(2):
        decays = level_decays(rows_ref.at[pl.ds(at * steps, steps)], False)
        for step, line in enumerate(decays):
            lines[at * steps + step] = line
            columns.append(line.T)
    for i, (at, step) in enumerate(chunks):
        if step == 0:
            start = jnp.concatenate(
                [gather_pieces(start_ref, at, h, heads) for h in range(heads)], axis=1
            ).astype(BF16)
        if i == 0:
            refs = [c_ref, local_ref, gate_ref, out_grad_ref]
        else:
            wait_all(copies[i - 1])
            start_all(sum(copies[i + 1 : i + 2], []))
            refs = [
                buffer.at[at, step * SPAN : (step + 1) * SPAN]
                for buffer in (c, local, gate, out_grad)
            ]
        piece = dot(refs[0][...], start, 1, 0)
        pairs = []
        for j in range(CHUNK):
            carried = piece[block(j)] * spread(columns[i], 0, j, heads)
            place = block(step * CHUNK + j)
            _, scaled_act[at, place], gated_act[at, place], pair = gated_sums(
                carried + refs[1][block(j)].astype(F32),
                refs[2][block(j)],
                refs[3][block(j)],
                gain_ref[...],
            )
            pairs.append(pair)
        store_sums(sums.at[0], step, (at + 1) * FOLD, pairs)
    for copy in range(1, sums.shape[0]):
        sums[copy] = sums[0]
    out = pltpu.make_async_copy(sums, sums_out, out_sem)
    out.start()
    turned_copy.wait()
    out.wait()


def grads_body(heads, steps, features, lines_ref, turned_ref, scaled_act_ref, gated_act_ref,
               total_ref, grad_out, send_out, grads, send, grad_sems, sems):
    total = jnp.sum(total_ref[...], axis=0)
    half = send.shape[1] // 2
    outs = []
    for at in (1, 0):
        states = [jnp.zeros((STATE, HDIM), F32)] * heads
        for step in range(steps):
            norm = norm_columns(total, step, (at + 1) * FOLD, features)
            span = slice(step * SPAN, (step + 1) * SPAN)
            inv_rms, back = norm[:, 0:1], norm[:, 1:2]
            grad = inv_rms * scaled_act_ref[at, span] - back * gated_act_ref[at, span]
            grad = grad.astype(BF16)
            grads[at, span] = grad
            turned = turned_ref[at, :, span].astype(F32)
            lines = lines_ref[at * steps + step]
            for h in range(heads):
                line = jnp.concatenate(
                    [lines[8 * j + h : 8 * j + h + 1] for j in range(CHUNK)], axis=1
                )
                decayed = (turned * line).astype(BF16)
                states[h] = states[h] + dot(decayed, grad[:, head(h)], 1, 0)
            span = pl.ds(step * SPAN, SPAN)
            outs.append(
                pltpu.make_async_copy(
                    grads.at[at, span], grad_out.at[at, span], grad_sems.at[at * steps + step]
                )
            )
            outs[-1].start()
        scatter_pieces(send, 1 - at, states)
        part = pl.ds((1 - at) * half, half)
        outs.append(pltpu.make_async_copy(send.at[:, part], send_out.at[:, part], sems.at[at]))
        outs[-1].start()
    wait_all(outs)


def back_chunk(heads, rows, packed, grad_of, b_ref, c_ref, state):
    current = state[...]
    for j in reversed(range(CHUNK)):
        b, c = b_ref[0, 0, block(j)], c_ref[0, 0, block(j)]
        grad = grad_of(j)
        within = weighted_back(heads, j, rows, packed, grad, b, c)
        carried = dot(b, current.astype(BF16), 1, 0) * spread(packed, TO_BLOCK, j, heads)
        yield j, (within + carried).astype(BF16)
        decayed = (grad.astype(F32) * spread(packed, FROM_BLOCK, j, heads)).astype(BF16)
        factor = spread(packed[BLOCK - 1 :], FROM_BLOCK, j, heads)
        current = current * factor + dot(c, decayed, 0, 0)
    state[...] = current


def back0_body(heads, steps, features, rows_ref, gain_ref, total_ref, gate_ref, b_ref, c_ref,
               out_grad_ref, gated_ref, partial_ref, state_grad_ref, state, packs, norms):
    step = steps - 1 - pl.program_id(0)

    @pl.when(step == steps - 1)
    def _():
        pack(rows_ref, packs)
        total = jnp.sum(total_ref[...], axis=0)
        for part in range(steps):
            norms[part] = norm_columns(total, part, 0, features)
        state[...] = jnp.zeros_like(state)

    norm = norms[step]

    def grad_of(j):
        return ssm_gradient(
            j,
            norm,
            gain_ref[...],
            gate_ref[0, 0, block(j)],
            out_grad_ref[0, 0, block(j)],
            gated_ref[0, block(j)],
        )

    for j, part in back_chunk(heads, rows_ref[step], packs[step], grad_of, b_ref, c_ref, state):
        partial_ref[0, 0, block(j)] = part

    @pl.when(step == 0)
    def _():
        for h in range(heads):
            state_grad_ref[0, 0, h] = state[:, head(h)].T


def back_body(heads, steps, rows_ref, grad_ref, b_ref, c_ref, b_hbm, rows_hbm, given_in,
              given_state, partial_ref, state_grad_ref, near_ref, near_state_ref, b_out, rows_out,
              state, packs, sems):
    level, step = 2 - pl.program_id(0), steps - 1 - pl.program_id(1)
    copies = [
        pltpu.make_async_copy(b_hbm.at[1, 0], b_out, sems.at[0]),
        pltpu.make_async_copy(rows_hbm.at[pl.ds(0, 2 * steps)], rows_out, sems.at[1]),
    ]

    @pl.when((level == 2) & (step == steps - 1))
    def _():
        start_all(copies)

    @pl.when(step == steps - 1)
    def _():
        pack(rows_ref, packs)
        state[...] = jnp.zeros_like(state)

    def grad_of(j):
        return grad_ref[0, block(j)]

    for j, part in back_chunk(heads, rows_ref[step], packs[step], grad_of, b_ref, c_ref, state):
        partial_ref[0, 0, block(j)] = part

    @pl.when(step == 0)
    def _():
        for h in range(heads):
            state_grad_ref[0, 0, h] = state[:, head(h)].T

    @pl.when(level == 1)
    def _():
        near_ref[...] = partial_ref[0, 0]

    @pl.when((level == 1) & (step == 0))
    def _():
        near_state_ref[...] = state_grad_ref[0, 0]
        wait_all(copies)


def inputs_body(heads, steps, b_hbm, partial_hbm, local_hbm, b_ref, partial_ref, local_ref,
                rows_ref, end_ref, input_grad_out, state_grad_out, b, partial, grads, states, sems,
                local_sem, out_sems, state_sems):
    chunks = [(level, step) for level in (1, 0) for step in range(steps)]
    pieces = [(0, step * CHUNK, CHUNK) for step in range(steps)]
    copies = piece_copies(
        [lambda at, span: b_hbm.at[0, 0, span], lambda at, span: partial_hbm.at[0, 0, span]],
        [b, partial],
        sems,
        pieces,
    )
    local_copy = pltpu.make_async_copy(local_hbm.at[0, 0], states.at[0], local_sem)
    local_copy.start()
    for some in copies:
        start_all(some)
    outs = []
    for i, (level, step) in enumerate(chunks):
        if step == 0:
            ends = [gather_pieces(end_ref, 1 - level, h, heads) for h in range(heads)]
            rounded = jnp.concatenate(ends, axis=1).astype(BF16)
            level_rows = rows_ref.at[pl.ds(level * steps, steps)]
            columns = [line.T for line in level_decays(level_rows, True)]
            total = level_decays(level_rows, False)[-1][8 * (CHUNK - 1) :, BLOCK - 1 :]
            if level == 0:
                local_copy.wait()
            for h in range(heads):
                local = local_ref[h] if level == 1 else states[0, h]
                states[level, h] = local + (ends[h] * total[h : h + 1]).T
            outs.append(
                pltpu.make_async_copy(
                    states.at[level], state_grad_out.at[level, 0], state_sems.at[level]
                )
            )
            outs[-1].start()
        span = slice(step * SPAN, (step + 1) * SPAN)
        if level == 1:
            some_b, some_partial = b_ref.at[span], partial_ref.at[span]
        else:
            wait_all(copies[step])
            some_b, some_partial = b.at[0, span], partial.at[0, span]
        piece = dot(some_b[...], rounded, 1, 0)
        for j in range(CHUNK):
            extra = piece[block(j)] * spread(columns[step], 0, j, heads)
            grads[level, block(step * CHUNK + j)] = (
                some_partial[block(j)].astype(F32) + extra
            ).astype(BF16)
        span = pl.ds(step * SPAN, SPAN)
        outs.append(
            pltpu.make_async_copy(
                grads.at[level, span], input_grad_out.at[level, 0, span], out_sems.at[i]
            )
        )
        outs[-1].start()
    wait_all(outs)


def shards(features, head_devices, ssm_input, gate_input, b_input, c_output, log_decay,
           root_state, norm_gain, out_grad, parent_ids):
    levels, _, length, columns = ssm_input.shape
    heads = columns // HDIM
    blocks = length // BLOCK
    steps = blocks // CHUNK
    segments = parent_ids.shape[1]
    rows = STATE // segments
    gain = norm_gain.reshape(1, columns)
    decay = jnp.transpose(log_decay, (0, 2, 1, 3))

    smem = pl.BlockSpec(memory_space=pltpu.SMEM)
    vmem = pl.BlockSpec(memory_space=pltpu.VMEM)
    anywhere = pl.BlockSpec(memory_space=pl.ANY)
    rows_shape = (levels * steps, WIDTH, BLOCK)
    pair_shape = (segments, 2 * heads * rows, HDIM)
    first_shape = (segments, 2 * heads * rows + 8, HDIM)
    sums_shape = (head_devices, 8, levels * FOLD)
    state_shape = (levels, 1, heads, HDIM, STATE)
    state_scratch = pltpu.VMEM((STATE, columns), F32)
    packs_scratch = pltpu.VMEM((steps, BLOCK, 128), F32)
    pair_scratch = pltpu.VMEM(pair_shape, F32)
    dma = pltpu.SemaphoreType.DMA

    far = lambda array: pin(array, pltpu.HBM)
    near = lambda array: pin(array, pltpu.VMEM)
    x, gate, out_grad = far(ssm_input), far(gate_input), far(out_grad)
    decay = far(decay)
    b, c, root = far(b_input), far(c_output), far(root_state)

    def pair_of_levels(width):
        return pltpu.VMEM((2, length, width), BF16)

    def tokens(width, place):
        return pl.BlockSpec((1, 1, SPAN, width), lambda *g: (place(*g)[0], 0, place(*g)[1], 0))

    def flat(width, place):
        return pl.BlockSpec((1, SPAN, width), lambda *g: (*place(*g), 0))

    def level_rows(place):
        return pl.BlockSpec((steps,) + rows_shape[1:], lambda *g: (place(*g)[0], 0, 0))

    def state_grads(place):
        return pl.BlockSpec((1, 1, heads, HDIM, STATE), lambda *g: (place(*g)[0], 0, 0, 0, 0))

    exchange = functools.partial(
        lax.all_to_all, axis_name="seg", split_axis=0, concat_axis=0, tiled=True
    )

    send, cum_rows = call(
        functools.partial(states_body, heads, steps),
        "states",
        6,
        in_specs=[anywhere] * 4,
        out_specs=[anywhere, anywhere],
        out_shape=[pltpu.HBM(first_shape, F32), pltpu.HBM(rows_shape, F32)],
        scratch_shapes=[
            pltpu.VMEM((levels * blocks * 8, BLOCK), F32),
            pltpu.VMEM(rows_shape, F32),
            pltpu.VMEM(decay.shape, F32),
            pltpu.VMEM(first_shape, F32),
            pltpu.VMEM(root_state.shape[1:], F32),
            pair_of_levels(columns),
            pair_of_levels(STATE),
            dma,
            dma,
            dma((4, 2)),
            dma((3,)),
        ],
    )(decay, root, x, b)
    got = exchange(send)

    own = lambda k: (0, k)
    gated0, sums0 = call(
        functools.partial(forward0_body, heads, steps),
        "forward0",
        6,
        grid=(steps,),
        in_specs=[
            level_rows(own),
            whole(root_state),
            whole(gain),
            tokens(columns, own),
            tokens(columns, own),
            tokens(STATE, own),
            tokens(STATE, own),
            tokens(columns, own),
        ],
        out_specs=[flat(columns, own), pl.BlockSpec((8, FOLD), lambda _: (0, 0))],
        out_shape=[pltpu.HBM((1, length, columns), BF16), pltpu.HBM((8, FOLD), F32)],
        scratch_shapes=[state_scratch, packs_scratch],
    )(far(cum_rows), root, gain, x, gate, b, c, out_grad)

    got, sums0 = lax.optimization_barrier((got, sums0))
    picked = call(
        functools.partial(pick_body, heads),
        "pick",
        1,
        in_specs=[smem, vmem],
        out_specs=anywhere,
        out_shape=pltpu.HBM(pair_shape, F32),
        scratch_shapes=[pair_scratch, dma((4,))],
    )(parent_ids, near(got))

    picked, late_rows = lax.optimization_barrier((picked, cum_rows))
    starts = exchange(picked)
    both = lambda l, k: (l, k)
    later = lambda l, k: (l + 1, k)
    local, turned, *first = call(
        functools.partial(local_body, heads, steps),
        "local",
        7,
        grid=(2, steps),
        in_specs=[
            level_rows(later),
            tokens(columns, later),
            tokens(STATE, later),
            tokens(STATE, later),
        ]
        + [anywhere] * 4,
        out_specs=[
            flat(columns, both),
            pl.BlockSpec((1, STATE, SPAN), lambda l, k: (l, 0, k)),
            pl.BlockSpec((SPAN, columns), lambda l, k: (0, 0)),
        ]
        + [anywhere] * 4,
        out_shape=[
            pltpu.HBM((2, length, columns), BF16),
            pltpu.HBM((2, STATE, length), BF16),
            pltpu.VMEM((SPAN, columns), BF16),
            pltpu.VMEM((SPAN, columns), BF16),
            pltpu.VMEM((SPAN, STATE), BF16),
            pltpu.VMEM((SPAN, columns), BF16),
            pltpu.VMEM((2 * steps,) + rows_shape[1:], F32),
        ],
        scratch_shapes=[state_scratch, packs_scratch, dma((4,))],
    )(far(late_rows), x, b, c, gate, c, out_grad, far(late_rows))

    scaled_act, gated_act, turned, lines, sums = call(
        functools.partial(readout_body, heads, steps),
        "readout",
        5,
        in_specs=[anywhere] * 5 + [vmem] * 8,
        out_specs=[vmem] * 4 + [anywhere],
        out_shape=[
            pltpu.VMEM((2, length, columns), F32),
            pltpu.VMEM((2, length, columns), F32),
            pltpu.VMEM((2, STATE, length), BF16),
            pltpu.VMEM((2 * steps,) + rows_shape[1:], F32),
            pltpu.HBM(sums_shape, F32),
        ],
        scratch_shapes=[
            pair_of_levels(columns),
            pair_of_levels(columns),
            pair_of_levels(columns),
            pair_of_levels(STATE),
            pltpu.VMEM(sums_shape, F32),
            dma((2 * steps - 1, 4)),
            dma,
            dma,
        ],
    )(
        far(local),
        gate,
        c,
        out_grad,
        far(turned),
        near(first[0]),
        near(first[1]),
        near(first[2]),
        near(first[3]),
        near(first[4]),
        near(starts),
        gain,
        sums0,
    )
    totals = lax.all_to_all(sums, "head", split_axis=0, concat_axis=0, tiled=True)

    grads, send_back = call(
        functools.partial(grads_body, heads, steps, features),
        "grads",
        4,
        in_specs=[vmem] * 5,
        out_specs=[anywhere, anywhere],
        out_shape=[pltpu.HBM((2, length, columns), BF16), pltpu.HBM(pair_shape, F32)],
        scratch_shapes=[pair_of_levels(columns), pair_scratch, dma((2 * steps,)), dma((2,))],
    )(near(lines), near(turned), near(scaled_act), near(gated_act), near(totals))
    got_back = exchange(send_back)

    own_back = lambda k: (0, steps - 1 - k)
    given = call(
        functools.partial(back0_body, heads, steps, features),
        "back0",
        6,
        grid=(steps,),
        in_specs=[
            level_rows(own_back),
            whole(gain),
            pl.BlockSpec(sums_shape, lambda _: (0, 0, 0)),
            tokens(columns, own_back),
            tokens(STATE, own_back),
            tokens(STATE, own_back),
            tokens(columns, own_back),
            flat(columns, own_back),
        ],
        out_specs=[tokens(columns, own_back), state_grads(own_back)],
        out_shape=[pltpu.HBM(ssm_input.shape, BF16), pltpu.HBM(state_shape, F32)],
        scratch_shapes=[state_scratch, packs_scratch, pltpu.VMEM((steps, SPAN, 8), F32)],
    )(far(cum_rows), gain, totals, gate, b, c, out_grad, far(gated0))

    got_back, *given = lax.optimization_barrier((got_back, *given))
    folded = call(
        functools.partial(fold_body, heads),
        "fold",
        1,
        in_specs=[smem, vmem, vmem],
        out_specs=anywhere,
        out_shape=pltpu.HBM(pair_shape, F32),
        scratch_shapes=[pair_scratch, dma((2,))],
    )(parent_ids, got[:, pair_shape[1] :], near(got_back))

    folded, late_rows = lax.optimization_barrier((folded, cum_rows))
    ends = exchange(folded)
    down_back = lambda l, k: (2 - l, steps - 1 - k)
    both_down_back = lambda l, k: (1 - l, steps - 1 - k)
    late = lambda l, k: (l, jnp.where(l == 0, steps - 1, steps - 1 - k))
    *given, near_partial, near_state, near_b, near_rows = call(
        functools.partial(back_body, heads, steps),
        "back",
        8,
        grid=(2, steps),
        in_specs=[
            level_rows(down_back),
            flat(columns, both_down_back),
            tokens(STATE, down_back),
            tokens(STATE, down_back),
        ]
        + [anywhere] * 4,
        out_specs=[
            tokens(columns, down_back),
            state_grads(down_back),
            pl.BlockSpec((SPAN, columns), lambda *g: (late(*g)[1], 0)),
            pl.BlockSpec((heads, HDIM, STATE), lambda *g: (0, 0, 0)),
            anywhere,
            anywhere,
        ],
        out_shape=[
            pltpu.HBM(ssm_input.shape, BF16),
            pltpu.HBM(state_shape, F32),
            pltpu.VMEM((length, columns), BF16),
            pltpu.VMEM(state_shape[2:], F32),
            pltpu.VMEM((length, STATE), BF16),
            pltpu.VMEM((2 * steps,) + rows_shape[1:], F32),
        ],
        input_output_aliases={6: 0, 7: 1},
        scratch_shapes=[state_scratch, packs_scratch, dma((2,))],
    )(far(late_rows), far(grads), b, c, b, far(late_rows), *given)

    return call(
        functools.partial(inputs_body, heads, steps),
        "inputs",
        4,
        in_specs=[anywhere] * 3 + [vmem] * 5,
        out_specs=[anywhere, anywhere],
        out_shape=[pltpu.HBM(ssm_input.shape, BF16), pltpu.HBM(state_shape, F32)],
        input_output_aliases={1: 0, 2: 1},
        scratch_shapes=[
            pltpu.VMEM((1, length, STATE), BF16),
            pltpu.VMEM((1, length, columns), BF16),
            pair_of_levels(columns),
            pltpu.VMEM((2,) + state_shape[2:], F32),
            dma((steps, 2)),
            dma,
            dma((2 * steps,)),
            dma((2,)),
        ],
    )(b, *given, near(near_b), near(near_partial), near(near_state), near(near_rows), near(ends))


def solution(mesh):
    in_specs = (
        P(None, "seg", None, "head"),
        P(None, "seg", None, "head"),
        P(None, "seg", None, None),
        P(None, "seg", None, None),
        P(None, "seg", "head", None),
        P("seg", "head", None, None),
        P("head"),
        P(None, "seg", None, "head"),
        P(),
    )
    out_specs = (P(None, "seg", None, "head"), P(None, "seg", "head", None, None))

    def run(*arrays):
        body = functools.partial(shards, arrays[0].shape[3], mesh.shape["head"])
        return tuple(
            jax.shard_map(
                body, mesh=mesh, in_specs=in_specs, out_specs=out_specs, check_vma=False
            )(*arrays)
        )

    return run
```

```python
import functools
import math

import jax
import jax.numpy as jnp
from jax import lax
from jax.experimental import pallas as pl
from jax.experimental.pallas import tpu as pltpu
from jax.sharding import PartitionSpec as P

BLOCK = 256
HALF = BLOCK // 2
HEADS = 24
HDIM = 128
STATE = 256
CHUNK = 3
SPAN = CHUNK * BLOCK
FIRST = 2 * BLOCK
FOLD = SPAN // 2
EPSILON = 1e-05
VMEM_LIMIT = 24 * 1024 * 1024
LOG2E = math.log2(math.e)

WIDTH = 8 * CHUNK
CUM = 0
FROM_BLOCK = WIDTH
TO_BLOCK = 2 * WIDTH

F32 = jnp.float32
BF16 = jnp.bfloat16
shaped = jax.ShapeDtypeStruct
pin = pltpu.with_memory_space_constraint


def call(body, name, micros, **kwargs):
    return pl.pallas_call(
        body,
        name=name,
        compiler_params=pltpu.CompilerParams(vmem_limit_bytes=VMEM_LIMIT),
        cost_estimate=pl.CostEstimate(
            flops=int(micros * 1e9), bytes_accessed=int(micros * 3e6), transcendentals=0
        ),
        **kwargs,
    )


def whole(array):
    rank = len(array.shape)
    return pl.BlockSpec(array.shape, lambda *_: (0,) * rank)


def dot(left, right, left_dim, right_dim, precision=None):
    return lax.dot_general(
        left,
        right,
        (((left_dim,), (right_dim,)), ((), ())),
        precision=precision,
        preferred_element_type=F32,
    )


def spread(packed, group, j, heads):
    at = group + 8 * j
    return jnp.concatenate(
        [
            jnp.broadcast_to(packed[:, at + h : at + h + 1], (packed.shape[0], HDIM))
            for h in range(heads)
        ],
        axis=1,
    )


def block(j):
    return slice(j * BLOCK, (j + 1) * BLOCK)


def head(h):
    return slice(h * HDIM, (h + 1) * HDIM)


def turn(values):
    size = values.shape[0]
    unit = lax.broadcasted_iota(jnp.int32, (size, size), 0) == lax.broadcasted_iota(
        jnp.int32, (size, size), 1
    )
    return dot(jnp.where(unit, 1.0, 0.0).astype(BF16), values, 1, 1)


def silu(values):
    half = 0.5 * values
    return half + half * jnp.tanh(half)


def scatter_pieces(send, number, states):
    rows = STATE // send.shape[0]
    for piece in range(send.shape[0]):
        for h, state in enumerate(states):
            at = (number * len(states) + h) * rows
            send[piece, at : at + rows] = state[piece * rows : (piece + 1) * rows]


def gather_pieces(got, number, h, heads):
    rows = STATE // got.shape[0]
    at = (number * heads + h) * rows
    return got[:, at : at + rows].reshape(STATE, HDIM)


def start_all(copies):
    for copy in copies:
        copy.start()


def wait_all(copies):
    for copy in copies:
        copy.wait()


def piece_copies(sources, targets, sems, pieces):
    result = []
    for i, (at, first, count) in enumerate(pieces):
        rows = pl.ds(first * BLOCK, count * BLOCK)
        result.append(
            [
                pltpu.make_async_copy(source(at, rows), target.at[at, rows], sems.at[i, a])
                for a, (source, target) in enumerate(zip(sources, targets))
            ]
        )
    return result


def block_ends(parts):
    lasts = [part[:, BLOCK - 1 :] for part in parts]
    before = [jnp.zeros((8, 1), F32)]
    for last in lasts[:-1]:
        before.append(before[-1] + last)
    after = [jnp.zeros((8, 1), F32)]
    for last in lasts[:0:-1]:
        after.insert(0, after[0] + last)
    return lasts, before, after


def states_body(heads, steps, decay_hbm, root_hbm, x_hbm, b_hbm, send, rows_out, rates, rows, decay,
                root, x, b, decay_sem, root_sem, sems, out_sem):
    blocks = steps * CHUNK
    decay_copy = pltpu.make_async_copy(decay_hbm, decay, decay_sem)
    decay_copy.start()
    pieces = [(0, 0, CHUNK), (0, CHUNK, CHUNK), (1, 0, CHUNK), (1, CHUNK, CHUNK)]
    copies = piece_copies(
        [lambda at, span: x_hbm.at[at, 0, span], lambda at, span: b_hbm.at[at, 0, span]],
        [x, b],
        sems,
        pieces,
    )
    root_copy = pltpu.make_async_copy(root_hbm.at[0], root, root_sem)
    start_all(copies[0])
    root_copy.start()

    rates[...] = jnp.zeros_like(rates)
    upper = (
        lax.broadcasted_iota(jnp.int32, (BLOCK, BLOCK), 0)
        <= lax.broadcasted_iota(jnp.int32, (BLOCK, BLOCK), 1)
    )
    upper = jnp.where(upper, 1.0, 0.0).astype(BF16)
    decay_copy.wait()
    start_all(copies[1])
    for level in range(decay.shape[0]):
        for number in range(blocks):
            for h in range(heads):
                row = 8 * (level * blocks + number) + h
                rates[row : row + 1] = decay[level, h, :, block(number)]
    rest = rates[...]
    sums = jnp.zeros_like(rest)
    for _ in range(3):
        part = rest.astype(BF16)
        rest = rest - part.astype(F32)
        sums = sums + dot(part, upper, 1, 0)
    sums = sums * -LOG2E
    for chunk in range(rows.shape[0]):
        rows[chunk] = sums[WIDTH * chunk : WIDTH * (chunk + 1)]
    rows_copy = pltpu.make_async_copy(rows, rows_out, out_sem)
    rows_copy.start()

    to_level = []
    totals = []
    for level in range(2):
        numbers = range(level * blocks, (level + 1) * blocks)
        parts = [sums[8 * number : 8 * number + 8] for number in numbers]
        lasts, _, after = block_ends(parts)
        for part, last, suffix in zip(parts, lasts, after):
            to_level.append(jnp.exp2(last - part + suffix))
        totals.append(jnp.exp2(after[0] + lasts[0]))

    root_copy.wait()
    states = [(root[h] * totals[0][h : h + 1]).T for h in range(heads)]
    for i, (level, first, count) in enumerate(pieces):
        if (level, first) == (1, 0):
            scatter_pieces(send, 0, states)
            states = [jnp.zeros((STATE, HDIM), F32)] * heads
        wait_all(copies[i])
        if i > 0:
            start_all(sum(copies[i + 1 : i + 2], []))
        numbers = range(first, first + count)
        turned = [turn(b[level, block(number)]) for number in numbers]
        span = slice(first * BLOCK, (first + count) * BLOCK)
        for h in range(heads):
            decayed = [
                (values * to_level[level * blocks + number][h : h + 1]).astype(BF16)
                for number, values in zip(numbers, turned)
            ]
            states[h] = states[h] + dot(
                jnp.concatenate(decayed, axis=1), x[level, span, head(h)], 1, 0
            )
    scatter_pieces(send, 1, states)
    decays = jnp.broadcast_to(totals[1], (8, HDIM))
    for piece in range(send.shape[0]):
        send[piece, send.shape[1] - 8 :] = decays
    rows_copy.wait()


def level_decays(rows, to_end):
    steps = rows.shape[0]
    parts = [rows[step, 8 * j : 8 * j + 8] for step in range(steps) for j in range(CHUNK)]
    lasts, before, after = block_ends(parts)
    if to_end:
        lines = [last - part + end for part, last, end in zip(parts, lasts, after)]
    else:
        lines = [start + part for part, start in zip(parts, before)]
    return [
        jnp.exp2(jnp.concatenate(lines[step * CHUNK : (step + 1) * CHUNK], axis=0))
        for step in range(steps)
    ]


def pack(rows, packed):
    for step in range(packed.shape[0]):
        part = rows[step]
        last = jnp.concatenate(
            [
                jnp.broadcast_to(part[8 * j : 8 * j + 8, BLOCK - 1 :], (8, BLOCK))
                for j in range(CHUNK)
            ],
            axis=0,
        )
        packed[step] = jnp.concatenate(
            [
                part,
                jnp.exp2(part),
                jnp.exp2(last - part),
                jnp.zeros((128 - 3 * WIDTH, BLOCK), F32),
            ],
            axis=0,
        ).T


def pick_body(heads, parent_ref, got_ref, send, decay_out):
    segments = got_ref.shape[0]
    rows = STATE // segments
    pair = send.shape[1]
    half = pair // 2
    for seg in range(segments):
        first = parent_ref[0, seg]
        second = parent_ref[1, seg]
        root = parent_ref[0, second]
        send[seg, :half] = got_ref[first, :half]
        decay = got_ref[second, pair : pair + 8]
        decay_out[seg] = got_ref[seg, pair : pair + 8]
        for h in range(heads):
            a = slice(h * rows, (h + 1) * rows)
            b = slice(half + h * rows, half + (h + 1) * rows)
            send[seg, b] = decay[h : h + 1] * got_ref[root, a] + got_ref[second, b]


def fold_body(heads, parent_ref, decay_ref, got_ref, send):
    rows = STATE // got_ref.shape[0]
    half = send.shape[1] // 2
    send[...] = jnp.zeros_like(send)
    for seg in range(got_ref.shape[0]):
        second = parent_ref[1, seg]
        send[second, :half] += got_ref[seg, :half]
    for seg in range(got_ref.shape[0]):
        first = parent_ref[0, seg]
        decay = decay_ref[seg]
        for h in range(heads):
            a = slice(h * rows, (h + 1) * rows)
            b = slice(half + h * rows, half + (h + 1) * rows)
            send[first, b] += decay[h : h + 1] * send[seg, a] + got_ref[seg, b]


def causal_mask(transposed):
    first = lax.broadcasted_iota(jnp.int32, (HALF, HALF), 0)
    second = lax.broadcasted_iota(jnp.int32, (HALF, HALF), 1)
    return first <= second if transposed else first >= second


def weighted(heads, j, rows, packed, x, b, c):
    scores = dot(c, b, 1, 1)
    causal = causal_mask(False)
    results = []
    for h in range(heads):
        row = rows[8 * j + h : 8 * j + h + 1]
        col = packed[:, CUM + 8 * j + h : CUM + 8 * j + h + 1]
        first = jnp.where(causal, col[:HALF] - row[:, :HALF], -jnp.inf)
        last = jnp.where(causal, col[HALF:] - row[:, HALF:], -jnp.inf)
        across = col[HALF:] - row[:, :HALF]
        top = jnp.concatenate(
            [(scores[:HALF, :HALF] * jnp.exp2(first)).astype(BF16), jnp.zeros((HALF, HALF), BF16)],
            axis=1,
        )
        bottom = jnp.concatenate(
            [
                (scores[HALF:, :HALF] * jnp.exp2(across)).astype(BF16),
                (scores[HALF:, HALF:] * jnp.exp2(last)).astype(BF16),
            ],
            axis=1,
        )
        results.append(dot(jnp.concatenate([top, bottom], axis=0), x[:, head(h)], 1, 0))
    return jnp.concatenate(results, axis=1)


def weighted_back(heads, j, rows, packed, grad, b, c):
    scores = dot(b, c, 1, 1)
    causal = causal_mask(True)
    results = []
    for h in range(heads):
        row = rows[8 * j + h : 8 * j + h + 1]
        col = packed[:, CUM + 8 * j + h : CUM + 8 * j + h + 1]
        first = jnp.where(causal, row[:, :HALF] - col[:HALF], -jnp.inf)
        last = jnp.where(causal, row[:, HALF:] - col[HALF:], -jnp.inf)
        across = row[:, HALF:] - col[:HALF]
        top = jnp.concatenate(
            [
                (scores[:HALF, :HALF] * jnp.exp2(first)).astype(BF16),
                (scores[:HALF, HALF:] * jnp.exp2(across)).astype(BF16),
            ],
            axis=1,
        )
        bottom = jnp.concatenate(
            [jnp.zeros((HALF, HALF), BF16), (scores[HALF:, HALF:] * jnp.exp2(last)).astype(BF16)],
            axis=1,
        )
        results.append(dot(jnp.concatenate([top, bottom], axis=0), grad[:, head(h)], 1, 0))
    return jnp.concatenate(results, axis=1)


def gated_sums(ssm_out, gate, out_grad, gain):
    act = silu(gate.astype(F32))
    gated = ssm_out * act
    scaled = out_grad.astype(F32) * gain
    squares = jnp.sum(gated * gated, axis=1, keepdims=True)
    products = jnp.sum(scaled * gated, axis=1, keepdims=True)
    pair = jnp.concatenate([squares, products, jnp.zeros((BLOCK, 6), F32)], axis=1).T
    return gated, scaled * act, gated * act, pair


def store_sums(sums, step, at, pairs):
    both = jnp.concatenate(pairs, axis=1)
    for q in range(2):
        for half in range(2):
            sums[4 * step + 2 * q + half : 4 * step + 2 * q + half + 1, at : at + FOLD] = both[
                q : q + 1, half * FOLD : (half + 1) * FOLD
            ]


def norm_columns(total, step, at, features):
    lines = [total[4 * step + i : 4 * step + i + 1, at : at + FOLD] for i in range(4)]
    squares = jnp.concatenate(lines[:2], axis=1) / features
    dots = jnp.concatenate(lines[2:], axis=1) / features
    inv_rms = lax.rsqrt(squares + EPSILON)
    back = inv_rms * inv_rms * inv_rms * dots
    return jnp.concatenate([inv_rms, back, jnp.zeros((6, SPAN), F32)], axis=0).T


def ssm_gradient(j, norm, gain, gate, out_grad, gated):
    inv_rms, back = norm[block(j), 0:1], norm[block(j), 1:2]
    grad = inv_rms * (out_grad.astype(F32) * gain) - gated.astype(F32) * back
    return (grad * silu(gate.astype(F32))).astype(BF16)


def forward0_body(heads, steps, rows_ref, root_ref, gain_ref, x_ref, gate_ref, b_ref, c_ref,
                  out_grad_ref, gated_ref, sums_ref, state, packs):
    step = pl.program_id(0)

    @pl.when(step == 0)
    def _():
        pack(rows_ref, packs)
        for h in range(heads):
            state[:, head(h)] = root_ref[0, h].T

    rows, packed = rows_ref[step], packs[step]
    current = state[...]
    pairs = []
    for j in range(CHUNK):
        x, b, c = x_ref[0, 0, block(j)], b_ref[0, 0, block(j)], c_ref[0, 0, block(j)]
        within = weighted(heads, j, rows, packed, x, b, c)
        carried = dot(c, current.astype(BF16), 1, 0) * spread(packed, FROM_BLOCK, j, heads)
        gated, _, _, pair = gated_sums(
            within + carried, gate_ref[0, 0, block(j)], out_grad_ref[0, 0, block(j)], gain_ref[...]
        )
        gated_ref[0, block(j)] = gated.astype(BF16)
        pairs.append(pair)
        decayed = (x.astype(F32) * spread(packed, TO_BLOCK, j, heads)).astype(BF16)
        factor = spread(packed[BLOCK - 1 :], FROM_BLOCK, j, heads)
        current = current * factor + dot(b, decayed, 0, 0)
    state[...] = current
    for part in range(steps):

        @pl.when(step == part)
        def _():
            store_sums(sums_ref, part, 0, pairs)


def local_body(heads, steps, rows_ref, x_ref, b_ref, c_ref, gate_hbm, c_hbm, out_grad_hbm,
               rows_hbm, out_ref, turned_ref, first_ref, gate_out, c_out, out_grad_out, rows_out,
               state, packs, sems):
    level, step = pl.program_id(0), pl.program_id(1)
    span = pl.ds(0, FIRST)
    copies = [
        pltpu.make_async_copy(source, target, sems.at[i])
        for i, (source, target) in enumerate(
            [
                (gate_hbm.at[1, 0, span], gate_out),
                (c_hbm.at[1, 0, span], c_out),
                (out_grad_hbm.at[1, 0, span], out_grad_out),
                (rows_hbm.at[pl.ds(steps, 2 * steps)], rows_out),
            ]
        )
    ]

    @pl.when((level == 0) & (step == 0))
    def _():
        start_all(copies)

    @pl.when(step == 0)
    def _():
        pack(rows_ref, packs)
        state[...] = jnp.zeros_like(state)

    rows, packed = rows_ref[step], packs[step]
    current = state[...]
    for j in range(CHUNK):
        x, b, c = x_ref[0, 0, block(j)], b_ref[0, 0, block(j)], c_ref[0, 0, block(j)]
        within = weighted(heads, j, rows, packed, x, b, c)
        carried = dot(c, current.astype(BF16), 1, 0) * spread(packed, FROM_BLOCK, j, heads)
        out_ref[0, block(j)] = (within + carried).astype(BF16)
        turned_ref[0, :, block(j)] = turn(c).astype(BF16)
        decayed = (x.astype(F32) * spread(packed, TO_BLOCK, j, heads)).astype(BF16)
        factor = spread(packed[BLOCK - 1 :], FROM_BLOCK, j, heads)
        current = current * factor + dot(b, decayed, 0, 0)
    state[...] = current

    @pl.when((level == 0) & (step == 0))
    def _():
        first_ref[...] = out_ref[0, :FIRST]

    @pl.when((level == 1) & (step == steps - 1))
    def _():
        wait_all(copies)


def readout_body(heads, steps, local_hbm, gate_hbm, c_hbm, out_grad_hbm, turned_hbm, local_ref,
                 gate_ref, c_ref, out_grad_ref, rows_ref, start_ref, gain_ref, first_sums_ref,
                 scaled_act, gated_act, turned, lines, sums, local, gate, out_grad, c, sems,
                 turned_sem):
    early = FIRST // BLOCK
    pieces = [(0, early, CHUNK - early)]
    pieces += [(at, step * CHUNK, CHUNK) for at in range(2) for step in range(steps)][1:]
    copies = piece_copies(
        [
            lambda at, span: c_hbm.at[at + 1, 0, span],
            lambda at, span: local_hbm.at[at, span],
            lambda at, span: gate_hbm.at[at + 1, 0, span],
            lambda at, span: out_grad_hbm.at[at + 1, 0, span],
        ],
        [c, local, gate, out_grad],
        sems,
        pieces,
    )
    turned_copy = pltpu.make_async_copy(turned_hbm, turned, turned_sem)
    copies.append([turned_copy])
    start_all(copies[0] + copies[1])
    sums[0, :, :FOLD] = first_sums_ref[...]
    columns = []
    for at in range(2):
        decays = level_decays(rows_ref.at[pl.ds(at * steps, steps)], False)
        for step, line in enumerate(decays):
            lines[at * steps + step] = line
            columns.append(line.T)
    pairs = []
    for i, (at, first, count) in enumerate([(0, 0, early)] + pieces):
        if first == 0:
            start = jnp.concatenate(
                [gather_pieces(start_ref, at, h, heads) for h in range(heads)], axis=1
            ).astype(BF16)
        if i == 0:
            refs = [c_ref, local_ref, gate_ref, out_grad_ref]
        else:
            wait_all(copies[i - 1])
            start_all(sum(copies[i + 1 : i + 2], []))
            span = slice(first * BLOCK, (first + count) * BLOCK)
            refs = [buffer.at[at, span] for buffer in (c, local, gate, out_grad)]
        piece = dot(refs[0][...], start, 1, 0)
        for number in range(first, first + count):
            step, j = number // CHUNK, number % CHUNK
            mine = block(number - first)
            carried = piece[mine] * spread(columns[at * steps + step], 0, j, heads)
            place = block(number)
            _, scaled_act[at, place], gated_act[at, place], pair = gated_sums(
                carried + refs[1][mine].astype(F32), refs[2][mine], refs[3][mine], gain_ref[...]
            )
            pairs.append(pair)
            if j == CHUNK - 1:
                store_sums(sums.at[0], step, (at + 1) * FOLD, pairs)
                pairs = []
    for copy in range(1, sums.shape[0]):
        sums[copy] = sums[0]
    turned_copy.wait()


def grads_body(heads, steps, features, lines_ref, turned_ref, scaled_act_ref, gated_act_ref,
               total_ref, grad_out, send, grads, grad_sems):
    total = jnp.sum(total_ref[...], axis=0)
    outs = []
    for at in (1, 0):
        for step in range(steps):
            norm = norm_columns(total, step, (at + 1) * FOLD, features)
            span = slice(step * SPAN, (step + 1) * SPAN)
            inv_rms, back = norm[:, 0:1], norm[:, 1:2]
            grad = inv_rms * scaled_act_ref[at, span] - back * gated_act_ref[at, span]
            grads[at, span] = grad.astype(BF16)
            span = pl.ds(step * SPAN, SPAN)
            outs.append(
                pltpu.make_async_copy(
                    grads.at[at, span], grad_out.at[at, span], grad_sems.at[at * steps + step]
                )
            )
            outs[-1].start()
    for at in (1, 0):
        states = [jnp.zeros((STATE, HDIM), F32)] * heads
        for step in range(steps):
            span = slice(step * SPAN, (step + 1) * SPAN)
            turned = turned_ref[at, :, span].astype(F32)
            lines = lines_ref[at * steps + step]
            for h in range(heads):
                line = jnp.concatenate(
                    [lines[8 * j + h : 8 * j + h + 1] for j in range(CHUNK)], axis=1
                )
                decayed = (turned * line).astype(BF16)
                states[h] = states[h] + dot(decayed, grads[at, span, head(h)], 1, 0)
        scatter_pieces(send, 1 - at, states)
    wait_all(outs)


def back_chunk(heads, rows, packed, grad_of, b_ref, c_ref, state):
    current = state[...]
    for j in reversed(range(CHUNK)):
        b, c = b_ref[0, 0, block(j)], c_ref[0, 0, block(j)]
        grad = grad_of(j)
        within = weighted_back(heads, j, rows, packed, grad, b, c)
        carried = dot(b, current.astype(BF16), 1, 0) * spread(packed, TO_BLOCK, j, heads)
        yield j, (within + carried).astype(BF16)
        decayed = (grad.astype(F32) * spread(packed, FROM_BLOCK, j, heads)).astype(BF16)
        factor = spread(packed[BLOCK - 1 :], FROM_BLOCK, j, heads)
        current = current * factor + dot(c, decayed, 0, 0)
    state[...] = current


def back0_body(heads, steps, features, rows_ref, gain_ref, total_ref, gate_ref, b_ref, c_ref,
               out_grad_ref, gated_ref, partial_ref, state_grad_ref, state, packs, norms):
    step = steps - 1 - pl.program_id(0)

    @pl.when(step == steps - 1)
    def _():
        pack(rows_ref, packs)
        total = jnp.sum(total_ref[...], axis=0)
        for part in range(steps):
            norms[part] = norm_columns(total, part, 0, features)
        state[...] = jnp.zeros_like(state)

    norm = norms[step]

    def grad_of(j):
        return ssm_gradient(
            j,
            norm,
            gain_ref[...],
            gate_ref[0, 0, block(j)],
            out_grad_ref[0, 0, block(j)],
            gated_ref[0, block(j)],
        )

    for j, part in back_chunk(heads, rows_ref[step], packs[step], grad_of, b_ref, c_ref, state):
        partial_ref[0, 0, block(j)] = part

    @pl.when(step == 0)
    def _():
        for h in range(heads):
            state_grad_ref[0, 0, h] = state[:, head(h)].T


def back_body(heads, steps, rows_ref, grad_ref, b_ref, c_ref, b_hbm, rows_hbm, given_in,
              given_state, partial_ref, state_grad_ref, near_ref, near_state_ref, b_out, rows_out,
              state, packs, sems):
    level, step = 2 - pl.program_id(0), steps - 1 - pl.program_id(1)
    copies = [
        pltpu.make_async_copy(b_hbm.at[1, 0, pl.ds(0, SPAN)], b_out, sems.at[0]),
        pltpu.make_async_copy(rows_hbm.at[pl.ds(0, 2 * steps)], rows_out, sems.at[1]),
    ]

    @pl.when((level == 2) & (step == steps - 1))
    def _():
        start_all(copies)

    @pl.when(step == steps - 1)
    def _():
        pack(rows_ref, packs)
        state[...] = jnp.zeros_like(state)

    def grad_of(j):
        return grad_ref[0, block(j)]

    for j, part in back_chunk(heads, rows_ref[step], packs[step], grad_of, b_ref, c_ref, state):
        partial_ref[0, 0, block(j)] = part

    @pl.when(step == 0)
    def _():
        for h in range(heads):
            state_grad_ref[0, 0, h] = state[:, head(h)].T

    @pl.when((level == 1) & (step == 0))
    def _():
        near_ref[...] = partial_ref[0, 0]
        near_state_ref[...] = state_grad_ref[0, 0]
        wait_all(copies)


def inputs_body(heads, steps, b_hbm, partial_hbm, local_hbm, b_ref, partial_ref, local_ref,
                rows_ref, end_ref, input_grad_out, state_grad_out, b, partial, grads, states, sems,
                local_sem, out_sems, state_sems):
    chunks = [(level, step) for level in (1, 0) for step in range(steps)]
    pieces = [(level, step * CHUNK, CHUNK) for level, step in chunks[1:]]
    copies = piece_copies(
        [lambda at, span: b_hbm.at[at, 0, span], lambda at, span: partial_hbm.at[at, 0, span]],
        [b, partial],
        sems,
        pieces,
    )
    local_copy = pltpu.make_async_copy(local_hbm.at[0, 0], states.at[0], local_sem)
    start_all(copies[0])
    local_copy.start()
    for some in copies[1:]:
        start_all(some)
    outs = []
    for i, (level, step) in enumerate(chunks):
        if step == 0:
            ends = [gather_pieces(end_ref, 1 - level, h, heads) for h in range(heads)]
            rounded = jnp.concatenate(ends, axis=1).astype(BF16)
            level_rows = rows_ref.at[pl.ds(level * steps, steps)]
            columns = [line.T for line in level_decays(level_rows, True)]
            total = level_decays(level_rows, False)[-1][8 * (CHUNK - 1) :, BLOCK - 1 :]
            if level == 0:
                local_copy.wait()
            for h in range(heads):
                local = local_ref[h] if level == 1 else states[0, h]
                states[level, h] = local + (ends[h] * total[h : h + 1]).T
            outs.append(
                pltpu.make_async_copy(
                    states.at[level], state_grad_out.at[level, 0], state_sems.at[level]
                )
            )
            outs[-1].start()
        span = slice(step * SPAN, (step + 1) * SPAN)
        if i == 0:
            some_b, some_partial = b_ref, partial_ref
        else:
            wait_all(copies[i - 1])
            some_b, some_partial = b.at[level, span], partial.at[level, span]
        piece = dot(some_b[...], rounded, 1, 0)
        for j in range(CHUNK):
            extra = piece[block(j)] * spread(columns[step], 0, j, heads)
            grads[level, block(step * CHUNK + j)] = (
                some_partial[block(j)].astype(F32) + extra
            ).astype(BF16)
        span = pl.ds(step * SPAN, SPAN)
        outs.append(
            pltpu.make_async_copy(
                grads.at[level, span], input_grad_out.at[level, 0, span], out_sems.at[i]
            )
        )
        outs[-1].start()
    wait_all(outs)


def shards(features, head_devices, ssm_input, gate_input, b_input, c_output, log_decay,
           root_state, norm_gain, out_grad, parent_ids):
    levels, _, length, columns = ssm_input.shape
    heads = columns // HDIM
    blocks = length // BLOCK
    steps = blocks // CHUNK
    segments = parent_ids.shape[1]
    rows = STATE // segments
    gain = norm_gain.reshape(1, columns)
    decay = jnp.transpose(log_decay, (0, 2, 1, 3))

    smem = pl.BlockSpec(memory_space=pltpu.SMEM)
    vmem = pl.BlockSpec(memory_space=pltpu.VMEM)
    anywhere = pl.BlockSpec(memory_space=pl.ANY)
    rows_shape = (levels * steps, WIDTH, BLOCK)
    pair_shape = (segments, 2 * heads * rows, HDIM)
    first_shape = (segments, 2 * heads * rows + 8, HDIM)
    sums_shape = (head_devices, 8, levels * FOLD)
    state_shape = (levels, 1, heads, HDIM, STATE)
    state_scratch = pltpu.VMEM((STATE, columns), F32)
    packs_scratch = pltpu.VMEM((steps, BLOCK, 128), F32)
    dma = pltpu.SemaphoreType.DMA

    far = lambda array: pin(array, pltpu.HBM)
    near = lambda array: pin(array, pltpu.VMEM)
    x, gate, out_grad = far(ssm_input), far(gate_input), far(out_grad)
    decay = far(decay)
    b, c, root = far(b_input), far(c_output), far(root_state)

    def pair_of_levels(width):
        return pltpu.VMEM((2, length, width), BF16)

    def tokens(width, place):
        return pl.BlockSpec((1, 1, SPAN, width), lambda *g: (place(*g)[0], 0, place(*g)[1], 0))

    def flat(width, place):
        return pl.BlockSpec((1, SPAN, width), lambda *g: (*place(*g), 0))

    def level_rows(place):
        return pl.BlockSpec((steps,) + rows_shape[1:], lambda *g: (place(*g)[0], 0, 0))

    def state_grads(place):
        return pl.BlockSpec((1, 1, heads, HDIM, STATE), lambda *g: (place(*g)[0], 0, 0, 0, 0))

    exchange = functools.partial(
        lax.all_to_all, axis_name="seg", split_axis=0, concat_axis=0, tiled=True
    )

    send, cum_rows = call(
        functools.partial(states_body, heads, steps),
        "states",
        6,
        in_specs=[anywhere] * 4,
        out_specs=[vmem, anywhere],
        out_shape=[pltpu.VMEM(first_shape, F32), pltpu.HBM(rows_shape, F32)],
        scratch_shapes=[
            pltpu.VMEM((levels * blocks * 8, BLOCK), F32),
            pltpu.VMEM(rows_shape, F32),
            pltpu.VMEM(decay.shape, F32),
            pltpu.VMEM(root_state.shape[1:], F32),
            pair_of_levels(columns),
            pair_of_levels(STATE),
            dma,
            dma,
            dma((4, 2)),
            dma,
        ],
    )(decay, root, x, b)
    got = exchange(send)

    own = lambda k: (0, k)
    gated0, sums0 = call(
        functools.partial(forward0_body, heads, steps),
        "forward0",
        6,
        grid=(steps,),
        in_specs=[
            level_rows(own),
            whole(root_state),
            whole(gain),
            tokens(columns, own),
            tokens(columns, own),
            tokens(STATE, own),
            tokens(STATE, own),
            tokens(columns, own),
        ],
        out_specs=[flat(columns, own), pl.BlockSpec((8, FOLD), lambda _: (0, 0))],
        out_shape=[pltpu.HBM((1, length, columns), BF16), pltpu.HBM((8, FOLD), F32)],
        scratch_shapes=[state_scratch, packs_scratch],
    )(far(cum_rows), root, gain, x, gate, b, c, out_grad)

    got, sums0 = lax.optimization_barrier((got, sums0))
    picked, decays = call(
        functools.partial(pick_body, heads),
        "pick",
        1,
        in_specs=[smem, vmem],
        out_specs=[vmem, vmem],
        out_shape=[pltpu.VMEM(pair_shape, F32), pltpu.VMEM((segments, 8, HDIM), F32)],
    )(parent_ids, near(got))

    picked, late_rows = lax.optimization_barrier((picked, cum_rows))
    starts = exchange(picked)
    both = lambda l, k: (l, k)
    later = lambda l, k: (l + 1, k)
    local, turned, *first = call(
        functools.partial(local_body, heads, steps),
        "local",
        7,
        grid=(2, steps),
        in_specs=[
            level_rows(later),
            tokens(columns, later),
            tokens(STATE, later),
            tokens(STATE, later),
        ]
        + [anywhere] * 4,
        out_specs=[
            flat(columns, both),
            pl.BlockSpec((1, STATE, SPAN), lambda l, k: (l, 0, k)),
            pl.BlockSpec((FIRST, columns), lambda l, k: (0, 0)),
        ]
        + [anywhere] * 4,
        out_shape=[
            pltpu.HBM((2, length, columns), BF16),
            pltpu.HBM((2, STATE, length), BF16),
            pltpu.VMEM((FIRST, columns), BF16),
            pltpu.VMEM((FIRST, columns), BF16),
            pltpu.VMEM((FIRST, STATE), BF16),
            pltpu.VMEM((FIRST, columns), BF16),
            pltpu.VMEM((2 * steps,) + rows_shape[1:], F32),
        ],
        scratch_shapes=[state_scratch, packs_scratch, dma((4,))],
    )(far(late_rows), x, b, c, gate, c, out_grad, far(late_rows))

    scaled_act, gated_act, turned, lines, sums = call(
        functools.partial(readout_body, heads, steps),
        "readout",
        5,
        in_specs=[anywhere] * 5 + [vmem] * 8,
        out_specs=[vmem] * 5,
        out_shape=[
            pltpu.VMEM((2, length, columns), F32),
            pltpu.VMEM((2, length, columns), F32),
            pltpu.VMEM((2, STATE, length), BF16),
            pltpu.VMEM((2 * steps,) + rows_shape[1:], F32),
            pltpu.VMEM(sums_shape, F32),
        ],
        scratch_shapes=[
            pair_of_levels(columns),
            pair_of_levels(columns),
            pair_of_levels(columns),
            pair_of_levels(STATE),
            dma((2 * steps, 4)),
            dma,
        ],
    )(
        far(local),
        gate,
        c,
        out_grad,
        far(turned),
        near(first[0]),
        near(first[1]),
        near(first[2]),
        near(first[3]),
        near(first[4]),
        near(starts),
        gain,
        sums0,
    )
    totals = lax.all_to_all(sums, "head", split_axis=0, concat_axis=0, tiled=True)

    grads, send_back = call(
        functools.partial(grads_body, heads, steps, features),
        "grads",
        4,
        in_specs=[vmem] * 5,
        out_specs=[anywhere, vmem],
        out_shape=[pltpu.HBM((2, length, columns), BF16), pltpu.VMEM(pair_shape, F32)],
        scratch_shapes=[pair_of_levels(columns), dma((2 * steps,))],
    )(near(lines), near(turned), near(scaled_act), near(gated_act), near(totals))
    got_back = exchange(send_back)

    own_back = lambda k: (0, steps - 1 - k)
    given = call(
        functools.partial(back0_body, heads, steps, features),
        "back0",
        6,
        grid=(steps,),
        in_specs=[
            level_rows(own_back),
            whole(gain),
            pl.BlockSpec(sums_shape, lambda _: (0, 0, 0)),
            tokens(columns, own_back),
            tokens(STATE, own_back),
            tokens(STATE, own_back),
            tokens(columns, own_back),
            flat(columns, own_back),
        ],
        out_specs=[tokens(columns, own_back), state_grads(own_back)],
        out_shape=[pltpu.HBM(ssm_input.shape, BF16), pltpu.HBM(state_shape, F32)],
        scratch_shapes=[state_scratch, packs_scratch, pltpu.VMEM((steps, SPAN, 8), F32)],
    )(far(cum_rows), gain, totals, gate, b, c, out_grad, far(gated0))

    got_back, *given = lax.optimization_barrier((got_back, *given))
    folded = call(
        functools.partial(fold_body, heads),
        "fold",
        1,
        in_specs=[smem, vmem, vmem],
        out_specs=vmem,
        out_shape=pltpu.VMEM(pair_shape, F32),
    )(parent_ids, near(decays), near(got_back))

    folded, late_rows = lax.optimization_barrier((folded, cum_rows))
    ends = exchange(folded)
    down_back = lambda l, k: (2 - l, steps - 1 - k)
    both_down_back = lambda l, k: (1 - l, steps - 1 - k)
    *given, near_partial, near_state, near_b, near_rows = call(
        functools.partial(back_body, heads, steps),
        "back",
        8,
        grid=(2, steps),
        in_specs=[
            level_rows(down_back),
            flat(columns, both_down_back),
            tokens(STATE, down_back),
            tokens(STATE, down_back),
        ]
        + [anywhere] * 4,
        out_specs=[
            tokens(columns, down_back),
            state_grads(down_back),
            pl.BlockSpec((SPAN, columns), lambda *g: (0, 0)),
            pl.BlockSpec((heads, HDIM, STATE), lambda *g: (0, 0, 0)),
            anywhere,
            anywhere,
        ],
        out_shape=[
            pltpu.HBM(ssm_input.shape, BF16),
            pltpu.HBM(state_shape, F32),
            pltpu.VMEM((SPAN, columns), BF16),
            pltpu.VMEM(state_shape[2:], F32),
            pltpu.VMEM((SPAN, STATE), BF16),
            pltpu.VMEM((2 * steps,) + rows_shape[1:], F32),
        ],
        input_output_aliases={6: 0, 7: 1},
        scratch_shapes=[state_scratch, packs_scratch, dma((2,))],
    )(far(late_rows), far(grads), b, c, b, far(late_rows), *given)

    return call(
        functools.partial(inputs_body, heads, steps),
        "inputs",
        4,
        in_specs=[anywhere] * 3 + [vmem] * 5,
        out_specs=[anywhere, anywhere],
        out_shape=[pltpu.HBM(ssm_input.shape, BF16), pltpu.HBM(state_shape, F32)],
        input_output_aliases={1: 0, 2: 1},
        scratch_shapes=[
            pair_of_levels(STATE),
            pair_of_levels(columns),
            pair_of_levels(columns),
            pltpu.VMEM((2,) + state_shape[2:], F32),
            dma((2 * steps - 1, 2)),
            dma,
            dma((2 * steps,)),
            dma((2,)),
        ],
    )(b, *given, near(near_b), near(near_partial), near(near_state), near(near_rows), near(ends))


def solution(mesh):
    in_specs = (
        P(None, "seg", None, "head"),
        P(None, "seg", None, "head"),
        P(None, "seg", None, None),
        P(None, "seg", None, None),
        P(None, "seg", "head", None),
        P("seg", "head", None, None),
        P("head"),
        P(None, "seg", None, "head"),
        P(),
    )
    out_specs = (P(None, "seg", None, "head"), P(None, "seg", "head", None, None))

    def run(*arrays):
        body = functools.partial(shards, arrays[0].shape[3], mesh.shape["head"])
        return tuple(
            jax.shard_map(
                body, mesh=mesh, in_specs=in_specs, out_specs=out_specs, check_vma=False
            )(*arrays)
        )

    return run
```

```python
import functools
import math

import jax
import jax.numpy as jnp
from jax import lax
from jax.experimental import pallas as pl
from jax.experimental.pallas import tpu as pltpu
from jax.sharding import PartitionSpec as P

BLOCK = 256
HALF = BLOCK // 2
HEADS = 24
HDIM = 128
STATE = 256
CHUNK = 3
SPAN = CHUNK * BLOCK
FIRST = 2 * BLOCK
FOLD = SPAN // 2
EPSILON = 1e-05
VMEM_LIMIT = 24 * 1024 * 1024
LOG2E = math.log2(math.e)

WIDTH = 8 * CHUNK
CUM = 0
FROM_BLOCK = WIDTH
TO_BLOCK = 2 * WIDTH

F32 = jnp.float32
BF16 = jnp.bfloat16
shaped = jax.ShapeDtypeStruct
pin = pltpu.with_memory_space_constraint


def call(body, name, micros, **kwargs):
    return pl.pallas_call(
        body,
        name=name,
        compiler_params=pltpu.CompilerParams(vmem_limit_bytes=VMEM_LIMIT),
        cost_estimate=pl.CostEstimate(
            flops=int(micros * 1e9), bytes_accessed=int(micros * 3e6), transcendentals=0
        ),
        **kwargs,
    )


def whole(array):
    rank = len(array.shape)
    return pl.BlockSpec(array.shape, lambda *_: (0,) * rank)


def dot(left, right, left_dim, right_dim, precision=None):
    return lax.dot_general(
        left,
        right,
        (((left_dim,), (right_dim,)), ((), ())),
        precision=precision,
        preferred_element_type=F32,
    )


def spread(packed, group, j, heads):
    at = group + 8 * j
    return jnp.concatenate(
        [
            jnp.broadcast_to(packed[:, at + h : at + h + 1], (packed.shape[0], HDIM))
            for h in range(heads)
        ],
        axis=1,
    )


def block(j):
    return slice(j * BLOCK, (j + 1) * BLOCK)


def head(h):
    return slice(h * HDIM, (h + 1) * HDIM)


def turn(values):
    size = values.shape[0]
    unit = lax.broadcasted_iota(jnp.int32, (size, size), 0) == lax.broadcasted_iota(
        jnp.int32, (size, size), 1
    )
    return dot(jnp.where(unit, 1.0, 0.0).astype(BF16), values, 1, 1)


def silu(values):
    half = 0.5 * values
    return half + half * jnp.tanh(half)


def scatter_pieces(send, number, states):
    rows = STATE // send.shape[0]
    for piece in range(send.shape[0]):
        for h, state in enumerate(states):
            at = (number * len(states) + h) * rows
            send[piece, at : at + rows] = state[piece * rows : (piece + 1) * rows]


def gather_pieces(got, number, h, heads):
    rows = STATE // got.shape[0]
    at = (number * heads + h) * rows
    return got[:, at : at + rows].reshape(STATE, HDIM)


def start_all(copies):
    for copy in copies:
        copy.start()


def wait_all(copies):
    for copy in copies:
        copy.wait()


def piece_copies(sources, targets, sems, pieces):
    result = []
    for i, (at, first, count) in enumerate(pieces):
        rows = pl.ds(first * BLOCK, count * BLOCK)
        result.append(
            [
                pltpu.make_async_copy(source(at, rows), target.at[at, rows], sems.at[i, a])
                for a, (source, target) in enumerate(zip(sources, targets))
            ]
        )
    return result


def block_ends(parts):
    lasts = [part[:, BLOCK - 1 :] for part in parts]
    before = [jnp.zeros((8, 1), F32)]
    for last in lasts[:-1]:
        before.append(before[-1] + last)
    after = [jnp.zeros((8, 1), F32)]
    for last in lasts[:0:-1]:
        after.insert(0, after[0] + last)
    return lasts, before, after


def states_body(heads, steps, decay_hbm, root_hbm, x_hbm, b_hbm, send, rows_out, rates, rows, decay,
                root, x, b, decay_sem, root_sem, sems, out_sem):
    blocks = steps * CHUNK
    decay_copy = pltpu.make_async_copy(decay_hbm, decay, decay_sem)
    decay_copy.start()
    pieces = [(0, 0, CHUNK), (0, CHUNK, CHUNK), (1, 0, CHUNK), (1, CHUNK, CHUNK)]
    copies = piece_copies(
        [lambda at, span: x_hbm.at[at, 0, span], lambda at, span: b_hbm.at[at, 0, span]],
        [x, b],
        sems,
        pieces,
    )
    root_copy = pltpu.make_async_copy(root_hbm.at[0], root, root_sem)
    start_all(copies[0])
    root_copy.start()

    rates[...] = jnp.zeros_like(rates)
    upper = (
        lax.broadcasted_iota(jnp.int32, (BLOCK, BLOCK), 0)
        <= lax.broadcasted_iota(jnp.int32, (BLOCK, BLOCK), 1)
    )
    upper = jnp.where(upper, 1.0, 0.0).astype(BF16)
    decay_copy.wait()
    start_all(copies[1])
    for level in range(decay.shape[0]):
        for number in range(blocks):
            for h in range(heads):
                row = 8 * (level * blocks + number) + h
                rates[row : row + 1] = decay[level, h, :, block(number)]
    rest = rates[...]
    sums = jnp.zeros_like(rest)
    for _ in range(3):
        part = rest.astype(BF16)
        rest = rest - part.astype(F32)
        sums = sums + dot(part, upper, 1, 0)
    sums = sums * -LOG2E
    for chunk in range(rows.shape[0]):
        rows[chunk] = sums[WIDTH * chunk : WIDTH * (chunk + 1)]
    rows_copy = pltpu.make_async_copy(rows, rows_out, out_sem)
    rows_copy.start()

    to_level = []
    totals = []
    for level in range(2):
        numbers = range(level * blocks, (level + 1) * blocks)
        parts = [sums[8 * number : 8 * number + 8] for number in numbers]
        lasts, _, after = block_ends(parts)
        for part, last, suffix in zip(parts, lasts, after):
            to_level.append(jnp.exp2(last - part + suffix))
        totals.append(jnp.exp2(after[0] + lasts[0]))

    root_copy.wait()
    states = [(root[h] * totals[0][h : h + 1]).T for h in range(heads)]
    for i, (level, first, count) in enumerate(pieces):
        if (level, first) == (1, 0):
            scatter_pieces(send, 0, states)
            states = [jnp.zeros((STATE, HDIM), F32)] * heads
        wait_all(copies[i])
        if i > 0:
            start_all(sum(copies[i + 1 : i + 2], []))
        numbers = range(first, first + count)
        turned = [turn(b[level, block(number)]) for number in numbers]
        span = slice(first * BLOCK, (first + count) * BLOCK)
        for h in range(heads):
            decayed = [
                (values * to_level[level * blocks + number][h : h + 1]).astype(BF16)
                for number, values in zip(numbers, turned)
            ]
            states[h] = states[h] + dot(
                jnp.concatenate(decayed, axis=1), x[level, span, head(h)], 1, 0
            )
    scatter_pieces(send, 1, states)
    decays = jnp.broadcast_to(totals[1], (8, HDIM))
    for piece in range(send.shape[0]):
        send[piece, send.shape[1] - 8 :] = decays
    rows_copy.wait()


def level_decays(rows, to_end):
    steps = rows.shape[0]
    parts = [rows[step, 8 * j : 8 * j + 8] for step in range(steps) for j in range(CHUNK)]
    lasts, before, after = block_ends(parts)
    if to_end:
        lines = [last - part + end for part, last, end in zip(parts, lasts, after)]
    else:
        lines = [start + part for part, start in zip(parts, before)]
    return [
        jnp.exp2(jnp.concatenate(lines[step * CHUNK : (step + 1) * CHUNK], axis=0))
        for step in range(steps)
    ]


def pack(rows, packed):
    for step in range(packed.shape[0]):
        part = rows[step]
        last = jnp.concatenate(
            [
                jnp.broadcast_to(part[8 * j : 8 * j + 8, BLOCK - 1 :], (8, BLOCK))
                for j in range(CHUNK)
            ],
            axis=0,
        )
        packed[step] = jnp.concatenate(
            [
                part,
                jnp.exp2(part),
                jnp.exp2(last - part),
                jnp.zeros((128 - 3 * WIDTH, BLOCK), F32),
            ],
            axis=0,
        ).T


def pick_body(heads, parent_ref, got_ref, send, decay_out):
    segments = got_ref.shape[0]
    rows = STATE // segments
    pair = send.shape[1]
    half = pair // 2
    for seg in range(segments):
        first = parent_ref[0, seg]
        second = parent_ref[1, seg]
        root = parent_ref[0, second]
        send[seg, :half] = got_ref[first, :half]
        decay = got_ref[second, pair : pair + 8]
        decay_out[seg] = got_ref[seg, pair : pair + 8]
        for h in range(heads):
            a = slice(h * rows, (h + 1) * rows)
            b = slice(half + h * rows, half + (h + 1) * rows)
            send[seg, b] = decay[h : h + 1] * got_ref[root, a] + got_ref[second, b]


def fold_body(heads, parent_ref, decay_ref, got_ref, send):
    rows = STATE // got_ref.shape[0]
    half = send.shape[1] // 2
    send[...] = jnp.zeros_like(send)
    for seg in range(got_ref.shape[0]):
        second = parent_ref[1, seg]
        send[second, :half] += got_ref[seg, :half]
    for seg in range(got_ref.shape[0]):
        first = parent_ref[0, seg]
        decay = decay_ref[seg]
        for h in range(heads):
            a = slice(h * rows, (h + 1) * rows)
            b = slice(half + h * rows, half + (h + 1) * rows)
            send[first, b] += decay[h : h + 1] * send[seg, a] + got_ref[seg, b]


def causal_mask(transposed):
    first = lax.broadcasted_iota(jnp.int32, (HALF, HALF), 0)
    second = lax.broadcasted_iota(jnp.int32, (HALF, HALF), 1)
    return first <= second if transposed else first >= second


def weighted(heads, j, rows, packed, x, b, c):
    scores = dot(c, b, 1, 1)
    causal = causal_mask(False)
    results = []
    for h in range(heads):
        row = rows[8 * j + h : 8 * j + h + 1]
        col = packed[:, CUM + 8 * j + h : CUM + 8 * j + h + 1]
        first = jnp.where(causal, col[:HALF] - row[:, :HALF], -jnp.inf)
        last = jnp.where(causal, col[HALF:] - row[:, HALF:], -jnp.inf)
        across = col[HALF:] - row[:, :HALF]
        top = jnp.concatenate(
            [(scores[:HALF, :HALF] * jnp.exp2(first)).astype(BF16), jnp.zeros((HALF, HALF), BF16)],
            axis=1,
        )
        bottom = jnp.concatenate(
            [
                (scores[HALF:, :HALF] * jnp.exp2(across)).astype(BF16),
                (scores[HALF:, HALF:] * jnp.exp2(last)).astype(BF16),
            ],
            axis=1,
        )
        results.append(dot(jnp.concatenate([top, bottom], axis=0), x[:, head(h)], 1, 0))
    return jnp.concatenate(results, axis=1)


def weighted_back(heads, j, rows, packed, grad, b, c):
    scores = dot(b, c, 1, 1)
    causal = causal_mask(True)
    results = []
    for h in range(heads):
        row = rows[8 * j + h : 8 * j + h + 1]
        col = packed[:, CUM + 8 * j + h : CUM + 8 * j + h + 1]
        first = jnp.where(causal, row[:, :HALF] - col[:HALF], -jnp.inf)
        last = jnp.where(causal, row[:, HALF:] - col[HALF:], -jnp.inf)
        across = row[:, HALF:] - col[:HALF]
        top = jnp.concatenate(
            [
                (scores[:HALF, :HALF] * jnp.exp2(first)).astype(BF16),
                (scores[:HALF, HALF:] * jnp.exp2(across)).astype(BF16),
            ],
            axis=1,
        )
        bottom = jnp.concatenate(
            [jnp.zeros((HALF, HALF), BF16), (scores[HALF:, HALF:] * jnp.exp2(last)).astype(BF16)],
            axis=1,
        )
        results.append(dot(jnp.concatenate([top, bottom], axis=0), grad[:, head(h)], 1, 0))
    return jnp.concatenate(results, axis=1)


def gated_sums(ssm_out, gate, out_grad, gain):
    act = silu(gate.astype(F32))
    gated = ssm_out * act
    scaled = out_grad.astype(F32) * gain
    ones = jnp.ones((8, gated.shape[1]), BF16)
    squares = dot(ones, (gated * gated).astype(BF16), 1, 1)
    products = dot(ones, (scaled * gated).astype(BF16), 1, 1)
    return gated, scaled * act, gated * act, (squares[:1], products[:1])


def store_sums(sums, step, at, pairs):
    for q in range(2):
        line = jnp.concatenate([pair[q] for pair in pairs], axis=1)
        for half in range(2):
            sums[4 * step + 2 * q + half : 4 * step + 2 * q + half + 1, at : at + FOLD] = line[
                :, half * FOLD : (half + 1) * FOLD
            ]


def norm_columns(total, step, at, features):
    lines = [total[4 * step + i : 4 * step + i + 1, at : at + FOLD] for i in range(4)]
    squares = jnp.concatenate(lines[:2], axis=1) / features
    dots = jnp.concatenate(lines[2:], axis=1) / features
    inv_rms = lax.rsqrt(squares + EPSILON)
    back = inv_rms * inv_rms * inv_rms * dots
    return jnp.concatenate([inv_rms, back, jnp.zeros((6, SPAN), F32)], axis=0).T


def ssm_gradient(j, norm, gain, gate, out_grad, gated):
    inv_rms, back = norm[block(j), 0:1], norm[block(j), 1:2]
    grad = inv_rms * (out_grad.astype(F32) * gain) - gated.astype(F32) * back
    return (grad * silu(gate.astype(F32))).astype(BF16)


def forward0_body(heads, steps, rows_ref, root_ref, gain_ref, x_ref, gate_ref, b_ref, c_ref,
                  out_grad_ref, gated_ref, sums_ref, state, packs):
    step = pl.program_id(0)

    @pl.when(step == 0)
    def _():
        pack(rows_ref, packs)
        for h in range(heads):
            state[:, head(h)] = root_ref[0, h].T

    rows, packed = rows_ref[step], packs[step]
    current = state[...]
    pairs = []
    for j in range(CHUNK):
        x, b, c = x_ref[0, 0, block(j)], b_ref[0, 0, block(j)], c_ref[0, 0, block(j)]
        within = weighted(heads, j, rows, packed, x, b, c)
        carried = dot(c, current.astype(BF16), 1, 0) * spread(packed, FROM_BLOCK, j, heads)
        gated, _, _, pair = gated_sums(
            within + carried, gate_ref[0, 0, block(j)], out_grad_ref[0, 0, block(j)], gain_ref[...]
        )
        gated_ref[0, block(j)] = gated.astype(BF16)
        pairs.append(pair)
        decayed = (x.astype(F32) * spread(packed, TO_BLOCK, j, heads)).astype(BF16)
        factor = spread(packed[BLOCK - 1 :], FROM_BLOCK, j, heads)
        current = current * factor + dot(b, decayed, 0, 0)
    state[...] = current
    for part in range(steps):

        @pl.when(step == part)
        def _():
            store_sums(sums_ref, part, 0, pairs)


def local_body(heads, steps, rows_ref, x_ref, b_ref, c_ref, gate_hbm, c_hbm, out_grad_hbm,
               rows_hbm, out_ref, turned_ref, first_ref, gate_out, c_out, out_grad_out, rows_out,
               state, packs, sems):
    level, step = pl.program_id(0), pl.program_id(1)
    span = pl.ds(0, FIRST)
    copies = [
        pltpu.make_async_copy(source, target, sems.at[i])
        for i, (source, target) in enumerate(
            [
                (gate_hbm.at[1, 0, span], gate_out),
                (c_hbm.at[1, 0, span], c_out),
                (out_grad_hbm.at[1, 0, span], out_grad_out),
                (rows_hbm.at[pl.ds(steps, 2 * steps)], rows_out),
            ]
        )
    ]

    @pl.when((level == 0) & (step == 0))
    def _():
        start_all(copies)

    @pl.when(step == 0)
    def _():
        pack(rows_ref, packs)
        state[...] = jnp.zeros_like(state)

    rows, packed = rows_ref[step], packs[step]
    current = state[...]
    for j in range(CHUNK):
        x, b, c = x_ref[0, 0, block(j)], b_ref[0, 0, block(j)], c_ref[0, 0, block(j)]
        within = weighted(heads, j, rows, packed, x, b, c)
        carried = dot(c, current.astype(BF16), 1, 0) * spread(packed, FROM_BLOCK, j, heads)
        out_ref[0, block(j)] = (within + carried).astype(BF16)
        turned_ref[0, :, block(j)] = turn(c).astype(BF16)
        decayed = (x.astype(F32) * spread(packed, TO_BLOCK, j, heads)).astype(BF16)
        factor = spread(packed[BLOCK - 1 :], FROM_BLOCK, j, heads)
        current = current * factor + dot(b, decayed, 0, 0)
    state[...] = current

    @pl.when((level == 0) & (step == 0))
    def _():
        first_ref[...] = out_ref[0, :FIRST]

    @pl.when((level == 1) & (step == steps - 1))
    def _():
        wait_all(copies)


def readout_body(heads, steps, local_hbm, gate_hbm, c_hbm, out_grad_hbm, turned_hbm, local_ref,
                 gate_ref, c_ref, out_grad_ref, rows_ref, start_ref, gain_ref, first_sums_ref,
                 scaled_act, gated_act, turned, lines, sums, local, gate, out_grad, c, sems,
                 turned_sem):
    early = FIRST // BLOCK
    pieces = [(0, early, CHUNK - early)]
    pieces += [(at, step * CHUNK, CHUNK) for at in range(2) for step in range(steps)][1:]
    copies = piece_copies(
        [
            lambda at, span: c_hbm.at[at + 1, 0, span],
            lambda at, span: local_hbm.at[at, span],
            lambda at, span: gate_hbm.at[at + 1, 0, span],
            lambda at, span: out_grad_hbm.at[at + 1, 0, span],
        ],
        [c, local, gate, out_grad],
        sems,
        pieces,
    )
    turned_copy = pltpu.make_async_copy(turned_hbm, turned, turned_sem)
    copies.append([turned_copy])
    start_all(copies[0] + copies[1])
    sums[0, :, :FOLD] = first_sums_ref[...]
    columns = []
    for at in range(2):
        decays = level_decays(rows_ref.at[pl.ds(at * steps, steps)], False)
        for step, line in enumerate(decays):
            lines[at * steps + step] = line
            columns.append(line.T)
    pairs = []
    for i, (at, first, count) in enumerate([(0, 0, early)] + pieces):
        if first == 0:
            start = jnp.concatenate(
                [gather_pieces(start_ref, at, h, heads) for h in range(heads)], axis=1
            ).astype(BF16)
        if i == 0:
            refs = [c_ref, local_ref, gate_ref, out_grad_ref]
        else:
            wait_all(copies[i - 1])
            start_all(sum(copies[i + 1 : i + 2], []))
            span = slice(first * BLOCK, (first + count) * BLOCK)
            refs = [buffer.at[at, span] for buffer in (c, local, gate, out_grad)]
        piece = dot(refs[0][...], start, 1, 0)
        for number in range(first, first + count):
            step, j = number // CHUNK, number % CHUNK
            mine = block(number - first)
            carried = piece[mine] * spread(columns[at * steps + step], 0, j, heads)
            place = block(number)
            _, scaled_act[at, place], gated_act[at, place], pair = gated_sums(
                carried + refs[1][mine].astype(F32), refs[2][mine], refs[3][mine], gain_ref[...]
            )
            pairs.append(pair)
            if j == CHUNK - 1:
                store_sums(sums.at[0], step, (at + 1) * FOLD, pairs)
                pairs = []
    for copy in range(1, sums.shape[0]):
        sums[copy] = sums[0]
    turned_copy.wait()


def grads_body(heads, steps, features, lines_ref, turned_ref, scaled_act_ref, gated_act_ref,
               total_ref, grad_out, send, grads, grad_sems):
    total = jnp.sum(total_ref[...], axis=0)
    outs = []
    for at in (1, 0):
        for step in range(steps):
            norm = norm_columns(total, step, (at + 1) * FOLD, features)
            span = slice(step * SPAN, (step + 1) * SPAN)
            inv_rms, back = norm[:, 0:1], norm[:, 1:2]
            grad = inv_rms * scaled_act_ref[at, span] - back * gated_act_ref[at, span]
            grads[at, span] = grad.astype(BF16)
            span = pl.ds(step * SPAN, SPAN)
            outs.append(
                pltpu.make_async_copy(
                    grads.at[at, span], grad_out.at[at, span], grad_sems.at[at * steps + step]
                )
            )
            outs[-1].start()
    for at in (1, 0):
        states = [jnp.zeros((STATE, HDIM), F32)] * heads
        for step in range(steps):
            span = slice(step * SPAN, (step + 1) * SPAN)
            turned = turned_ref[at, :, span].astype(F32)
            lines = lines_ref[at * steps + step]
            for h in range(heads):
                line = jnp.concatenate(
                    [lines[8 * j + h : 8 * j + h + 1] for j in range(CHUNK)], axis=1
                )
                decayed = (turned * line).astype(BF16)
                states[h] = states[h] + dot(decayed, grads[at, span, head(h)], 1, 0)
        scatter_pieces(send, 1 - at, states)
    wait_all(outs)


def back_chunk(heads, rows, packed, grad_of, b_ref, c_ref, state):
    current = state[...]
    for j in reversed(range(CHUNK)):
        b, c = b_ref[0, 0, block(j)], c_ref[0, 0, block(j)]
        grad = grad_of(j)
        within = weighted_back(heads, j, rows, packed, grad, b, c)
        carried = dot(b, current.astype(BF16), 1, 0) * spread(packed, TO_BLOCK, j, heads)
        yield j, (within + carried).astype(BF16)
        decayed = (grad.astype(F32) * spread(packed, FROM_BLOCK, j, heads)).astype(BF16)
        factor = spread(packed[BLOCK - 1 :], FROM_BLOCK, j, heads)
        current = current * factor + dot(c, decayed, 0, 0)
    state[...] = current


def back0_body(heads, steps, features, rows_ref, gain_ref, total_ref, gate_ref, b_ref, c_ref,
               out_grad_ref, gated_ref, partial_ref, state_grad_ref, state, packs, norms):
    step = steps - 1 - pl.program_id(0)

    @pl.when(step == steps - 1)
    def _():
        pack(rows_ref, packs)
        total = jnp.sum(total_ref[...], axis=0)
        for part in range(steps):
            norms[part] = norm_columns(total, part, 0, features)
        state[...] = jnp.zeros_like(state)

    norm = norms[step]

    def grad_of(j):
        return ssm_gradient(
            j,
            norm,
            gain_ref[...],
            gate_ref[0, 0, block(j)],
            out_grad_ref[0, 0, block(j)],
            gated_ref[0, block(j)],
        )

    for j, part in back_chunk(heads, rows_ref[step], packs[step], grad_of, b_ref, c_ref, state):
        partial_ref[0, 0, block(j)] = part

    @pl.when(step == 0)
    def _():
        for h in range(heads):
            state_grad_ref[0, 0, h] = state[:, head(h)].T


def back_body(heads, steps, rows_ref, grad_ref, b_ref, c_ref, b_hbm, rows_hbm, given_in,
              given_state, partial_ref, state_grad_ref, near_ref, near_state_ref, b_out, rows_out,
              state, packs, sems):
    level, step = 2 - pl.program_id(0), steps - 1 - pl.program_id(1)
    copies = [
        pltpu.make_async_copy(b_hbm.at[1, 0, pl.ds(0, SPAN)], b_out, sems.at[0]),
        pltpu.make_async_copy(rows_hbm.at[pl.ds(0, 2 * steps)], rows_out, sems.at[1]),
    ]

    @pl.when((level == 2) & (step == steps - 1))
    def _():
        start_all(copies)

    @pl.when(step == steps - 1)
    def _():
        pack(rows_ref, packs)
        state[...] = jnp.zeros_like(state)

    def grad_of(j):
        return grad_ref[0, block(j)]

    for j, part in back_chunk(heads, rows_ref[step], packs[step], grad_of, b_ref, c_ref, state):
        partial_ref[0, 0, block(j)] = part

    @pl.when(step == 0)
    def _():
        for h in range(heads):
            state_grad_ref[0, 0, h] = state[:, head(h)].T

    @pl.when((level == 1) & (step == 0))
    def _():
        near_ref[...] = partial_ref[0, 0]
        near_state_ref[...] = state_grad_ref[0, 0]
        wait_all(copies)


def inputs_body(heads, steps, b_hbm, partial_hbm, local_hbm, b_ref, partial_ref, local_ref,
                rows_ref, end_ref, input_grad_out, state_grad_out, b, partial, grads, states, sems,
                local_sem, out_sems, state_sems):
    chunks = [(level, step) for level in (1, 0) for step in range(steps)]
    pieces = [(level, step * CHUNK, CHUNK) for level, step in chunks[1:]]
    copies = piece_copies(
        [lambda at, span: b_hbm.at[at, 0, span], lambda at, span: partial_hbm.at[at, 0, span]],
        [b, partial],
        sems,
        pieces,
    )
    local_copy = pltpu.make_async_copy(local_hbm.at[0, 0], states.at[0], local_sem)
    start_all(copies[0])
    local_copy.start()
    for some in copies[1:]:
        start_all(some)
    outs = []
    for i, (level, step) in enumerate(chunks):
        if step == 0:
            ends = [gather_pieces(end_ref, 1 - level, h, heads) for h in range(heads)]
            rounded = jnp.concatenate(ends, axis=1).astype(BF16)
            level_rows = rows_ref.at[pl.ds(level * steps, steps)]
            columns = [line.T for line in level_decays(level_rows, True)]
            total = level_decays(level_rows, False)[-1][8 * (CHUNK - 1) :, BLOCK - 1 :]
            if level == 0:
                local_copy.wait()
            for h in range(heads):
                local = local_ref[h] if level == 1 else states[0, h]
                states[level, h] = local + (ends[h] * total[h : h + 1]).T
            outs.append(
                pltpu.make_async_copy(
                    states.at[level], state_grad_out.at[level, 0], state_sems.at[level]
                )
            )
            outs[-1].start()
        span = slice(step * SPAN, (step + 1) * SPAN)
        if i == 0:
            some_b, some_partial = b_ref, partial_ref
        else:
            wait_all(copies[i - 1])
            some_b, some_partial = b.at[level, span], partial.at[level, span]
        piece = dot(some_b[...], rounded, 1, 0)
        for j in range(CHUNK):
            extra = piece[block(j)] * spread(columns[step], 0, j, heads)
            grads[level, block(step * CHUNK + j)] = (
                some_partial[block(j)].astype(F32) + extra
            ).astype(BF16)
        span = pl.ds(step * SPAN, SPAN)
        outs.append(
            pltpu.make_async_copy(
                grads.at[level, span], input_grad_out.at[level, 0, span], out_sems.at[i]
            )
        )
        outs[-1].start()
    wait_all(outs)


def shards(features, head_devices, ssm_input, gate_input, b_input, c_output, log_decay,
           root_state, norm_gain, out_grad, parent_ids):
    levels, _, length, columns = ssm_input.shape
    heads = columns // HDIM
    blocks = length // BLOCK
    steps = blocks // CHUNK
    segments = parent_ids.shape[1]
    rows = STATE // segments
    gain = norm_gain.reshape(1, columns)
    decay = jnp.transpose(log_decay, (0, 2, 1, 3))

    smem = pl.BlockSpec(memory_space=pltpu.SMEM)
    vmem = pl.BlockSpec(memory_space=pltpu.VMEM)
    anywhere = pl.BlockSpec(memory_space=pl.ANY)
    rows_shape = (levels * steps, WIDTH, BLOCK)
    pair_shape = (segments, 2 * heads * rows, HDIM)
    first_shape = (segments, 2 * heads * rows + 8, HDIM)
    sums_shape = (head_devices, 8, levels * FOLD)
    state_shape = (levels, 1, heads, HDIM, STATE)
    state_scratch = pltpu.VMEM((STATE, columns), F32)
    packs_scratch = pltpu.VMEM((steps, BLOCK, 128), F32)
    dma = pltpu.SemaphoreType.DMA

    far = lambda array: pin(array, pltpu.HBM)
    near = lambda array: pin(array, pltpu.VMEM)
    x, gate, out_grad = far(ssm_input), far(gate_input), far(out_grad)
    decay = far(decay)
    b, c, root = far(b_input), far(c_output), far(root_state)

    def pair_of_levels(width):
        return pltpu.VMEM((2, length, width), BF16)

    def tokens(width, place):
        return pl.BlockSpec((1, 1, SPAN, width), lambda *g: (place(*g)[0], 0, place(*g)[1], 0))

    def flat(width, place):
        return pl.BlockSpec((1, SPAN, width), lambda *g: (*place(*g), 0))

    def level_rows(place):
        return pl.BlockSpec((steps,) + rows_shape[1:], lambda *g: (place(*g)[0], 0, 0))

    def state_grads(place):
        return pl.BlockSpec((1, 1, heads, HDIM, STATE), lambda *g: (place(*g)[0], 0, 0, 0, 0))

    exchange = functools.partial(
        lax.all_to_all, axis_name="seg", split_axis=0, concat_axis=0, tiled=True
    )

    send, cum_rows = call(
        functools.partial(states_body, heads, steps),
        "states",
        6,
        in_specs=[anywhere] * 4,
        out_specs=[vmem, anywhere],
        out_shape=[pltpu.VMEM(first_shape, F32), pltpu.HBM(rows_shape, F32)],
        scratch_shapes=[
            pltpu.VMEM((levels * blocks * 8, BLOCK), F32),
            pltpu.VMEM(rows_shape, F32),
            pltpu.VMEM(decay.shape, F32),
            pltpu.VMEM(root_state.shape[1:], F32),
            pair_of_levels(columns),
            pair_of_levels(STATE),
            dma,
            dma,
            dma((4, 2)),
            dma,
        ],
    )(decay, root, x, b)
    got = exchange(send)

    own = lambda k: (0, k)
    gated0, sums0 = call(
        functools.partial(forward0_body, heads, steps),
        "forward0",
        6,
        grid=(steps,),
        in_specs=[
            level_rows(own),
            whole(root_state),
            whole(gain),
            tokens(columns, own),
            tokens(columns, own),
            tokens(STATE, own),
            tokens(STATE, own),
            tokens(columns, own),
        ],
        out_specs=[flat(columns, own), pl.BlockSpec((8, FOLD), lambda _: (0, 0))],
        out_shape=[pltpu.HBM((1, length, columns), BF16), pltpu.HBM((8, FOLD), F32)],
        scratch_shapes=[state_scratch, packs_scratch],
    )(far(cum_rows), root, gain, x, gate, b, c, out_grad)

    got, sums0 = lax.optimization_barrier((got, sums0))
    picked, decays = call(
        functools.partial(pick_body, heads),
        "pick",
        1,
        in_specs=[smem, vmem],
        out_specs=[vmem, vmem],
        out_shape=[pltpu.VMEM(pair_shape, F32), pltpu.VMEM((segments, 8, HDIM), F32)],
    )(parent_ids, near(got))

    picked, late_rows = lax.optimization_barrier((picked, cum_rows))
    starts = exchange(picked)
    both = lambda l, k: (l, k)
    later = lambda l, k: (l + 1, k)
    local, turned, *first = call(
        functools.partial(local_body, heads, steps),
        "local",
        7,
        grid=(2, steps),
        in_specs=[
            level_rows(later),
            tokens(columns, later),
            tokens(STATE, later),
            tokens(STATE, later),
        ]
        + [anywhere] * 4,
        out_specs=[
            flat(columns, both),
            pl.BlockSpec((1, STATE, SPAN), lambda l, k: (l, 0, k)),
            pl.BlockSpec((FIRST, columns), lambda l, k: (0, 0)),
        ]
        + [anywhere] * 4,
        out_shape=[
            pltpu.HBM((2, length, columns), BF16),
            pltpu.HBM((2, STATE, length), BF16),
            pltpu.VMEM((FIRST, columns), BF16),
            pltpu.VMEM((FIRST, columns), BF16),
            pltpu.VMEM((FIRST, STATE), BF16),
            pltpu.VMEM((FIRST, columns), BF16),
            pltpu.VMEM((2 * steps,) + rows_shape[1:], F32),
        ],
        scratch_shapes=[state_scratch, packs_scratch, dma((4,))],
    )(far(late_rows), x, b, c, gate, c, out_grad, far(late_rows))

    scaled_act, gated_act, turned, lines, sums = call(
        functools.partial(readout_body, heads, steps),
        "readout",
        5,
        in_specs=[anywhere] * 5 + [vmem] * 8,
        out_specs=[vmem] * 5,
        out_shape=[
            pltpu.VMEM((2, length, columns), F32),
            pltpu.VMEM((2, length, columns), F32),
            pltpu.VMEM((2, STATE, length), BF16),
            pltpu.VMEM((2 * steps,) + rows_shape[1:], F32),
            pltpu.VMEM(sums_shape, F32),
        ],
        scratch_shapes=[
            pair_of_levels(columns),
            pair_of_levels(columns),
            pair_of_levels(columns),
            pair_of_levels(STATE),
            dma((2 * steps, 4)),
            dma,
        ],
    )(
        far(local),
        gate,
        c,
        out_grad,
        far(turned),
        near(first[0]),
        near(first[1]),
        near(first[2]),
        near(first[3]),
        near(first[4]),
        near(starts),
        gain,
        sums0,
    )
    totals = lax.all_to_all(sums, "head", split_axis=0, concat_axis=0, tiled=True)

    grads, send_back = call(
        functools.partial(grads_body, heads, steps, features),
        "grads",
        4,
        in_specs=[vmem] * 5,
        out_specs=[anywhere, vmem],
        out_shape=[pltpu.HBM((2, length, columns), BF16), pltpu.VMEM(pair_shape, F32)],
        scratch_shapes=[pair_of_levels(columns), dma((2 * steps,))],
    )(near(lines), near(turned), near(scaled_act), near(gated_act), near(totals))
    got_back = exchange(send_back)

    own_back = lambda k: (0, steps - 1 - k)
    given = call(
        functools.partial(back0_body, heads, steps, features),
        "back0",
        6,
        grid=(steps,),
        in_specs=[
            level_rows(own_back),
            whole(gain),
            pl.BlockSpec(sums_shape, lambda _: (0, 0, 0)),
            tokens(columns, own_back),
            tokens(STATE, own_back),
            tokens(STATE, own_back),
            tokens(columns, own_back),
            flat(columns, own_back),
        ],
        out_specs=[tokens(columns, own_back), state_grads(own_back)],
        out_shape=[pltpu.HBM(ssm_input.shape, BF16), pltpu.HBM(state_shape, F32)],
        scratch_shapes=[state_scratch, packs_scratch, pltpu.VMEM((steps, SPAN, 8), F32)],
    )(far(cum_rows), gain, totals, gate, b, c, out_grad, far(gated0))

    got_back, *given = lax.optimization_barrier((got_back, *given))
    folded = call(
        functools.partial(fold_body, heads),
        "fold",
        1,
        in_specs=[smem, vmem, vmem],
        out_specs=vmem,
        out_shape=pltpu.VMEM(pair_shape, F32),
    )(parent_ids, near(decays), near(got_back))

    folded, late_rows = lax.optimization_barrier((folded, cum_rows))
    ends = exchange(folded)
    down_back = lambda l, k: (2 - l, steps - 1 - k)
    both_down_back = lambda l, k: (1 - l, steps - 1 - k)
    *given, near_partial, near_state, near_b, near_rows = call(
        functools.partial(back_body, heads, steps),
        "back",
        8,
        grid=(2, steps),
        in_specs=[
            level_rows(down_back),
            flat(columns, both_down_back),
            tokens(STATE, down_back),
            tokens(STATE, down_back),
        ]
        + [anywhere] * 4,
        out_specs=[
            tokens(columns, down_back),
            state_grads(down_back),
            pl.BlockSpec((SPAN, columns), lambda *g: (0, 0)),
            pl.BlockSpec((heads, HDIM, STATE), lambda *g: (0, 0, 0)),
            anywhere,
            anywhere,
        ],
        out_shape=[
            pltpu.HBM(ssm_input.shape, BF16),
            pltpu.HBM(state_shape, F32),
            pltpu.VMEM((SPAN, columns), BF16),
            pltpu.VMEM(state_shape[2:], F32),
            pltpu.VMEM((SPAN, STATE), BF16),
            pltpu.VMEM((2 * steps,) + rows_shape[1:], F32),
        ],
        input_output_aliases={6: 0, 7: 1},
        scratch_shapes=[state_scratch, packs_scratch, dma((2,))],
    )(far(late_rows), far(grads), b, c, b, far(late_rows), *given)

    return call(
        functools.partial(inputs_body, heads, steps),
        "inputs",
        4,
        in_specs=[anywhere] * 3 + [vmem] * 5,
        out_specs=[anywhere, anywhere],
        out_shape=[pltpu.HBM(ssm_input.shape, BF16), pltpu.HBM(state_shape, F32)],
        input_output_aliases={1: 0, 2: 1},
        scratch_shapes=[
            pair_of_levels(STATE),
            pair_of_levels(columns),
            pair_of_levels(columns),
            pltpu.VMEM((2,) + state_shape[2:], F32),
            dma((2 * steps - 1, 2)),
            dma,
            dma((2 * steps,)),
            dma((2,)),
        ],
    )(b, *given, near(near_b), near(near_partial), near(near_state), near(near_rows), near(ends))


def solution(mesh):
    in_specs = (
        P(None, "seg", None, "head"),
        P(None, "seg", None, "head"),
        P(None, "seg", None, None),
        P(None, "seg", None, None),
        P(None, "seg", "head", None),
        P("seg", "head", None, None),
        P("head"),
        P(None, "seg", None, "head"),
        P(),
    )
    out_specs = (P(None, "seg", None, "head"), P(None, "seg", "head", None, None))

    def run(*arrays):
        body = functools.partial(shards, arrays[0].shape[3], mesh.shape["head"])
        return tuple(
            jax.shard_map(
                body, mesh=mesh, in_specs=in_specs, out_specs=out_specs, check_vma=False
            )(*arrays)
        )

    return run
```

```python
import functools
import math

import jax
import jax.numpy as jnp
from jax import lax
from jax.experimental import pallas as pl
from jax.experimental.pallas import tpu as pltpu
from jax.sharding import PartitionSpec as P

BLOCK = 256
HALF = BLOCK // 2
HEADS = 24
HDIM = 128
STATE = 256
CHUNK = 3
SPAN = CHUNK * BLOCK
FIRST = 2 * BLOCK
FOLD = SPAN // 2
EPSILON = 1e-05
VMEM_LIMIT = 24 * 1024 * 1024
LOG2E = math.log2(math.e)

WIDTH = 8 * CHUNK
CUM = 0
FROM_BLOCK = WIDTH
TO_BLOCK = 2 * WIDTH

F32 = jnp.float32
BF16 = jnp.bfloat16
shaped = jax.ShapeDtypeStruct
pin = pltpu.with_memory_space_constraint


def call(body, name, micros, **kwargs):
    return pl.pallas_call(
        body,
        name=name,
        compiler_params=pltpu.CompilerParams(vmem_limit_bytes=VMEM_LIMIT),
        cost_estimate=pl.CostEstimate(
            flops=int(micros * 1e9), bytes_accessed=int(micros * 3e6), transcendentals=0
        ),
        **kwargs,
    )


def whole(array):
    rank = len(array.shape)
    return pl.BlockSpec(array.shape, lambda *_: (0,) * rank)


def dot(left, right, left_dim, right_dim, precision=None):
    return lax.dot_general(
        left,
        right,
        (((left_dim,), (right_dim,)), ((), ())),
        precision=precision,
        preferred_element_type=F32,
    )


def spread(packed, group, j, heads):
    at = group + 8 * j
    return jnp.concatenate(
        [
            jnp.broadcast_to(packed[:, at + h : at + h + 1], (packed.shape[0], HDIM))
            for h in range(heads)
        ],
        axis=1,
    )


def spread_rows(lines, width):
    high = lines.astype(BF16)
    low = (lines - high.astype(F32)).astype(BF16)
    row = lax.broadcasted_iota(jnp.int32, (16, width), 0)
    lane = lax.broadcasted_iota(jnp.int32, (16, width), 1)
    chosen = jnp.where((row & 7) == (lane >> 7), 1.0, 0.0).astype(BF16)
    return dot(jnp.concatenate([high, low], axis=0), chosen, 0, 0)


def block(j):
    return slice(j * BLOCK, (j + 1) * BLOCK)


def head(h):
    return slice(h * HDIM, (h + 1) * HDIM)


def turn(values):
    size = values.shape[0]
    unit = lax.broadcasted_iota(jnp.int32, (size, size), 0) == lax.broadcasted_iota(
        jnp.int32, (size, size), 1
    )
    return dot(jnp.where(unit, 1.0, 0.0).astype(BF16), values, 1, 1)


def silu(values):
    half = 0.5 * values
    return half + half * jnp.tanh(half)


def scatter_pieces(send, number, states):
    rows = STATE // send.shape[0]
    for piece in range(send.shape[0]):
        for h, state in enumerate(states):
            at = (number * len(states) + h) * rows
            send[piece, at : at + rows] = state[piece * rows : (piece + 1) * rows]


def gather_pieces(got, number, h, heads):
    rows = STATE // got.shape[0]
    at = (number * heads + h) * rows
    return got[:, at : at + rows].reshape(STATE, HDIM)


def start_all(copies):
    for copy in copies:
        copy.start()


def wait_all(copies):
    for copy in copies:
        copy.wait()


def piece_copies(sources, targets, sems, pieces):
    result = []
    for i, (at, first, count) in enumerate(pieces):
        rows = pl.ds(first * BLOCK, count * BLOCK)
        result.append(
            [
                pltpu.make_async_copy(source(at, rows), target.at[at, rows], sems.at[i, a])
                for a, (source, target) in enumerate(zip(sources, targets))
            ]
        )
    return result


def block_ends(parts):
    lasts = [part[:, BLOCK - 1 :] for part in parts]
    before = [jnp.zeros((8, 1), F32)]
    for last in lasts[:-1]:
        before.append(before[-1] + last)
    after = [jnp.zeros((8, 1), F32)]
    for last in lasts[:0:-1]:
        after.insert(0, after[0] + last)
    return lasts, before, after


def states_body(heads, steps, decay_hbm, root_hbm, x_hbm, b_hbm, send, rows_out, rates, rows, decay,
                root, x, b, decay_sem, root_sem, sems, out_sem):
    blocks = steps * CHUNK
    decay_copy = pltpu.make_async_copy(decay_hbm, decay, decay_sem)
    decay_copy.start()
    pieces = [(0, 0, CHUNK), (0, CHUNK, CHUNK), (1, 0, CHUNK), (1, CHUNK, CHUNK)]
    copies = piece_copies(
        [lambda at, span: x_hbm.at[at, 0, span], lambda at, span: b_hbm.at[at, 0, span]],
        [x, b],
        sems,
        pieces,
    )
    root_copy = pltpu.make_async_copy(root_hbm.at[0], root, root_sem)
    start_all(copies[0])
    root_copy.start()

    rates[...] = jnp.zeros_like(rates)
    upper = (
        lax.broadcasted_iota(jnp.int32, (BLOCK, BLOCK), 0)
        <= lax.broadcasted_iota(jnp.int32, (BLOCK, BLOCK), 1)
    )
    upper = jnp.where(upper, 1.0, 0.0).astype(BF16)
    decay_copy.wait()
    start_all(copies[1])
    for level in range(decay.shape[0]):
        for number in range(blocks):
            for h in range(heads):
                row = 8 * (level * blocks + number) + h
                rates[row : row + 1] = decay[level, h, :, block(number)]
    rest = rates[...]
    sums = jnp.zeros_like(rest)
    for _ in range(3):
        part = rest.astype(BF16)
        rest = rest - part.astype(F32)
        sums = sums + dot(part, upper, 1, 0)
    sums = sums * -LOG2E
    for chunk in range(rows.shape[0]):
        rows[chunk] = sums[WIDTH * chunk : WIDTH * (chunk + 1)]
    rows_copy = pltpu.make_async_copy(rows, rows_out, out_sem)
    rows_copy.start()

    to_level = []
    totals = []
    for level in range(2):
        numbers = range(level * blocks, (level + 1) * blocks)
        parts = [sums[8 * number : 8 * number + 8] for number in numbers]
        lasts, _, after = block_ends(parts)
        for part, last, suffix in zip(parts, lasts, after):
            to_level.append(jnp.exp2(last - part + suffix))
        totals.append(jnp.exp2(after[0] + lasts[0]))

    root_copy.wait()
    states = [(root[h] * totals[0][h : h + 1]).T for h in range(heads)]
    for i, (level, first, count) in enumerate(pieces):
        if (level, first) == (1, 0):
            scatter_pieces(send, 0, states)
            states = [jnp.zeros((STATE, HDIM), F32)] * heads
        wait_all(copies[i])
        if i > 0:
            start_all(sum(copies[i + 1 : i + 2], []))
        numbers = range(first, first + count)
        turned = [turn(b[level, block(number)]) for number in numbers]
        span = slice(first * BLOCK, (first + count) * BLOCK)
        for h in range(heads):
            decayed = [
                (values * to_level[level * blocks + number][h : h + 1]).astype(BF16)
                for number, values in zip(numbers, turned)
            ]
            states[h] = states[h] + dot(
                jnp.concatenate(decayed, axis=1), x[level, span, head(h)], 1, 0
            )
    scatter_pieces(send, 1, states)
    decays = jnp.broadcast_to(totals[1], (8, HDIM))
    for piece in range(send.shape[0]):
        send[piece, send.shape[1] - 8 :] = decays
    rows_copy.wait()


def level_decays(rows, to_end):
    steps = rows.shape[0]
    parts = [rows[step, 8 * j : 8 * j + 8] for step in range(steps) for j in range(CHUNK)]
    lasts, before, after = block_ends(parts)
    if to_end:
        lines = [last - part + end for part, last, end in zip(parts, lasts, after)]
    else:
        lines = [start + part for part, start in zip(parts, before)]
    return [
        jnp.exp2(jnp.concatenate(lines[step * CHUNK : (step + 1) * CHUNK], axis=0))
        for step in range(steps)
    ]


def pack(rows, packed):
    for step in range(packed.shape[0]):
        part = rows[step]
        last = jnp.concatenate(
            [
                jnp.broadcast_to(part[8 * j : 8 * j + 8, BLOCK - 1 :], (8, BLOCK))
                for j in range(CHUNK)
            ],
            axis=0,
        )
        packed[step] = jnp.concatenate(
            [
                part,
                jnp.exp2(part),
                jnp.exp2(last - part),
                jnp.zeros((128 - 3 * WIDTH, BLOCK), F32),
            ],
            axis=0,
        ).T


def pick_body(heads, parent_ref, got_ref, send, decay_out):
    segments = got_ref.shape[0]
    rows = STATE // segments
    pair = send.shape[1]
    half = pair // 2
    for seg in range(segments):
        first = parent_ref[0, seg]
        second = parent_ref[1, seg]
        root = parent_ref[0, second]
        send[seg, :half] = got_ref[first, :half]
        decay = got_ref[second, pair : pair + 8]
        decay_out[seg] = got_ref[seg, pair : pair + 8]
        for h in range(heads):
            a = slice(h * rows, (h + 1) * rows)
            b = slice(half + h * rows, half + (h + 1) * rows)
            send[seg, b] = decay[h : h + 1] * got_ref[root, a] + got_ref[second, b]


def fold_body(heads, parent_ref, decay_ref, got_ref, send):
    rows = STATE // got_ref.shape[0]
    half = send.shape[1] // 2
    send[...] = jnp.zeros_like(send)
    for seg in range(got_ref.shape[0]):
        second = parent_ref[1, seg]
        send[second, :half] += got_ref[seg, :half]
    for seg in range(got_ref.shape[0]):
        first = parent_ref[0, seg]
        decay = decay_ref[seg]
        for h in range(heads):
            a = slice(h * rows, (h + 1) * rows)
            b = slice(half + h * rows, half + (h + 1) * rows)
            send[first, b] += decay[h : h + 1] * send[seg, a] + got_ref[seg, b]


def causal_mask(transposed):
    first = lax.broadcasted_iota(jnp.int32, (HALF, HALF), 0)
    second = lax.broadcasted_iota(jnp.int32, (HALF, HALF), 1)
    return first <= second if transposed else first >= second


def weighted(heads, j, rows, packed, x, b, c):
    scores = dot(c, b, 1, 1)
    causal = causal_mask(False)
    results = []
    for h in range(heads):
        row = rows[8 * j + h : 8 * j + h + 1]
        col = packed[:, CUM + 8 * j + h : CUM + 8 * j + h + 1]
        first = jnp.where(causal, col[:HALF] - row[:, :HALF], -jnp.inf)
        last = jnp.where(causal, col[HALF:] - row[:, HALF:], -jnp.inf)
        across = col[HALF:] - row[:, :HALF]
        top = jnp.concatenate(
            [(scores[:HALF, :HALF] * jnp.exp2(first)).astype(BF16), jnp.zeros((HALF, HALF), BF16)],
            axis=1,
        )
        bottom = jnp.concatenate(
            [
                (scores[HALF:, :HALF] * jnp.exp2(across)).astype(BF16),
                (scores[HALF:, HALF:] * jnp.exp2(last)).astype(BF16),
            ],
            axis=1,
        )
        results.append(dot(jnp.concatenate([top, bottom], axis=0), x[:, head(h)], 1, 0))
    return jnp.concatenate(results, axis=1)


def weighted_back(heads, j, rows, packed, grad, b, c):
    scores = dot(b, c, 1, 1)
    causal = causal_mask(True)
    results = []
    for h in range(heads):
        row = rows[8 * j + h : 8 * j + h + 1]
        col = packed[:, CUM + 8 * j + h : CUM + 8 * j + h + 1]
        first = jnp.where(causal, row[:, :HALF] - col[:HALF], -jnp.inf)
        last = jnp.where(causal, row[:, HALF:] - col[HALF:], -jnp.inf)
        across = row[:, HALF:] - col[:HALF]
        top = jnp.concatenate(
            [
                (scores[:HALF, :HALF] * jnp.exp2(first)).astype(BF16),
                (scores[:HALF, HALF:] * jnp.exp2(across)).astype(BF16),
            ],
            axis=1,
        )
        bottom = jnp.concatenate(
            [jnp.zeros((HALF, HALF), BF16), (scores[HALF:, HALF:] * jnp.exp2(last)).astype(BF16)],
            axis=1,
        )
        results.append(dot(jnp.concatenate([top, bottom], axis=0), grad[:, head(h)], 1, 0))
    return jnp.concatenate(results, axis=1)


def gated_sums(ssm_out, gate, out_grad, gain):
    act = silu(gate.astype(F32))
    gated = ssm_out * act
    scaled = out_grad.astype(F32) * gain
    ones = jnp.ones((8, gated.shape[1]), BF16)
    squares = dot(ones, (gated * gated).astype(BF16), 1, 1)
    products = dot(ones, (scaled * gated).astype(BF16), 1, 1)
    return gated, scaled * act, gated * act, (squares[:1], products[:1])


def store_sums(sums, step, at, pairs):
    for q in range(2):
        line = jnp.concatenate([pair[q] for pair in pairs], axis=1)
        for half in range(2):
            sums[4 * step + 2 * q + half : 4 * step + 2 * q + half + 1, at : at + FOLD] = line[
                :, half * FOLD : (half + 1) * FOLD
            ]


def norm_rows(total, step, at, features):
    lines = [total[4 * step + i : 4 * step + i + 1, at : at + FOLD] for i in range(4)]
    squares = jnp.concatenate(lines[:2], axis=1) / features
    dots = jnp.concatenate(lines[2:], axis=1) / features
    inv_rms = lax.rsqrt(squares + EPSILON)
    back = inv_rms * inv_rms * inv_rms * dots
    return jnp.concatenate([inv_rms, back, jnp.zeros((6, SPAN), F32)], axis=0)


def ssm_gradient(j, norm, gain, gate, out_grad, gated):
    inv_rms, back = norm[block(j), 0:1], norm[block(j), 1:2]
    grad = inv_rms * (out_grad.astype(F32) * gain) - gated.astype(F32) * back
    return (grad * silu(gate.astype(F32))).astype(BF16)


def forward0_body(heads, steps, rows_ref, root_ref, gain_ref, x_ref, gate_ref, b_ref, c_ref,
                  out_grad_ref, gated_ref, sums_ref, state, packs):
    step = pl.program_id(0)

    @pl.when(step == 0)
    def _():
        pack(rows_ref, packs)
        for h in range(heads):
            state[:, head(h)] = root_ref[0, h].T

    rows, packed = rows_ref[step], packs[step]
    current = state[...]
    pairs = []
    for j in range(CHUNK):
        x, b, c = x_ref[0, 0, block(j)], b_ref[0, 0, block(j)], c_ref[0, 0, block(j)]
        within = weighted(heads, j, rows, packed, x, b, c)
        carried = dot(c, current.astype(BF16), 1, 0) * spread(packed, FROM_BLOCK, j, heads)
        gated, _, _, pair = gated_sums(
            within + carried, gate_ref[0, 0, block(j)], out_grad_ref[0, 0, block(j)], gain_ref[...]
        )
        gated_ref[0, block(j)] = gated.astype(BF16)
        pairs.append(pair)
        decayed = (x.astype(F32) * spread(packed, TO_BLOCK, j, heads)).astype(BF16)
        factor = spread(packed[BLOCK - 1 :], FROM_BLOCK, j, heads)
        current = current * factor + dot(b, decayed, 0, 0)
    state[...] = current
    for part in range(steps):

        @pl.when(step == part)
        def _():
            store_sums(sums_ref, part, 0, pairs)


def local_body(heads, steps, rows_ref, x_ref, b_ref, c_ref, gate_hbm, c_hbm, out_grad_hbm,
               rows_hbm, out_ref, turned_ref, first_ref, gate_out, c_out, out_grad_out, rows_out,
               state, packs, sems):
    level, step = pl.program_id(0), pl.program_id(1)
    span = pl.ds(0, FIRST)
    copies = [
        pltpu.make_async_copy(source, target, sems.at[i])
        for i, (source, target) in enumerate(
            [
                (gate_hbm.at[1, 0, span], gate_out),
                (c_hbm.at[1, 0, span], c_out),
                (out_grad_hbm.at[1, 0, span], out_grad_out),
                (rows_hbm.at[pl.ds(steps, 2 * steps)], rows_out),
            ]
        )
    ]

    @pl.when((level == 0) & (step == 0))
    def _():
        start_all(copies)

    @pl.when(step == 0)
    def _():
        pack(rows_ref, packs)
        state[...] = jnp.zeros_like(state)

    rows, packed = rows_ref[step], packs[step]
    current = state[...]
    for j in range(CHUNK):
        x, b, c = x_ref[0, 0, block(j)], b_ref[0, 0, block(j)], c_ref[0, 0, block(j)]
        within = weighted(heads, j, rows, packed, x, b, c)
        carried = dot(c, current.astype(BF16), 1, 0) * spread(packed, FROM_BLOCK, j, heads)
        out_ref[0, block(j)] = (within + carried).astype(BF16)
        turned_ref[0, :, block(j)] = turn(c).astype(BF16)
        decayed = (x.astype(F32) * spread(packed, TO_BLOCK, j, heads)).astype(BF16)
        factor = spread(packed[BLOCK - 1 :], FROM_BLOCK, j, heads)
        current = current * factor + dot(b, decayed, 0, 0)
    state[...] = current

    @pl.when((level == 0) & (step == 0))
    def _():
        first_ref[...] = out_ref[0, :FIRST]

    @pl.when((level == 1) & (step == steps - 1))
    def _():
        wait_all(copies)


def readout_body(heads, steps, local_hbm, gate_hbm, c_hbm, out_grad_hbm, turned_hbm, local_ref,
                 gate_ref, c_ref, out_grad_ref, rows_ref, start_ref, gain_ref, first_sums_ref,
                 scaled_act, gated_act, turned, lines, sums, local, gate, out_grad, c, sems,
                 turned_sem):
    early = FIRST // BLOCK
    pieces = [(0, early, CHUNK - early)]
    pieces += [(at, step * CHUNK, CHUNK) for at in range(2) for step in range(steps)][1:]
    copies = piece_copies(
        [
            lambda at, span: c_hbm.at[at + 1, 0, span],
            lambda at, span: local_hbm.at[at, span],
            lambda at, span: gate_hbm.at[at + 1, 0, span],
            lambda at, span: out_grad_hbm.at[at + 1, 0, span],
        ],
        [c, local, gate, out_grad],
        sems,
        pieces,
    )
    turned_copy = pltpu.make_async_copy(turned_hbm, turned, turned_sem)
    copies.append([turned_copy])
    start_all(copies[0] + copies[1])
    sums[0, :, :FOLD] = first_sums_ref[...]
    decays = []
    for at in range(2):
        decays += level_decays(rows_ref.at[pl.ds(at * steps, steps)], False)
    for chunk, line in enumerate(decays):
        lines[chunk] = line
    pairs = []
    for i, (at, first, count) in enumerate([(0, 0, early)] + pieces):
        if first == 0:
            start = jnp.concatenate(
                [gather_pieces(start_ref, at, h, heads) for h in range(heads)], axis=1
            ).astype(BF16)
        if i == 0:
            refs = [c_ref, local_ref, gate_ref, out_grad_ref]
        else:
            wait_all(copies[i - 1])
            start_all(sum(copies[i + 1 : i + 2], []))
            span = slice(first * BLOCK, (first + count) * BLOCK)
            refs = [buffer.at[at, span] for buffer in (c, local, gate, out_grad)]
        piece = dot(refs[0][...], start, 1, 0)
        for number in range(first, first + count):
            step, j = number // CHUNK, number % CHUNK
            mine = block(number - first)
            line = decays[at * steps + step][8 * j : 8 * j + 8]
            carried = piece[mine] * spread_rows(line, heads * HDIM)
            place = block(number)
            _, scaled_act[at, place], gated_act[at, place], pair = gated_sums(
                carried + refs[1][mine].astype(F32), refs[2][mine], refs[3][mine], gain_ref[...]
            )
            pairs.append(pair)
            if j == CHUNK - 1:
                store_sums(sums.at[0], step, (at + 1) * FOLD, pairs)
                pairs = []
    for copy in range(1, sums.shape[0]):
        sums[copy] = sums[0]
    turned_copy.wait()


def grads_body(heads, steps, features, lines_ref, turned_ref, scaled_act_ref, gated_act_ref,
               total_ref, grad_out, send, grads, grad_sems):
    total = jnp.sum(total_ref[...], axis=0)
    outs = []
    for at in (1, 0):
        for step in range(steps):
            norm = norm_rows(total, step, (at + 1) * FOLD, features)
            for j in range(CHUNK):
                place = block(step * CHUNK + j)
                factors = spread_rows(norm[:, block(j)], 2 * HDIM)
                inv_rms, back = factors[:, :HDIM], factors[:, HDIM:]
                for h in range(heads):
                    grad = inv_rms * scaled_act_ref[at, place, head(h)]
                    grad = grad - back * gated_act_ref[at, place, head(h)]
                    grads[at, place, head(h)] = grad.astype(BF16)
            span = pl.ds(step * SPAN, SPAN)
            outs.append(
                pltpu.make_async_copy(
                    grads.at[at, span], grad_out.at[at, span], grad_sems.at[at * steps + step]
                )
            )
            outs[-1].start()
    for at in (1, 0):
        states = [jnp.zeros((STATE, HDIM), F32)] * heads
        for step in range(steps):
            span = slice(step * SPAN, (step + 1) * SPAN)
            turned = turned_ref[at, :, span].astype(F32)
            lines = lines_ref[at * steps + step]
            for h in range(heads):
                line = jnp.concatenate(
                    [lines[8 * j + h : 8 * j + h + 1] for j in range(CHUNK)], axis=1
                )
                decayed = (turned * line).astype(BF16)
                states[h] = states[h] + dot(decayed, grads[at, span, head(h)], 1, 0)
        scatter_pieces(send, 1 - at, states)
    wait_all(outs)


def back_chunk(heads, rows, packed, grad_of, b_ref, c_ref, state):
    current = state[...]
    for j in reversed(range(CHUNK)):
        b, c = b_ref[0, 0, block(j)], c_ref[0, 0, block(j)]
        grad = grad_of(j)
        within = weighted_back(heads, j, rows, packed, grad, b, c)
        carried = dot(b, current.astype(BF16), 1, 0) * spread(packed, TO_BLOCK, j, heads)
        yield j, (within + carried).astype(BF16)
        decayed = (grad.astype(F32) * spread(packed, FROM_BLOCK, j, heads)).astype(BF16)
        factor = spread(packed[BLOCK - 1 :], FROM_BLOCK, j, heads)
        current = current * factor + dot(c, decayed, 0, 0)
    state[...] = current


def back0_body(heads, steps, features, rows_ref, gain_ref, total_ref, gate_ref, b_ref, c_ref,
               out_grad_ref, gated_ref, partial_ref, state_grad_ref, state, packs, norms):
    step = steps - 1 - pl.program_id(0)

    @pl.when(step == steps - 1)
    def _():
        pack(rows_ref, packs)
        total = jnp.sum(total_ref[...], axis=0)
        for part in range(steps):
            norms[part] = norm_rows(total, part, 0, features).T
        state[...] = jnp.zeros_like(state)

    norm = norms[step]

    def grad_of(j):
        return ssm_gradient(
            j,
            norm,
            gain_ref[...],
            gate_ref[0, 0, block(j)],
            out_grad_ref[0, 0, block(j)],
            gated_ref[0, block(j)],
        )

    for j, part in back_chunk(heads, rows_ref[step], packs[step], grad_of, b_ref, c_ref, state):
        partial_ref[0, 0, block(j)] = part

    @pl.when(step == 0)
    def _():
        for h in range(heads):
            state_grad_ref[0, 0, h] = state[:, head(h)].T


def back_body(heads, steps, rows_ref, grad_ref, b_ref, c_ref, b_hbm, rows_hbm, given_in,
              given_state, partial_ref, state_grad_ref, near_ref, near_state_ref, b_out, rows_out,
              state, packs, sems):
    level, step = 2 - pl.program_id(0), steps - 1 - pl.program_id(1)
    copies = [
        pltpu.make_async_copy(b_hbm.at[1, 0, pl.ds(0, SPAN)], b_out, sems.at[0]),
        pltpu.make_async_copy(rows_hbm.at[pl.ds(0, 2 * steps)], rows_out, sems.at[1]),
    ]

    @pl.when((level == 2) & (step == steps - 1))
    def _():
        start_all(copies)

    @pl.when(step == steps - 1)
    def _():
        pack(rows_ref, packs)
        state[...] = jnp.zeros_like(state)

    def grad_of(j):
        return grad_ref[0, block(j)]

    for j, part in back_chunk(heads, rows_ref[step], packs[step], grad_of, b_ref, c_ref, state):
        partial_ref[0, 0, block(j)] = part

    @pl.when(step == 0)
    def _():
        for h in range(heads):
            state_grad_ref[0, 0, h] = state[:, head(h)].T

    @pl.when((level == 1) & (step == 0))
    def _():
        near_ref[...] = partial_ref[0, 0]
        near_state_ref[...] = state_grad_ref[0, 0]
        wait_all(copies)


def inputs_body(heads, steps, b_hbm, partial_hbm, local_hbm, b_ref, partial_ref, local_ref,
                rows_ref, end_ref, input_grad_out, state_grad_out, b, partial, grads, states, sems,
                local_sem, out_sems, state_sems):
    chunks = [(level, step) for level in (1, 0) for step in range(steps)]
    pieces = [(level, step * CHUNK, CHUNK) for level, step in chunks[1:]]
    copies = piece_copies(
        [lambda at, span: b_hbm.at[at, 0, span], lambda at, span: partial_hbm.at[at, 0, span]],
        [b, partial],
        sems,
        pieces,
    )
    local_copy = pltpu.make_async_copy(local_hbm.at[0, 0], states.at[0], local_sem)
    start_all(copies[0])
    local_copy.start()
    for some in copies[1:]:
        start_all(some)
    outs = []
    for i, (level, step) in enumerate(chunks):
        if step == 0:
            ends = [gather_pieces(end_ref, 1 - level, h, heads) for h in range(heads)]
            rounded = jnp.concatenate(ends, axis=1).astype(BF16)
            level_rows = rows_ref.at[pl.ds(level * steps, steps)]
            decays = level_decays(level_rows, True)
            total = level_decays(level_rows, False)[-1][8 * (CHUNK - 1) :, BLOCK - 1 :]
            if level == 0:
                local_copy.wait()
            for h in range(heads):
                local = local_ref[h] if level == 1 else states[0, h]
                states[level, h] = local + (ends[h] * total[h : h + 1]).T
            outs.append(
                pltpu.make_async_copy(
                    states.at[level], state_grad_out.at[level, 0], state_sems.at[level]
                )
            )
            outs[-1].start()
        span = slice(step * SPAN, (step + 1) * SPAN)
        if i == 0:
            some_b, some_partial = b_ref, partial_ref
        else:
            wait_all(copies[i - 1])
            some_b, some_partial = b.at[level, span], partial.at[level, span]
        piece = dot(some_b[...], rounded, 1, 0)
        for j in range(CHUNK):
            line = decays[step][8 * j : 8 * j + 8]
            extra = piece[block(j)] * spread_rows(line, heads * HDIM)
            grads[level, block(step * CHUNK + j)] = (
                some_partial[block(j)].astype(F32) + extra
            ).astype(BF16)
        span = pl.ds(step * SPAN, SPAN)
        outs.append(
            pltpu.make_async_copy(
                grads.at[level, span], input_grad_out.at[level, 0, span], out_sems.at[i]
            )
        )
        outs[-1].start()
    wait_all(outs)


def shards(features, head_devices, ssm_input, gate_input, b_input, c_output, log_decay,
           root_state, norm_gain, out_grad, parent_ids):
    levels, _, length, columns = ssm_input.shape
    heads = columns // HDIM
    blocks = length // BLOCK
    steps = blocks // CHUNK
    segments = parent_ids.shape[1]
    rows = STATE // segments
    gain = norm_gain.reshape(1, columns)
    decay = jnp.transpose(log_decay, (0, 2, 1, 3))

    smem = pl.BlockSpec(memory_space=pltpu.SMEM)
    vmem = pl.BlockSpec(memory_space=pltpu.VMEM)
    anywhere = pl.BlockSpec(memory_space=pl.ANY)
    rows_shape = (levels * steps, WIDTH, BLOCK)
    pair_shape = (segments, 2 * heads * rows, HDIM)
    first_shape = (segments, 2 * heads * rows + 8, HDIM)
    sums_shape = (head_devices, 8, levels * FOLD)
    state_shape = (levels, 1, heads, HDIM, STATE)
    state_scratch = pltpu.VMEM((STATE, columns), F32)
    packs_scratch = pltpu.VMEM((steps, BLOCK, 128), F32)
    dma = pltpu.SemaphoreType.DMA

    far = lambda array: pin(array, pltpu.HBM)
    near = lambda array: pin(array, pltpu.VMEM)
    x, gate, out_grad = far(ssm_input), far(gate_input), far(out_grad)
    decay = far(decay)
    b, c, root = far(b_input), far(c_output), far(root_state)

    def pair_of_levels(width):
        return pltpu.VMEM((2, length, width), BF16)

    def tokens(width, place):
        return pl.BlockSpec((1, 1, SPAN, width), lambda *g: (place(*g)[0], 0, place(*g)[1], 0))

    def flat(width, place):
        return pl.BlockSpec((1, SPAN, width), lambda *g: (*place(*g), 0))

    def level_rows(place):
        return pl.BlockSpec((steps,) + rows_shape[1:], lambda *g: (place(*g)[0], 0, 0))

    def state_grads(place):
        return pl.BlockSpec((1, 1, heads, HDIM, STATE), lambda *g: (place(*g)[0], 0, 0, 0, 0))

    exchange = functools.partial(
        lax.all_to_all, axis_name="seg", split_axis=0, concat_axis=0, tiled=True
    )

    send, cum_rows = call(
        functools.partial(states_body, heads, steps),
        "states",
        6,
        in_specs=[anywhere] * 4,
        out_specs=[vmem, anywhere],
        out_shape=[pltpu.VMEM(first_shape, F32), pltpu.HBM(rows_shape, F32)],
        scratch_shapes=[
            pltpu.VMEM((levels * blocks * 8, BLOCK), F32),
            pltpu.VMEM(rows_shape, F32),
            pltpu.VMEM(decay.shape, F32),
            pltpu.VMEM(root_state.shape[1:], F32),
            pair_of_levels(columns),
            pair_of_levels(STATE),
            dma,
            dma,
            dma((4, 2)),
            dma,
        ],
    )(decay, root, x, b)
    got = exchange(send)

    own = lambda k: (0, k)
    gated0, sums0 = call(
        functools.partial(forward0_body, heads, steps),
        "forward0",
        6,
        grid=(steps,),
        in_specs=[
            level_rows(own),
            whole(root_state),
            whole(gain),
            tokens(columns, own),
            tokens(columns, own),
            tokens(STATE, own),
            tokens(STATE, own),
            tokens(columns, own),
        ],
        out_specs=[flat(columns, own), pl.BlockSpec((8, FOLD), lambda _: (0, 0))],
        out_shape=[pltpu.HBM((1, length, columns), BF16), pltpu.HBM((8, FOLD), F32)],
        scratch_shapes=[state_scratch, packs_scratch],
    )(far(cum_rows), root, gain, x, gate, b, c, out_grad)

    got, sums0 = lax.optimization_barrier((got, sums0))
    picked, decays = call(
        functools.partial(pick_body, heads),
        "pick",
        1,
        in_specs=[smem, vmem],
        out_specs=[vmem, vmem],
        out_shape=[pltpu.VMEM(pair_shape, F32), pltpu.VMEM((segments, 8, HDIM), F32)],
    )(parent_ids, near(got))

    picked, late_rows = lax.optimization_barrier((picked, cum_rows))
    starts = exchange(picked)
    both = lambda l, k: (l, k)
    later = lambda l, k: (l + 1, k)
    local, turned, *first = call(
        functools.partial(local_body, heads, steps),
        "local",
        7,
        grid=(2, steps),
        in_specs=[
            level_rows(later),
            tokens(columns, later),
            tokens(STATE, later),
            tokens(STATE, later),
        ]
        + [anywhere] * 4,
        out_specs=[
            flat(columns, both),
            pl.BlockSpec((1, STATE, SPAN), lambda l, k: (l, 0, k)),
            pl.BlockSpec((FIRST, columns), lambda l, k: (0, 0)),
        ]
        + [anywhere] * 4,
        out_shape=[
            pltpu.HBM((2, length, columns), BF16),
            pltpu.HBM((2, STATE, length), BF16),
            pltpu.VMEM((FIRST, columns), BF16),
            pltpu.VMEM((FIRST, columns), BF16),
            pltpu.VMEM((FIRST, STATE), BF16),
            pltpu.VMEM((FIRST, columns), BF16),
            pltpu.VMEM((2 * steps,) + rows_shape[1:], F32),
        ],
        scratch_shapes=[state_scratch, packs_scratch, dma((4,))],
    )(far(late_rows), x, b, c, gate, c, out_grad, far(late_rows))

    scaled_act, gated_act, turned, lines, sums = call(
        functools.partial(readout_body, heads, steps),
        "readout",
        5,
        in_specs=[anywhere] * 5 + [vmem] * 8,
        out_specs=[vmem] * 5,
        out_shape=[
            pltpu.VMEM((2, length, columns), F32),
            pltpu.VMEM((2, length, columns), F32),
            pltpu.VMEM((2, STATE, length), BF16),
            pltpu.VMEM((2 * steps,) + rows_shape[1:], F32),
            pltpu.VMEM(sums_shape, F32),
        ],
        scratch_shapes=[
            pair_of_levels(columns),
            pair_of_levels(columns),
            pair_of_levels(columns),
            pair_of_levels(STATE),
            dma((2 * steps, 4)),
            dma,
        ],
    )(
        far(local),
        gate,
        c,
        out_grad,
        far(turned),
        near(first[0]),
        near(first[1]),
        near(first[2]),
        near(first[3]),
        near(first[4]),
        near(starts),
        gain,
        sums0,
    )
    totals = lax.all_to_all(sums, "head", split_axis=0, concat_axis=0, tiled=True)

    grads, send_back = call(
        functools.partial(grads_body, heads, steps, features),
        "grads",
        4,
        in_specs=[vmem] * 5,
        out_specs=[anywhere, vmem],
        out_shape=[pltpu.HBM((2, length, columns), BF16), pltpu.VMEM(pair_shape, F32)],
        scratch_shapes=[pair_of_levels(columns), dma((2 * steps,))],
    )(near(lines), near(turned), near(scaled_act), near(gated_act), near(totals))
    got_back = exchange(send_back)

    own_back = lambda k: (0, steps - 1 - k)
    given = call(
        functools.partial(back0_body, heads, steps, features),
        "back0",
        6,
        grid=(steps,),
        in_specs=[
            level_rows(own_back),
            whole(gain),
            pl.BlockSpec(sums_shape, lambda _: (0, 0, 0)),
            tokens(columns, own_back),
            tokens(STATE, own_back),
            tokens(STATE, own_back),
            tokens(columns, own_back),
            flat(columns, own_back),
        ],
        out_specs=[tokens(columns, own_back), state_grads(own_back)],
        out_shape=[pltpu.HBM(ssm_input.shape, BF16), pltpu.HBM(state_shape, F32)],
        scratch_shapes=[state_scratch, packs_scratch, pltpu.VMEM((steps, SPAN, 8), F32)],
    )(far(cum_rows), gain, totals, gate, b, c, out_grad, far(gated0))

    got_back, *given = lax.optimization_barrier((got_back, *given))
    folded = call(
        functools.partial(fold_body, heads),
        "fold",
        1,
        in_specs=[smem, vmem, vmem],
        out_specs=vmem,
        out_shape=pltpu.VMEM(pair_shape, F32),
    )(parent_ids, near(decays), near(got_back))

    folded, late_rows = lax.optimization_barrier((folded, cum_rows))
    ends = exchange(folded)
    down_back = lambda l, k: (2 - l, steps - 1 - k)
    both_down_back = lambda l, k: (1 - l, steps - 1 - k)
    *given, near_partial, near_state, near_b, near_rows = call(
        functools.partial(back_body, heads, steps),
        "back",
        8,
        grid=(2, steps),
        in_specs=[
            level_rows(down_back),
            flat(columns, both_down_back),
            tokens(STATE, down_back),
            tokens(STATE, down_back),
        ]
        + [anywhere] * 4,
        out_specs=[
            tokens(columns, down_back),
            state_grads(down_back),
            pl.BlockSpec((SPAN, columns), lambda *g: (0, 0)),
            pl.BlockSpec((heads, HDIM, STATE), lambda *g: (0, 0, 0)),
            anywhere,
            anywhere,
        ],
        out_shape=[
            pltpu.HBM(ssm_input.shape, BF16),
            pltpu.HBM(state_shape, F32),
            pltpu.VMEM((SPAN, columns), BF16),
            pltpu.VMEM(state_shape[2:], F32),
            pltpu.VMEM((SPAN, STATE), BF16),
            pltpu.VMEM((2 * steps,) + rows_shape[1:], F32),
        ],
        input_output_aliases={6: 0, 7: 1},
        scratch_shapes=[state_scratch, packs_scratch, dma((2,))],
    )(far(late_rows), far(grads), b, c, b, far(late_rows), *given)

    return call(
        functools.partial(inputs_body, heads, steps),
        "inputs",
        4,
        in_specs=[anywhere] * 3 + [vmem] * 5,
        out_specs=[anywhere, anywhere],
        out_shape=[pltpu.HBM(ssm_input.shape, BF16), pltpu.HBM(state_shape, F32)],
        input_output_aliases={1: 0, 2: 1},
        scratch_shapes=[
            pair_of_levels(STATE),
            pair_of_levels(columns),
            pair_of_levels(columns),
            pltpu.VMEM((2,) + state_shape[2:], F32),
            dma((2 * steps - 1, 2)),
            dma,
            dma((2 * steps,)),
            dma((2,)),
        ],
    )(b, *given, near(near_b), near(near_partial), near(near_state), near(near_rows), near(ends))


def solution(mesh):
    in_specs = (
        P(None, "seg", None, "head"),
        P(None, "seg", None, "head"),
        P(None, "seg", None, None),
        P(None, "seg", None, None),
        P(None, "seg", "head", None),
        P("seg", "head", None, None),
        P("head"),
        P(None, "seg", None, "head"),
        P(),
    )
    out_specs = (P(None, "seg", None, "head"), P(None, "seg", "head", None, None))

    def run(*arrays):
        body = functools.partial(shards, arrays[0].shape[3], mesh.shape["head"])
        return tuple(
            jax.shard_map(
                body, mesh=mesh, in_specs=in_specs, out_specs=out_specs, check_vma=False
            )(*arrays)
        )

    return run
```

```python
import functools
import math

import jax
import jax.numpy as jnp
from jax import lax
from jax.experimental import pallas as pl
from jax.experimental.pallas import tpu as pltpu
from jax.sharding import PartitionSpec as P

BLOCK = 256
HALF = BLOCK // 2
HEADS = 24
HDIM = 128
STATE = 256
CHUNK = 3
SPAN = CHUNK * BLOCK
FIRST = 2 * BLOCK
FOLD = SPAN // 2
EPSILON = 1e-05
VMEM_LIMIT = 24 * 1024 * 1024
LOG2E = math.log2(math.e)

WIDTH = 8 * CHUNK
CUM = 0
FROM_BLOCK = WIDTH
TO_BLOCK = 2 * WIDTH

F32 = jnp.float32
BF16 = jnp.bfloat16
shaped = jax.ShapeDtypeStruct
pin = pltpu.with_memory_space_constraint


def call(body, name, micros, **kwargs):
    return pl.pallas_call(
        body,
        name=name,
        compiler_params=pltpu.CompilerParams(vmem_limit_bytes=VMEM_LIMIT),
        cost_estimate=pl.CostEstimate(
            flops=int(micros * 1e9), bytes_accessed=int(micros * 3e6), transcendentals=0
        ),
        **kwargs,
    )


def whole(array):
    rank = len(array.shape)
    return pl.BlockSpec(array.shape, lambda *_: (0,) * rank)


def dot(left, right, left_dim, right_dim, precision=None):
    return lax.dot_general(
        left,
        right,
        (((left_dim,), (right_dim,)), ((), ())),
        precision=precision,
        preferred_element_type=F32,
    )


def spread(packed, group, j, heads):
    at = group + 8 * j
    return jnp.concatenate(
        [
            jnp.broadcast_to(packed[:, at + h : at + h + 1], (packed.shape[0], HDIM))
            for h in range(heads)
        ],
        axis=1,
    )


def spread_rows(lines, width):
    high = lines.astype(BF16)
    low = (lines - high.astype(F32)).astype(BF16)
    row = lax.broadcasted_iota(jnp.int32, (16, width), 0)
    lane = lax.broadcasted_iota(jnp.int32, (16, width), 1)
    chosen = jnp.where((row & 7) == (lane >> 7), 1.0, 0.0).astype(BF16)
    return dot(jnp.concatenate([high, low], axis=0), chosen, 0, 0)


def block(j):
    return slice(j * BLOCK, (j + 1) * BLOCK)


def head(h):
    return slice(h * HDIM, (h + 1) * HDIM)


def turn(values):
    size = values.shape[0]
    unit = lax.broadcasted_iota(jnp.int32, (size, size), 0) == lax.broadcasted_iota(
        jnp.int32, (size, size), 1
    )
    return dot(jnp.where(unit, 1.0, 0.0).astype(BF16), values, 1, 1)


def silu(values):
    half = 0.5 * values
    return half + half * jnp.tanh(half)


def scatter_pieces(send, number, states):
    rows = STATE // send.shape[0]
    for piece in range(send.shape[0]):
        for h, state in enumerate(states):
            at = (number * len(states) + h) * rows
            send[piece, at : at + rows] = state[piece * rows : (piece + 1) * rows]


def gather_pieces(got, number, h, heads):
    rows = STATE // got.shape[0]
    at = (number * heads + h) * rows
    return got[:, at : at + rows].reshape(STATE, HDIM)


def start_all(copies):
    for copy in copies:
        copy.start()


def wait_all(copies):
    for copy in copies:
        copy.wait()


def piece_copies(sources, targets, sems, pieces):
    result = []
    for i, (at, first, count) in enumerate(pieces):
        rows = pl.ds(first * BLOCK, count * BLOCK)
        result.append(
            [
                pltpu.make_async_copy(source(at, rows), target.at[at, rows], sems.at[i, a])
                for a, (source, target) in enumerate(zip(sources, targets))
            ]
        )
    return result


def block_ends(parts):
    lasts = [part[:, BLOCK - 1 :] for part in parts]
    before = [jnp.zeros((8, 1), F32)]
    for last in lasts[:-1]:
        before.append(before[-1] + last)
    after = [jnp.zeros((8, 1), F32)]
    for last in lasts[:0:-1]:
        after.insert(0, after[0] + last)
    return lasts, before, after


def states_body(heads, steps, decay_hbm, root_hbm, x_hbm, b_hbm, send, rows_out, rates, rows, decay,
                root, x, b, decay_sem, root_sem, sems, out_sem):
    blocks = steps * CHUNK
    decay_copy = pltpu.make_async_copy(decay_hbm, decay, decay_sem)
    decay_copy.start()
    pieces = [(0, 0, CHUNK), (0, CHUNK, CHUNK), (1, 0, CHUNK), (1, CHUNK, CHUNK)]
    copies = piece_copies(
        [lambda at, span: x_hbm.at[at, 0, span], lambda at, span: b_hbm.at[at, 0, span]],
        [x, b],
        sems,
        pieces,
    )
    root_copy = pltpu.make_async_copy(root_hbm.at[0], root, root_sem)
    start_all(copies[0])
    root_copy.start()

    rates[...] = jnp.zeros_like(rates)
    upper = (
        lax.broadcasted_iota(jnp.int32, (BLOCK, BLOCK), 0)
        <= lax.broadcasted_iota(jnp.int32, (BLOCK, BLOCK), 1)
    )
    upper = jnp.where(upper, 1.0, 0.0).astype(BF16)
    decay_copy.wait()
    start_all(copies[1])
    for level in range(decay.shape[0]):
        for number in range(blocks):
            for h in range(heads):
                row = 8 * (level * blocks + number) + h
                rates[row : row + 1] = decay[level, h, :, block(number)]
    rest = rates[...]
    sums = jnp.zeros_like(rest)
    for _ in range(3):
        part = rest.astype(BF16)
        rest = rest - part.astype(F32)
        sums = sums + dot(part, upper, 1, 0)
    sums = sums * -LOG2E
    for chunk in range(rows.shape[0]):
        rows[chunk] = sums[WIDTH * chunk : WIDTH * (chunk + 1)]
    rows_copy = pltpu.make_async_copy(rows, rows_out, out_sem)
    rows_copy.start()

    to_level = []
    totals = []
    for level in range(2):
        numbers = range(level * blocks, (level + 1) * blocks)
        parts = [sums[8 * number : 8 * number + 8] for number in numbers]
        lasts, _, after = block_ends(parts)
        for part, last, suffix in zip(parts, lasts, after):
            to_level.append(jnp.exp2(last - part + suffix))
        totals.append(jnp.exp2(after[0] + lasts[0]))

    root_copy.wait()
    states = [(root[h] * totals[0][h : h + 1]).T for h in range(heads)]
    for i, (level, first, count) in enumerate(pieces):
        if (level, first) == (1, 0):
            scatter_pieces(send, 0, states)
            states = [jnp.zeros((STATE, HDIM), F32)] * heads
        wait_all(copies[i])
        if i > 0:
            start_all(sum(copies[i + 1 : i + 2], []))
        numbers = range(first, first + count)
        turned = [turn(b[level, block(number)]) for number in numbers]
        span = slice(first * BLOCK, (first + count) * BLOCK)
        for h in range(heads):
            decayed = [
                (values * to_level[level * blocks + number][h : h + 1]).astype(BF16)
                for number, values in zip(numbers, turned)
            ]
            states[h] = states[h] + dot(
                jnp.concatenate(decayed, axis=1), x[level, span, head(h)], 1, 0
            )
    scatter_pieces(send, 1, states)
    decays = jnp.broadcast_to(totals[1], (8, HDIM))
    for piece in range(send.shape[0]):
        send[piece, send.shape[1] - 8 :] = decays
    rows_copy.wait()


def level_decays(rows, to_end):
    steps = rows.shape[0]
    parts = [rows[step, 8 * j : 8 * j + 8] for step in range(steps) for j in range(CHUNK)]
    lasts, before, after = block_ends(parts)
    if to_end:
        lines = [last - part + end for part, last, end in zip(parts, lasts, after)]
    else:
        lines = [start + part for part, start in zip(parts, before)]
    return [
        jnp.exp2(jnp.concatenate(lines[step * CHUNK : (step + 1) * CHUNK], axis=0))
        for step in range(steps)
    ]


def pack(rows, packed):
    for step in range(packed.shape[0]):
        part = rows[step]
        last = jnp.concatenate(
            [
                jnp.broadcast_to(part[8 * j : 8 * j + 8, BLOCK - 1 :], (8, BLOCK))
                for j in range(CHUNK)
            ],
            axis=0,
        )
        packed[step] = jnp.concatenate(
            [
                part,
                jnp.exp2(part),
                jnp.exp2(last - part),
                jnp.zeros((128 - 3 * WIDTH, BLOCK), F32),
            ],
            axis=0,
        ).T


def pick_body(heads, parent_ref, got_ref, send, decay_out):
    segments = got_ref.shape[0]
    rows = STATE // segments
    pair = send.shape[1]
    half = pair // 2
    for seg in range(segments):
        first = parent_ref[0, seg]
        second = parent_ref[1, seg]
        root = parent_ref[0, second]
        send[seg, :half] = got_ref[first, :half]
        decay = got_ref[second, pair : pair + 8]
        decay_out[seg] = got_ref[seg, pair : pair + 8]
        for h in range(heads):
            a = slice(h * rows, (h + 1) * rows)
            b = slice(half + h * rows, half + (h + 1) * rows)
            send[seg, b] = decay[h : h + 1] * got_ref[root, a] + got_ref[second, b]


def fold_body(heads, parent_ref, decay_ref, got_ref, send):
    rows = STATE // got_ref.shape[0]
    half = send.shape[1] // 2
    send[...] = jnp.zeros_like(send)
    for seg in range(got_ref.shape[0]):
        second = parent_ref[1, seg]
        send[second, :half] += got_ref[seg, :half]
    for seg in range(got_ref.shape[0]):
        first = parent_ref[0, seg]
        decay = decay_ref[seg]
        for h in range(heads):
            a = slice(h * rows, (h + 1) * rows)
            b = slice(half + h * rows, half + (h + 1) * rows)
            send[first, b] += decay[h : h + 1] * send[seg, a] + got_ref[seg, b]


def causal_mask(transposed):
    first = lax.broadcasted_iota(jnp.int32, (HALF, HALF), 0)
    second = lax.broadcasted_iota(jnp.int32, (HALF, HALF), 1)
    return first <= second if transposed else first >= second


def weighted(heads, j, rows, packed, x, b, c):
    scores = dot(c, b, 1, 1)
    causal = causal_mask(False)
    results = []
    for h in range(heads):
        row = rows[8 * j + h : 8 * j + h + 1]
        col = packed[:, CUM + 8 * j + h : CUM + 8 * j + h + 1]
        first = jnp.where(causal, col[:HALF] - row[:, :HALF], -jnp.inf)
        last = jnp.where(causal, col[HALF:] - row[:, HALF:], -jnp.inf)
        across = col[HALF:] - row[:, :HALF]
        top = jnp.concatenate(
            [(scores[:HALF, :HALF] * jnp.exp2(first)).astype(BF16), jnp.zeros((HALF, HALF), BF16)],
            axis=1,
        )
        bottom = jnp.concatenate(
            [
                (scores[HALF:, :HALF] * jnp.exp2(across)).astype(BF16),
                (scores[HALF:, HALF:] * jnp.exp2(last)).astype(BF16),
            ],
            axis=1,
        )
        results.append(dot(jnp.concatenate([top, bottom], axis=0), x[:, head(h)], 1, 0))
    return jnp.concatenate(results, axis=1)


def weighted_back(heads, j, rows, packed, grad, b, c):
    scores = dot(b, c, 1, 1)
    causal = causal_mask(True)
    results = []
    for h in range(heads):
        row = rows[8 * j + h : 8 * j + h + 1]
        col = packed[:, CUM + 8 * j + h : CUM + 8 * j + h + 1]
        first = jnp.where(causal, row[:, :HALF] - col[:HALF], -jnp.inf)
        last = jnp.where(causal, row[:, HALF:] - col[HALF:], -jnp.inf)
        across = row[:, HALF:] - col[:HALF]
        top = jnp.concatenate(
            [
                (scores[:HALF, :HALF] * jnp.exp2(first)).astype(BF16),
                (scores[:HALF, HALF:] * jnp.exp2(across)).astype(BF16),
            ],
            axis=1,
        )
        bottom = jnp.concatenate(
            [jnp.zeros((HALF, HALF), BF16), (scores[HALF:, HALF:] * jnp.exp2(last)).astype(BF16)],
            axis=1,
        )
        results.append(dot(jnp.concatenate([top, bottom], axis=0), grad[:, head(h)], 1, 0))
    return jnp.concatenate(results, axis=1)


def gated_sums(ssm_out, gate, out_grad, gain):
    act = silu(gate.astype(F32))
    gated = ssm_out * act
    scaled = out_grad.astype(F32) * gain
    ones = jnp.ones((8, gated.shape[1]), BF16)
    squares = dot(ones, (gated * gated).astype(BF16), 1, 1)
    products = dot(ones, (scaled * gated).astype(BF16), 1, 1)
    return gated, scaled * act, gated * act, (squares[:1], products[:1])


def store_sums(sums, step, at, pairs):
    for q in range(2):
        line = jnp.concatenate([pair[q] for pair in pairs], axis=1)
        for half in range(2):
            sums[4 * step + 2 * q + half : 4 * step + 2 * q + half + 1, at : at + FOLD] = line[
                :, half * FOLD : (half + 1) * FOLD
            ]


def norm_rows(total, step, at, features):
    lines = [total[4 * step + i : 4 * step + i + 1, at : at + FOLD] for i in range(4)]
    squares = jnp.concatenate(lines[:2], axis=1) / features
    dots = jnp.concatenate(lines[2:], axis=1) / features
    inv_rms = lax.rsqrt(squares + EPSILON)
    back = inv_rms * inv_rms * inv_rms * dots
    return jnp.concatenate([inv_rms, back, jnp.zeros((6, SPAN), F32)], axis=0)


def ssm_gradient(j, norm, gain, gate, out_grad, gated):
    inv_rms, back = norm[block(j), 0:1], norm[block(j), 1:2]
    grad = inv_rms * (out_grad.astype(F32) * gain) - gated.astype(F32) * back
    return (grad * silu(gate.astype(F32))).astype(BF16)


def forward0_body(heads, steps, rows_ref, root_ref, gain_ref, x_ref, gate_ref, b_ref, c_ref,
                  out_grad_ref, gated_ref, sums_ref, state, packs):
    step = pl.program_id(0)

    @pl.when(step == 0)
    def _():
        pack(rows_ref, packs)
        for h in range(heads):
            state[:, head(h)] = root_ref[0, h].T

    rows, packed = rows_ref[step], packs[step]
    current = state[...]
    pairs = []
    for j in range(CHUNK):
        x, b, c = x_ref[0, 0, block(j)], b_ref[0, 0, block(j)], c_ref[0, 0, block(j)]
        within = weighted(heads, j, rows, packed, x, b, c)
        carried = dot(c, current.astype(BF16), 1, 0) * spread(packed, FROM_BLOCK, j, heads)
        gated, _, _, pair = gated_sums(
            within + carried, gate_ref[0, 0, block(j)], out_grad_ref[0, 0, block(j)], gain_ref[...]
        )
        gated_ref[0, block(j)] = gated.astype(BF16)
        pairs.append(pair)
        decayed = (x.astype(F32) * spread(packed, TO_BLOCK, j, heads)).astype(BF16)
        factor = spread(packed[BLOCK - 1 :], FROM_BLOCK, j, heads)
        current = current * factor + dot(b, decayed, 0, 0)
    state[...] = current
    for part in range(steps):

        @pl.when(step == part)
        def _():
            store_sums(sums_ref, part, 0, pairs)


def local_body(heads, steps, rows_ref, x_ref, b_ref, c_ref, gate_hbm, c_hbm, out_grad_hbm,
               rows_hbm, out_ref, turned_ref, first_ref, gate_out, c_out, out_grad_out, rows_out,
               state, packs, sems):
    level, step = pl.program_id(0), pl.program_id(1)
    span = pl.ds(0, FIRST)
    copies = [
        pltpu.make_async_copy(source, target, sems.at[i])
        for i, (source, target) in enumerate(
            [
                (gate_hbm.at[1, 0, span], gate_out),
                (c_hbm.at[1, 0, span], c_out),
                (out_grad_hbm.at[1, 0, span], out_grad_out),
                (rows_hbm.at[pl.ds(steps, 2 * steps)], rows_out),
            ]
        )
    ]

    @pl.when((level == 0) & (step == 0))
    def _():
        start_all(copies)

    @pl.when(step == 0)
    def _():
        pack(rows_ref, packs)
        state[...] = jnp.zeros_like(state)

    rows, packed = rows_ref[step], packs[step]
    current = state[...]
    for j in range(CHUNK):
        x, b, c = x_ref[0, 0, block(j)], b_ref[0, 0, block(j)], c_ref[0, 0, block(j)]
        within = weighted(heads, j, rows, packed, x, b, c)
        carried = dot(c, current.astype(BF16), 1, 0) * spread(packed, FROM_BLOCK, j, heads)
        out_ref[0, block(j)] = (within + carried).astype(BF16)
        turned_ref[0, :, block(j)] = turn(c).astype(BF16)
        decayed = (x.astype(F32) * spread(packed, TO_BLOCK, j, heads)).astype(BF16)
        factor = spread(packed[BLOCK - 1 :], FROM_BLOCK, j, heads)
        current = current * factor + dot(b, decayed, 0, 0)
    state[...] = current

    @pl.when((level == 0) & (step == 0))
    def _():
        first_ref[...] = out_ref[0, :FIRST]

    @pl.when((level == 1) & (step == steps - 1))
    def _():
        wait_all(copies)


def readout_body(heads, steps, local_hbm, gate_hbm, c_hbm, out_grad_hbm, turned_hbm, local_ref,
                 gate_ref, c_ref, out_grad_ref, rows_ref, start_ref, gain_ref, first_sums_ref,
                 scaled_act, gated_act, turned, lines, sums, local, gate, out_grad, c, sems,
                 turned_sem):
    early = FIRST // BLOCK
    pieces = [(0, early, CHUNK - early)]
    pieces += [(at, step * CHUNK, CHUNK) for at in range(2) for step in range(steps)][1:]
    copies = piece_copies(
        [
            lambda at, span: c_hbm.at[at + 1, 0, span],
            lambda at, span: local_hbm.at[at, span],
            lambda at, span: gate_hbm.at[at + 1, 0, span],
            lambda at, span: out_grad_hbm.at[at + 1, 0, span],
        ],
        [c, local, gate, out_grad],
        sems,
        pieces,
    )
    turned_copy = pltpu.make_async_copy(turned_hbm, turned, turned_sem)
    copies.append([turned_copy])
    start_all(copies[0] + copies[1])
    sums[0, :, :FOLD] = first_sums_ref[...]
    decays = []
    for at in range(2):
        decays += level_decays(rows_ref.at[pl.ds(at * steps, steps)], False)
    columns = []
    for chunk, line in enumerate(decays):
        lines[chunk] = line
        columns.append(line.T)
    pairs = []
    for i, (at, first, count) in enumerate([(0, 0, early)] + pieces):
        if first == 0:
            start = jnp.concatenate(
                [gather_pieces(start_ref, at, h, heads) for h in range(heads)], axis=1
            ).astype(BF16)
        if i == 0:
            refs = [c_ref, local_ref, gate_ref, out_grad_ref]
        else:
            wait_all(copies[i - 1])
            start_all(sum(copies[i + 1 : i + 2], []))
            span = slice(first * BLOCK, (first + count) * BLOCK)
            refs = [buffer.at[at, span] for buffer in (c, local, gate, out_grad)]
        piece = dot(refs[0][...], start, 1, 0)
        for number in range(first, first + count):
            step, j = number // CHUNK, number % CHUNK
            mine = block(number - first)
            carried = piece[mine] * spread(columns[at * steps + step], 0, j, heads)
            place = block(number)
            _, scaled_act[at, place], gated_act[at, place], pair = gated_sums(
                carried + refs[1][mine].astype(F32), refs[2][mine], refs[3][mine], gain_ref[...]
            )
            pairs.append(pair)
            if j == CHUNK - 1:
                store_sums(sums.at[0], step, (at + 1) * FOLD, pairs)
                pairs = []
    for copy in range(1, sums.shape[0]):
        sums[copy] = sums[0]
    turned_copy.wait()


def grads_body(heads, steps, features, lines_ref, turned_ref, scaled_act_ref, gated_act_ref,
               total_ref, grad_out, send, grads, grad_sems):
    total = jnp.sum(total_ref[...], axis=0)
    outs = []
    for at in (1, 0):
        for step in range(steps):
            norm = norm_rows(total, step, (at + 1) * FOLD, features)
            for j in range(CHUNK):
                place = block(step * CHUNK + j)
                factors = spread_rows(norm[:, block(j)], 2 * HDIM)
                inv_rms, back = factors[:, :HDIM], factors[:, HDIM:]
                for h in range(heads):
                    grad = inv_rms * scaled_act_ref[at, place, head(h)]
                    grad = grad - back * gated_act_ref[at, place, head(h)]
                    grads[at, place, head(h)] = grad.astype(BF16)
            span = pl.ds(step * SPAN, SPAN)
            outs.append(
                pltpu.make_async_copy(
                    grads.at[at, span], grad_out.at[at, span], grad_sems.at[at * steps + step]
                )
            )
            outs[-1].start()
    for at in (1, 0):
        states = [jnp.zeros((STATE, HDIM), F32)] * heads
        for step in range(steps):
            span = slice(step * SPAN, (step + 1) * SPAN)
            turned = turned_ref[at, :, span].astype(F32)
            lines = lines_ref[at * steps + step]
            for h in range(heads):
                line = jnp.concatenate(
                    [lines[8 * j + h : 8 * j + h + 1] for j in range(CHUNK)], axis=1
                )
                decayed = (turned * line).astype(BF16)
                states[h] = states[h] + dot(decayed, grads[at, span, head(h)], 1, 0)
        scatter_pieces(send, 1 - at, states)
    wait_all(outs)


def back_chunk(heads, rows, packed, grad_of, b_ref, c_ref, state):
    current = state[...]
    for j in reversed(range(CHUNK)):
        b, c = b_ref[0, 0, block(j)], c_ref[0, 0, block(j)]
        grad = grad_of(j)
        within = weighted_back(heads, j, rows, packed, grad, b, c)
        carried = dot(b, current.astype(BF16), 1, 0) * spread(packed, TO_BLOCK, j, heads)
        yield j, (within + carried).astype(BF16)
        decayed = (grad.astype(F32) * spread(packed, FROM_BLOCK, j, heads)).astype(BF16)
        factor = spread(packed[BLOCK - 1 :], FROM_BLOCK, j, heads)
        current = current * factor + dot(c, decayed, 0, 0)
    state[...] = current


def back0_body(heads, steps, features, rows_ref, gain_ref, total_ref, gate_ref, b_ref, c_ref,
               out_grad_ref, gated_ref, partial_ref, state_grad_ref, state, packs, norms):
    step = steps - 1 - pl.program_id(0)

    @pl.when(step == steps - 1)
    def _():
        pack(rows_ref, packs)
        total = jnp.sum(total_ref[...], axis=0)
        for part in range(steps):
            norms[part] = norm_rows(total, part, 0, features).T
        state[...] = jnp.zeros_like(state)

    norm = norms[step]

    def grad_of(j):
        return ssm_gradient(
            j,
            norm,
            gain_ref[...],
            gate_ref[0, 0, block(j)],
            out_grad_ref[0, 0, block(j)],
            gated_ref[0, block(j)],
        )

    for j, part in back_chunk(heads, rows_ref[step], packs[step], grad_of, b_ref, c_ref, state):
        partial_ref[0, 0, block(j)] = part

    @pl.when(step == 0)
    def _():
        for h in range(heads):
            state_grad_ref[0, 0, h] = state[:, head(h)].T


def back_body(heads, steps, rows_ref, grad_ref, b_ref, c_ref, b_hbm, rows_hbm, given_in,
              given_state, partial_ref, state_grad_ref, near_ref, near_state_ref, b_out, rows_out,
              state, packs, sems):
    level, step = 2 - pl.program_id(0), steps - 1 - pl.program_id(1)
    copies = [
        pltpu.make_async_copy(b_hbm.at[1, 0, pl.ds(0, SPAN)], b_out, sems.at[0]),
        pltpu.make_async_copy(rows_hbm.at[pl.ds(0, 2 * steps)], rows_out, sems.at[1]),
    ]

    @pl.when((level == 2) & (step == steps - 1))
    def _():
        start_all(copies)

    @pl.when(step == steps - 1)
    def _():
        pack(rows_ref, packs)
        state[...] = jnp.zeros_like(state)

    def grad_of(j):
        return grad_ref[0, block(j)]

    for j, part in back_chunk(heads, rows_ref[step], packs[step], grad_of, b_ref, c_ref, state):
        partial_ref[0, 0, block(j)] = part

    @pl.when(step == 0)
    def _():
        for h in range(heads):
            state_grad_ref[0, 0, h] = state[:, head(h)].T

    @pl.when((level == 1) & (step == 0))
    def _():
        near_ref[...] = partial_ref[0, 0]
        near_state_ref[...] = state_grad_ref[0, 0]
        wait_all(copies)


def inputs_body(heads, steps, b_hbm, partial_hbm, local_hbm, b_ref, partial_ref, local_ref,
                rows_ref, end_ref, input_grad_out, state_grad_out, b, partial, grads, states, sems,
                local_sem, out_sems, state_sems):
    chunks = [(level, step) for level in (1, 0) for step in range(steps)]
    pieces = [(level, step * CHUNK, CHUNK) for level, step in chunks[1:]]
    copies = piece_copies(
        [lambda at, span: b_hbm.at[at, 0, span], lambda at, span: partial_hbm.at[at, 0, span]],
        [b, partial],
        sems,
        pieces,
    )
    local_copy = pltpu.make_async_copy(local_hbm.at[0, 0], states.at[0], local_sem)
    start_all(copies[0])
    local_copy.start()
    for some in copies[1:]:
        start_all(some)
    outs = []
    for i, (level, step) in enumerate(chunks):
        if step == 0:
            ends = [gather_pieces(end_ref, 1 - level, h, heads) for h in range(heads)]
            rounded = jnp.concatenate(ends, axis=1).astype(BF16)
            level_rows = rows_ref.at[pl.ds(level * steps, steps)]
            decays = level_decays(level_rows, True)
            total = level_decays(level_rows, False)[-1][8 * (CHUNK - 1) :, BLOCK - 1 :]
            if level == 0:
                local_copy.wait()
            for h in range(heads):
                local = local_ref[h] if level == 1 else states[0, h]
                states[level, h] = local + (ends[h] * total[h : h + 1]).T
            outs.append(
                pltpu.make_async_copy(
                    states.at[level], state_grad_out.at[level, 0], state_sems.at[level]
                )
            )
            outs[-1].start()
        span = slice(step * SPAN, (step + 1) * SPAN)
        if i == 0:
            some_b, some_partial = b_ref, partial_ref
        else:
            wait_all(copies[i - 1])
            some_b, some_partial = b.at[level, span], partial.at[level, span]
        piece = dot(some_b[...], rounded, 1, 0)
        for j in range(CHUNK):
            line = decays[step][8 * j : 8 * j + 8]
            extra = piece[block(j)] * spread_rows(line, heads * HDIM)
            grads[level, block(step * CHUNK + j)] = (
                some_partial[block(j)].astype(F32) + extra
            ).astype(BF16)
        span = pl.ds(step * SPAN, SPAN)
        outs.append(
            pltpu.make_async_copy(
                grads.at[level, span], input_grad_out.at[level, 0, span], out_sems.at[i]
            )
        )
        outs[-1].start()
    wait_all(outs)


def shards(features, head_devices, ssm_input, gate_input, b_input, c_output, log_decay,
           root_state, norm_gain, out_grad, parent_ids):
    levels, _, length, columns = ssm_input.shape
    heads = columns // HDIM
    blocks = length // BLOCK
    steps = blocks // CHUNK
    segments = parent_ids.shape[1]
    rows = STATE // segments
    gain = norm_gain.reshape(1, columns)
    decay = jnp.transpose(log_decay, (0, 2, 1, 3))

    smem = pl.BlockSpec(memory_space=pltpu.SMEM)
    vmem = pl.BlockSpec(memory_space=pltpu.VMEM)
    anywhere = pl.BlockSpec(memory_space=pl.ANY)
    rows_shape = (levels * steps, WIDTH, BLOCK)
    pair_shape = (segments, 2 * heads * rows, HDIM)
    first_shape = (segments, 2 * heads * rows + 8, HDIM)
    sums_shape = (head_devices, 8, levels * FOLD)
    state_shape = (levels, 1, heads, HDIM, STATE)
    state_scratch = pltpu.VMEM((STATE, columns), F32)
    packs_scratch = pltpu.VMEM((steps, BLOCK, 128), F32)
    dma = pltpu.SemaphoreType.DMA

    far = lambda array: pin(array, pltpu.HBM)
    near = lambda array: pin(array, pltpu.VMEM)
    x, gate, out_grad = far(ssm_input), far(gate_input), far(out_grad)
    decay = far(decay)
    b, c, root = far(b_input), far(c_output), far(root_state)

    def pair_of_levels(width):
        return pltpu.VMEM((2, length, width), BF16)

    def tokens(width, place):
        return pl.BlockSpec((1, 1, SPAN, width), lambda *g: (place(*g)[0], 0, place(*g)[1], 0))

    def flat(width, place):
        return pl.BlockSpec((1, SPAN, width), lambda *g: (*place(*g), 0))

    def level_rows(place):
        return pl.BlockSpec((steps,) + rows_shape[1:], lambda *g: (place(*g)[0], 0, 0))

    def state_grads(place):
        return pl.BlockSpec((1, 1, heads, HDIM, STATE), lambda *g: (place(*g)[0], 0, 0, 0, 0))

    exchange = functools.partial(
        lax.all_to_all, axis_name="seg", split_axis=0, concat_axis=0, tiled=True
    )

    send, cum_rows = call(
        functools.partial(states_body, heads, steps),
        "states",
        6,
        in_specs=[anywhere] * 4,
        out_specs=[vmem, anywhere],
        out_shape=[pltpu.VMEM(first_shape, F32), pltpu.HBM(rows_shape, F32)],
        scratch_shapes=[
            pltpu.VMEM((levels * blocks * 8, BLOCK), F32),
            pltpu.VMEM(rows_shape, F32),
            pltpu.VMEM(decay.shape, F32),
            pltpu.VMEM(root_state.shape[1:], F32),
            pair_of_levels(columns),
            pair_of_levels(STATE),
            dma,
            dma,
            dma((4, 2)),
            dma,
        ],
    )(decay, root, x, b)
    got = exchange(send)

    own = lambda k: (0, k)
    gated0, sums0 = call(
        functools.partial(forward0_body, heads, steps),
        "forward0",
        6,
        grid=(steps,),
        in_specs=[
            level_rows(own),
            whole(root_state),
            whole(gain),
            tokens(columns, own),
            tokens(columns, own),
            tokens(STATE, own),
            tokens(STATE, own),
            tokens(columns, own),
        ],
        out_specs=[flat(columns, own), pl.BlockSpec((8, FOLD), lambda _: (0, 0))],
        out_shape=[pltpu.HBM((1, length, columns), BF16), pltpu.HBM((8, FOLD), F32)],
        scratch_shapes=[state_scratch, packs_scratch],
    )(far(cum_rows), root, gain, x, gate, b, c, out_grad)

    got, sums0 = lax.optimization_barrier((got, sums0))
    picked, decays = call(
        functools.partial(pick_body, heads),
        "pick",
        1,
        in_specs=[smem, vmem],
        out_specs=[vmem, vmem],
        out_shape=[pltpu.VMEM(pair_shape, F32), pltpu.VMEM((segments, 8, HDIM), F32)],
    )(parent_ids, near(got))

    picked, late_rows = lax.optimization_barrier((picked, cum_rows))
    starts = exchange(picked)
    both = lambda l, k: (l, k)
    later = lambda l, k: (l + 1, k)
    local, turned, *first = call(
        functools.partial(local_body, heads, steps),
        "local",
        7,
        grid=(2, steps),
        in_specs=[
            level_rows(later),
            tokens(columns, later),
            tokens(STATE, later),
            tokens(STATE, later),
        ]
        + [anywhere] * 4,
        out_specs=[
            flat(columns, both),
            pl.BlockSpec((1, STATE, SPAN), lambda l, k: (l, 0, k)),
            pl.BlockSpec((FIRST, columns), lambda l, k: (0, 0)),
        ]
        + [anywhere] * 4,
        out_shape=[
            pltpu.HBM((2, length, columns), BF16),
            pltpu.HBM((2, STATE, length), BF16),
            pltpu.VMEM((FIRST, columns), BF16),
            pltpu.VMEM((FIRST, columns), BF16),
            pltpu.VMEM((FIRST, STATE), BF16),
            pltpu.VMEM((FIRST, columns), BF16),
            pltpu.VMEM((2 * steps,) + rows_shape[1:], F32),
        ],
        scratch_shapes=[state_scratch, packs_scratch, dma((4,))],
    )(far(late_rows), x, b, c, gate, c, out_grad, far(late_rows))

    scaled_act, gated_act, turned, lines, sums = call(
        functools.partial(readout_body, heads, steps),
        "readout",
        5,
        in_specs=[anywhere] * 5 + [vmem] * 8,
        out_specs=[vmem] * 5,
        out_shape=[
            pltpu.VMEM((2, length, columns), F32),
            pltpu.VMEM((2, length, columns), F32),
            pltpu.VMEM((2, STATE, length), BF16),
            pltpu.VMEM((2 * steps,) + rows_shape[1:], F32),
            pltpu.VMEM(sums_shape, F32),
        ],
        scratch_shapes=[
            pair_of_levels(columns),
            pair_of_levels(columns),
            pair_of_levels(columns),
            pair_of_levels(STATE),
            dma((2 * steps, 4)),
            dma,
        ],
    )(
        far(local),
        gate,
        c,
        out_grad,
        far(turned),
        near(first[0]),
        near(first[1]),
        near(first[2]),
        near(first[3]),
        near(first[4]),
        near(starts),
        gain,
        sums0,
    )
    totals = lax.all_to_all(sums, "head", split_axis=0, concat_axis=0, tiled=True)

    grads, send_back = call(
        functools.partial(grads_body, heads, steps, features),
        "grads",
        4,
        in_specs=[vmem] * 5,
        out_specs=[anywhere, vmem],
        out_shape=[pltpu.HBM((2, length, columns), BF16), pltpu.VMEM(pair_shape, F32)],
        scratch_shapes=[pair_of_levels(columns), dma((2 * steps,))],
    )(near(lines), near(turned), near(scaled_act), near(gated_act), near(totals))
    got_back = exchange(send_back)

    own_back = lambda k: (0, steps - 1 - k)
    given = call(
        functools.partial(back0_body, heads, steps, features),
        "back0",
        6,
        grid=(steps,),
        in_specs=[
            level_rows(own_back),
            whole(gain),
            pl.BlockSpec(sums_shape, lambda _: (0, 0, 0)),
            tokens(columns, own_back),
            tokens(STATE, own_back),
            tokens(STATE, own_back),
            tokens(columns, own_back),
            flat(columns, own_back),
        ],
        out_specs=[tokens(columns, own_back), state_grads(own_back)],
        out_shape=[pltpu.HBM(ssm_input.shape, BF16), pltpu.HBM(state_shape, F32)],
        scratch_shapes=[state_scratch, packs_scratch, pltpu.VMEM((steps, SPAN, 8), F32)],
    )(far(cum_rows), gain, totals, gate, b, c, out_grad, far(gated0))

    got_back, *given = lax.optimization_barrier((got_back, *given))
    folded = call(
        functools.partial(fold_body, heads),
        "fold",
        1,
        in_specs=[smem, vmem, vmem],
        out_specs=vmem,
        out_shape=pltpu.VMEM(pair_shape, F32),
    )(parent_ids, near(decays), near(got_back))

    folded, late_rows = lax.optimization_barrier((folded, cum_rows))
    ends = exchange(folded)
    down_back = lambda l, k: (2 - l, steps - 1 - k)
    both_down_back = lambda l, k: (1 - l, steps - 1 - k)
    *given, near_partial, near_state, near_b, near_rows = call(
        functools.partial(back_body, heads, steps),
        "back",
        8,
        grid=(2, steps),
        in_specs=[
            level_rows(down_back),
            flat(columns, both_down_back),
            tokens(STATE, down_back),
            tokens(STATE, down_back),
        ]
        + [anywhere] * 4,
        out_specs=[
            tokens(columns, down_back),
            state_grads(down_back),
            pl.BlockSpec((SPAN, columns), lambda *g: (0, 0)),
            pl.BlockSpec((heads, HDIM, STATE), lambda *g: (0, 0, 0)),
            anywhere,
            anywhere,
        ],
        out_shape=[
            pltpu.HBM(ssm_input.shape, BF16),
            pltpu.HBM(state_shape, F32),
            pltpu.VMEM((SPAN, columns), BF16),
            pltpu.VMEM(state_shape[2:], F32),
            pltpu.VMEM((SPAN, STATE), BF16),
            pltpu.VMEM((2 * steps,) + rows_shape[1:], F32),
        ],
        input_output_aliases={6: 0, 7: 1},
        scratch_shapes=[state_scratch, packs_scratch, dma((2,))],
    )(far(late_rows), far(grads), b, c, b, far(late_rows), *given)

    return call(
        functools.partial(inputs_body, heads, steps),
        "inputs",
        4,
        in_specs=[anywhere] * 3 + [vmem] * 5,
        out_specs=[anywhere, anywhere],
        out_shape=[pltpu.HBM(ssm_input.shape, BF16), pltpu.HBM(state_shape, F32)],
        input_output_aliases={1: 0, 2: 1},
        scratch_shapes=[
            pair_of_levels(STATE),
            pair_of_levels(columns),
            pair_of_levels(columns),
            pltpu.VMEM((2,) + state_shape[2:], F32),
            dma((2 * steps - 1, 2)),
            dma,
            dma((2 * steps,)),
            dma((2,)),
        ],
    )(b, *given, near(near_b), near(near_partial), near(near_state), near(near_rows), near(ends))


def solution(mesh):
    in_specs = (
        P(None, "seg", None, "head"),
        P(None, "seg", None, "head"),
        P(None, "seg", None, None),
        P(None, "seg", None, None),
        P(None, "seg", "head", None),
        P("seg", "head", None, None),
        P("head"),
        P(None, "seg", None, "head"),
        P(),
    )
    out_specs = (P(None, "seg", None, "head"), P(None, "seg", "head", None, None))

    def run(*arrays):
        body = functools.partial(shards, arrays[0].shape[3], mesh.shape["head"])
        return tuple(
            jax.shard_map(
                body, mesh=mesh, in_specs=in_specs, out_specs=out_specs, check_vma=False
            )(*arrays)
        )

    return run
```

```python
import functools
import math

import jax
import jax.numpy as jnp
from jax import lax
from jax.experimental import pallas as pl
from jax.experimental.pallas import tpu as pltpu
from jax.sharding import PartitionSpec as P

BLOCK = 256
HALF = BLOCK // 2
HEADS = 24
HDIM = 128
STATE = 256
CHUNK = 3
SPAN = CHUNK * BLOCK
FIRST = 2 * BLOCK
FOLD = SPAN // 2
EPSILON = 1e-05
VMEM_LIMIT = 24 * 1024 * 1024
LOG2E = math.log2(math.e)

WIDTH = 8 * CHUNK
CUM = 0
FROM_BLOCK = WIDTH
TO_BLOCK = 2 * WIDTH

F32 = jnp.float32
BF16 = jnp.bfloat16
shaped = jax.ShapeDtypeStruct
pin = pltpu.with_memory_space_constraint


def call(body, name, micros, **kwargs):
    return pl.pallas_call(
        body,
        name=name,
        compiler_params=pltpu.CompilerParams(vmem_limit_bytes=VMEM_LIMIT),
        cost_estimate=pl.CostEstimate(
            flops=int(micros * 1e9), bytes_accessed=int(micros * 3e6), transcendentals=0
        ),
        **kwargs,
    )


def whole(array):
    rank = len(array.shape)
    return pl.BlockSpec(array.shape, lambda *_: (0,) * rank)


def dot(left, right, left_dim, right_dim, precision=None):
    return lax.dot_general(
        left,
        right,
        (((left_dim,), (right_dim,)), ((), ())),
        precision=precision,
        preferred_element_type=F32,
    )


def spread(packed, group, j, heads):
    at = group + 8 * j
    return jnp.concatenate(
        [
            jnp.broadcast_to(packed[:, at + h : at + h + 1], (packed.shape[0], HDIM))
            for h in range(heads)
        ],
        axis=1,
    )


def spread_rows(lines, width):
    high = lines.astype(BF16)
    low = (lines - high.astype(F32)).astype(BF16)
    row = lax.broadcasted_iota(jnp.int32, (16, width), 0)
    lane = lax.broadcasted_iota(jnp.int32, (16, width), 1)
    chosen = jnp.where((row & 7) == (lane >> 7), 1.0, 0.0).astype(BF16)
    return dot(jnp.concatenate([high, low], axis=0), chosen, 0, 0)


def block(j):
    return slice(j * BLOCK, (j + 1) * BLOCK)


def head(h):
    return slice(h * HDIM, (h + 1) * HDIM)


def turn(values):
    size = values.shape[0]
    unit = lax.broadcasted_iota(jnp.int32, (size, size), 0) == lax.broadcasted_iota(
        jnp.int32, (size, size), 1
    )
    return dot(jnp.where(unit, 1.0, 0.0).astype(BF16), values, 1, 1)


def silu(values):
    half = 0.5 * values
    return half + half * jnp.tanh(half)


def scatter_pieces(send, number, states):
    rows = STATE // send.shape[0]
    for piece in range(send.shape[0]):
        for h, state in enumerate(states):
            at = (number * len(states) + h) * rows
            send[piece, at : at + rows] = state[piece * rows : (piece + 1) * rows]


def gather_pieces(got, number, h, heads):
    rows = STATE // got.shape[0]
    at = (number * heads + h) * rows
    return got[:, at : at + rows].reshape(STATE, HDIM)


def start_all(copies):
    for copy in copies:
        copy.start()


def wait_all(copies):
    for copy in copies:
        copy.wait()


def part_copies(send, send_out, sems):
    half = send.shape[1] // 16 * 8
    parts = [pl.ds(0, half), pl.ds(half, send.shape[1] - half)]
    return [
        pltpu.make_async_copy(send.at[:, part], send_out.at[:, part], sems.at[i])
        for i, part in enumerate(parts)
    ]


def piece_copies(sources, targets, sems, pieces):
    result = []
    for i, (at, first, count) in enumerate(pieces):
        rows = pl.ds(first * BLOCK, count * BLOCK)
        result.append(
            [
                pltpu.make_async_copy(source(at, rows), target.at[at, rows], sems.at[i, a])
                for a, (source, target) in enumerate(zip(sources, targets))
            ]
        )
    return result


def block_ends(parts):
    lasts = [part[:, BLOCK - 1 :] for part in parts]
    before = [jnp.zeros((8, 1), F32)]
    for last in lasts[:-1]:
        before.append(before[-1] + last)
    after = [jnp.zeros((8, 1), F32)]
    for last in lasts[:0:-1]:
        after.insert(0, after[0] + last)
    return lasts, before, after


def states_body(heads, steps, decay_hbm, root_hbm, x_hbm, b_hbm, send_out, rows_out, rates, rows,
                decay, send, root, x, b, decay_sem, root_sem, sems, out_sem, send_sems):
    blocks = steps * CHUNK
    decay_copy = pltpu.make_async_copy(decay_hbm, decay, decay_sem)
    decay_copy.start()
    pieces = [(0, 0, CHUNK), (0, CHUNK, CHUNK), (1, 0, CHUNK), (1, CHUNK, CHUNK)]
    copies = piece_copies(
        [lambda at, span: x_hbm.at[at, 0, span], lambda at, span: b_hbm.at[at, 0, span]],
        [x, b],
        sems,
        pieces,
    )
    root_copy = pltpu.make_async_copy(root_hbm.at[0], root, root_sem)
    start_all(copies[0])
    root_copy.start()

    rates[...] = jnp.zeros_like(rates)
    upper = (
        lax.broadcasted_iota(jnp.int32, (BLOCK, BLOCK), 0)
        <= lax.broadcasted_iota(jnp.int32, (BLOCK, BLOCK), 1)
    )
    upper = jnp.where(upper, 1.0, 0.0).astype(BF16)
    decay_copy.wait()
    start_all(copies[1])
    for level in range(decay.shape[0]):
        for number in range(blocks):
            for h in range(heads):
                row = 8 * (level * blocks + number) + h
                rates[row : row + 1] = decay[level, h, :, block(number)]
    rest = rates[...]
    sums = jnp.zeros_like(rest)
    for _ in range(3):
        part = rest.astype(BF16)
        rest = rest - part.astype(F32)
        sums = sums + dot(part, upper, 1, 0)
    sums = sums * -LOG2E
    for chunk in range(rows.shape[0]):
        rows[chunk] = sums[WIDTH * chunk : WIDTH * (chunk + 1)]
    rows_copy = pltpu.make_async_copy(rows, rows_out, out_sem)
    rows_copy.start()

    to_level = []
    totals = []
    for level in range(2):
        numbers = range(level * blocks, (level + 1) * blocks)
        parts = [sums[8 * number : 8 * number + 8] for number in numbers]
        lasts, _, after = block_ends(parts)
        for part, last, suffix in zip(parts, lasts, after):
            to_level.append(jnp.exp2(last - part + suffix))
        totals.append(jnp.exp2(after[0] + lasts[0]))

    root_copy.wait()
    states = [(root[h] * totals[0][h : h + 1]).T for h in range(heads)]
    outs = part_copies(send, send_out, send_sems)
    for i, (level, first, count) in enumerate(pieces):
        if (level, first) == (1, 0):
            scatter_pieces(send, 0, states)
            outs[0].start()
            states = [jnp.zeros((STATE, HDIM), F32)] * heads
        wait_all(copies[i])
        if i > 0:
            start_all(sum(copies[i + 1 : i + 2], []))
        numbers = range(first, first + count)
        turned = [turn(b[level, block(number)]) for number in numbers]
        span = slice(first * BLOCK, (first + count) * BLOCK)
        for h in range(heads):
            decayed = [
                (values * to_level[level * blocks + number][h : h + 1]).astype(BF16)
                for number, values in zip(numbers, turned)
            ]
            states[h] = states[h] + dot(
                jnp.concatenate(decayed, axis=1), x[level, span, head(h)], 1, 0
            )
    scatter_pieces(send, 1, states)
    decays = jnp.broadcast_to(totals[1], (8, HDIM))
    for piece in range(send.shape[0]):
        send[piece, send.shape[1] - 8 :] = decays
    outs[1].start()
    wait_all(outs + [rows_copy])


def level_decays(rows, to_end):
    steps = rows.shape[0]
    parts = [rows[step, 8 * j : 8 * j + 8] for step in range(steps) for j in range(CHUNK)]
    lasts, before, after = block_ends(parts)
    if to_end:
        lines = [last - part + end for part, last, end in zip(parts, lasts, after)]
    else:
        lines = [start + part for part, start in zip(parts, before)]
    return [
        jnp.exp2(jnp.concatenate(lines[step * CHUNK : (step + 1) * CHUNK], axis=0))
        for step in range(steps)
    ]


def pack(rows, packed):
    for step in range(packed.shape[0]):
        part = rows[step]
        last = jnp.concatenate(
            [
                jnp.broadcast_to(part[8 * j : 8 * j + 8, BLOCK - 1 :], (8, BLOCK))
                for j in range(CHUNK)
            ],
            axis=0,
        )
        packed[step] = jnp.concatenate(
            [
                part,
                jnp.exp2(part),
                jnp.exp2(last - part),
                jnp.zeros((128 - 3 * WIDTH, BLOCK), F32),
            ],
            axis=0,
        ).T


def pick_body(heads, parent_ref, got_ref, send_out, decay_out, send, sems):
    segments = got_ref.shape[0]
    rows = STATE // segments
    pair = send.shape[1]
    half = pair // 2
    quarter = segments // 4
    copies = []
    for seg in range(segments):
        first = parent_ref[0, seg]
        second = parent_ref[1, seg]
        root = parent_ref[0, second]
        send[seg, :half] = got_ref[first, :half]
        decay = got_ref[second, pair : pair + 8]
        decay_out[seg] = got_ref[seg, pair : pair + 8]
        for h in range(heads):
            a = slice(h * rows, (h + 1) * rows)
            b = slice(half + h * rows, half + (h + 1) * rows)
            send[seg, b] = decay[h : h + 1] * got_ref[root, a] + got_ref[second, b]
        if (seg + 1) % quarter == 0:
            part = pl.ds(seg + 1 - quarter, quarter)
            copies.append(
                pltpu.make_async_copy(send.at[part], send_out.at[part], sems.at[len(copies)])
            )
            copies[-1].start()
    wait_all(copies)


def fold_body(heads, parent_ref, decay_ref, got_ref, send_out, send, sems):
    rows = STATE // got_ref.shape[0]
    half = send.shape[1] // 2
    send[...] = jnp.zeros_like(send)
    for seg in range(got_ref.shape[0]):
        second = parent_ref[1, seg]
        send[second, :half] += got_ref[seg, :half]
    copies = part_copies(send, send_out, sems)
    copies[0].start()
    for seg in range(got_ref.shape[0]):
        first = parent_ref[0, seg]
        decay = decay_ref[seg]
        for h in range(heads):
            a = slice(h * rows, (h + 1) * rows)
            b = slice(half + h * rows, half + (h + 1) * rows)
            send[first, b] += decay[h : h + 1] * send[seg, a] + got_ref[seg, b]
    copies[1].start()
    wait_all(copies)


def causal_mask(transposed):
    first = lax.broadcasted_iota(jnp.int32, (HALF, HALF), 0)
    second = lax.broadcasted_iota(jnp.int32, (HALF, HALF), 1)
    return first <= second if transposed else first >= second


def weighted(heads, j, rows, packed, x, b, c):
    scores = dot(c, b, 1, 1)
    causal = causal_mask(False)
    results = []
    for h in range(heads):
        row = rows[8 * j + h : 8 * j + h + 1]
        col = packed[:, CUM + 8 * j + h : CUM + 8 * j + h + 1]
        first = jnp.where(causal, col[:HALF] - row[:, :HALF], -jnp.inf)
        last = jnp.where(causal, col[HALF:] - row[:, HALF:], -jnp.inf)
        across = col[HALF:] - row[:, :HALF]
        top = jnp.concatenate(
            [(scores[:HALF, :HALF] * jnp.exp2(first)).astype(BF16), jnp.zeros((HALF, HALF), BF16)],
            axis=1,
        )
        bottom = jnp.concatenate(
            [
                (scores[HALF:, :HALF] * jnp.exp2(across)).astype(BF16),
                (scores[HALF:, HALF:] * jnp.exp2(last)).astype(BF16),
            ],
            axis=1,
        )
        results.append(dot(jnp.concatenate([top, bottom], axis=0), x[:, head(h)], 1, 0))
    return jnp.concatenate(results, axis=1)


def weighted_back(heads, j, rows, packed, grad, b, c):
    scores = dot(b, c, 1, 1)
    causal = causal_mask(True)
    results = []
    for h in range(heads):
        row = rows[8 * j + h : 8 * j + h + 1]
        col = packed[:, CUM + 8 * j + h : CUM + 8 * j + h + 1]
        first = jnp.where(causal, row[:, :HALF] - col[:HALF], -jnp.inf)
        last = jnp.where(causal, row[:, HALF:] - col[HALF:], -jnp.inf)
        across = row[:, HALF:] - col[:HALF]
        top = jnp.concatenate(
            [
                (scores[:HALF, :HALF] * jnp.exp2(first)).astype(BF16),
                (scores[:HALF, HALF:] * jnp.exp2(across)).astype(BF16),
            ],
            axis=1,
        )
        bottom = jnp.concatenate(
            [jnp.zeros((HALF, HALF), BF16), (scores[HALF:, HALF:] * jnp.exp2(last)).astype(BF16)],
            axis=1,
        )
        results.append(dot(jnp.concatenate([top, bottom], axis=0), grad[:, head(h)], 1, 0))
    return jnp.concatenate(results, axis=1)


def gated_sums(ssm_out, gate, out_grad, gain):
    act = silu(gate.astype(F32))
    gated = ssm_out * act
    scaled = out_grad.astype(F32) * gain
    ones = jnp.ones((8, gated.shape[1]), BF16)
    squares = dot(ones, (gated * gated).astype(BF16), 1, 1)
    products = dot(ones, (scaled * gated).astype(BF16), 1, 1)
    return gated, scaled * act, gated * act, (squares[:1], products[:1])


def store_sums(sums, step, at, pairs):
    for q in range(2):
        line = jnp.concatenate([pair[q] for pair in pairs], axis=1)
        for half in range(2):
            sums[4 * step + 2 * q + half : 4 * step + 2 * q + half + 1, at : at + FOLD] = line[
                :, half * FOLD : (half + 1) * FOLD
            ]


def norm_rows(total, step, at, features):
    lines = [total[4 * step + i : 4 * step + i + 1, at : at + FOLD] for i in range(4)]
    squares = jnp.concatenate(lines[:2], axis=1) / features
    dots = jnp.concatenate(lines[2:], axis=1) / features
    inv_rms = lax.rsqrt(squares + EPSILON)
    back = inv_rms * inv_rms * inv_rms * dots
    return jnp.concatenate([inv_rms, back, jnp.zeros((6, SPAN), F32)], axis=0)


def ssm_gradient(j, norm, gain, gate, out_grad, gated):
    inv_rms, back = norm[block(j), 0:1], norm[block(j), 1:2]
    grad = inv_rms * (out_grad.astype(F32) * gain) - gated.astype(F32) * back
    return (grad * silu(gate.astype(F32))).astype(BF16)


def forward0_body(heads, steps, rows_ref, root_ref, gain_ref, x_ref, gate_ref, b_ref, c_ref,
                  out_grad_ref, gated_ref, sums_ref, state, packs):
    step = pl.program_id(0)

    @pl.when(step == 0)
    def _():
        pack(rows_ref, packs)
        for h in range(heads):
            state[:, head(h)] = root_ref[0, h].T

    rows, packed = rows_ref[step], packs[step]
    current = state[...]
    pairs = []
    for j in range(CHUNK):
        x, b, c = x_ref[0, 0, block(j)], b_ref[0, 0, block(j)], c_ref[0, 0, block(j)]
        within = weighted(heads, j, rows, packed, x, b, c)
        carried = dot(c, current.astype(BF16), 1, 0) * spread(packed, FROM_BLOCK, j, heads)
        gated, _, _, pair = gated_sums(
            within + carried, gate_ref[0, 0, block(j)], out_grad_ref[0, 0, block(j)], gain_ref[...]
        )
        gated_ref[0, block(j)] = gated.astype(BF16)
        pairs.append(pair)
        decayed = (x.astype(F32) * spread(packed, TO_BLOCK, j, heads)).astype(BF16)
        factor = spread(packed[BLOCK - 1 :], FROM_BLOCK, j, heads)
        current = current * factor + dot(b, decayed, 0, 0)
    state[...] = current
    for part in range(steps):

        @pl.when(step == part)
        def _():
            store_sums(sums_ref, part, 0, pairs)


def scale_body(heads, steps, rows_ref, c_ref, out_ref, lines):
    step = pl.program_id(1)

    @pl.when(step == 0)
    def _():
        for part, line in enumerate(level_decays(rows_ref, False)):
            lines[part] = line

    columns = lines[step].T
    for j in range(CHUNK):
        c = c_ref[0, 0, block(j)].astype(F32)
        for h in range(heads):
            decay = columns[:, 8 * j + h : 8 * j + h + 1]
            out_ref[0, h, block(j)] = (c * decay).astype(BF16)


def local_body(heads, steps, rows_ref, x_ref, b_ref, c_ref, gate_hbm, scaled_hbm, out_grad_hbm,
               rows_hbm, out_ref, turned_ref, first_ref, gate_out, c_out, out_grad_out, rows_out,
               state, packs, sems):
    level, step = pl.program_id(0), pl.program_id(1)
    span = pl.ds(0, FIRST)
    copies = [
        pltpu.make_async_copy(source, target, sems.at[i])
        for i, (source, target) in enumerate(
            [
                (gate_hbm.at[1, 0, span], gate_out),
                (scaled_hbm.at[0, :, span], c_out),
                (out_grad_hbm.at[1, 0, span], out_grad_out),
                (rows_hbm.at[pl.ds(steps, 2 * steps)], rows_out),
            ]
        )
    ]

    @pl.when((level == 0) & (step == 0))
    def _():
        start_all(copies)

    @pl.when(step == 0)
    def _():
        pack(rows_ref, packs)
        state[...] = jnp.zeros_like(state)

    rows, packed = rows_ref[step], packs[step]
    current = state[...]
    for j in range(CHUNK):
        x, b, c = x_ref[0, 0, block(j)], b_ref[0, 0, block(j)], c_ref[0, 0, block(j)]
        within = weighted(heads, j, rows, packed, x, b, c)
        carried = dot(c, current.astype(BF16), 1, 0) * spread(packed, FROM_BLOCK, j, heads)
        out_ref[0, block(j)] = (within + carried).astype(BF16)
        turned_ref[0, :, block(j)] = turn(c).astype(BF16)
        decayed = (x.astype(F32) * spread(packed, TO_BLOCK, j, heads)).astype(BF16)
        factor = spread(packed[BLOCK - 1 :], FROM_BLOCK, j, heads)
        current = current * factor + dot(b, decayed, 0, 0)
    state[...] = current

    @pl.when((level == 0) & (step == 0))
    def _():
        first_ref[...] = out_ref[0, :FIRST]

    @pl.when((level == 1) & (step == steps - 1))
    def _():
        wait_all(copies)


def readout_body(heads, steps, local_hbm, gate_hbm, scaled_hbm, out_grad_hbm, turned_hbm, local_ref,
                 gate_ref, c_ref, out_grad_ref, rows_ref, start_ref, gain_ref, first_sums_ref,
                 scaled_act, gated_act, turned, lines, sums, local, gate, out_grad, c, sems,
                 turned_sem):
    early = FIRST // BLOCK
    pieces = [(0, early, CHUNK - early)]
    pieces += [(at, step * CHUNK, CHUNK) for at in range(2) for step in range(steps)][1:]
    copies = piece_copies(
        [
            lambda at, span: local_hbm.at[at, span],
            lambda at, span: gate_hbm.at[at + 1, 0, span],
            lambda at, span: out_grad_hbm.at[at + 1, 0, span],
        ]
        + [lambda at, span, h=h: scaled_hbm.at[at, h, span] for h in range(heads)],
        [local, gate, out_grad] + [c.at[h] for h in range(heads)],
        sems,
        pieces,
    )
    turned_copy = pltpu.make_async_copy(turned_hbm, turned, turned_sem)
    copies.append([turned_copy])
    start_all(copies[0] + copies[1])
    sums[0, :, :FOLD] = first_sums_ref[...]
    decays = []
    for at in range(2):
        decays += level_decays(rows_ref.at[pl.ds(at * steps, steps)], False)
    for chunk, line in enumerate(decays):
        lines[chunk] = line
    pairs = []
    for i, (at, first, count) in enumerate([(0, 0, early)] + pieces):
        if first == 0:
            starts = [gather_pieces(start_ref, at, h, heads).astype(BF16) for h in range(heads)]
        if i == 0:
            refs = [local_ref, gate_ref, out_grad_ref]
            scaled = [c_ref.at[h] for h in range(heads)]
        else:
            wait_all(copies[i - 1])
            start_all(sum(copies[i + 1 : i + 2], []))
            span = slice(first * BLOCK, (first + count) * BLOCK)
            refs = [buffer.at[at, span] for buffer in (local, gate, out_grad)]
            scaled = [c.at[h, at, span] for h in range(heads)]
        piece = jnp.concatenate(
            [dot(scaled[h][...], starts[h], 1, 0) for h in range(heads)], axis=1
        )
        for number in range(first, first + count):
            step, j = number // CHUNK, number % CHUNK
            mine = block(number - first)
            place = block(number)
            _, scaled_act[at, place], gated_act[at, place], pair = gated_sums(
                piece[mine] + refs[0][mine].astype(F32), refs[1][mine], refs[2][mine], gain_ref[...]
            )
            pairs.append(pair)
            if j == CHUNK - 1:
                store_sums(sums.at[0], step, (at + 1) * FOLD, pairs)
                pairs = []
    for copy in range(1, sums.shape[0]):
        sums[copy] = sums[0]
    turned_copy.wait()


def grads_body(heads, steps, features, lines_ref, turned_ref, scaled_act_ref, gated_act_ref,
               total_ref, grad_out, send_out, grads, send, grad_sems, sems):
    total = jnp.sum(total_ref[...], axis=0)
    sends = part_copies(send, send_out, sems)
    outs = []
    for at in (1, 0):
        for step in range(steps):
            norm = norm_rows(total, step, (at + 1) * FOLD, features)
            for j in range(CHUNK):
                place = block(step * CHUNK + j)
                factors = spread_rows(norm[:, block(j)], 2 * HDIM)
                inv_rms, back = factors[:, :HDIM], factors[:, HDIM:]
                for h in range(heads):
                    grad = inv_rms * scaled_act_ref[at, place, head(h)]
                    grad = grad - back * gated_act_ref[at, place, head(h)]
                    grads[at, place, head(h)] = grad.astype(BF16)
            span = pl.ds(step * SPAN, SPAN)
            outs.append(
                pltpu.make_async_copy(
                    grads.at[at, span], grad_out.at[at, span], grad_sems.at[at * steps + step]
                )
            )
            outs[-1].start()
    for at in (1, 0):
        states = [jnp.zeros((STATE, HDIM), F32)] * heads
        for step in range(steps):
            span = slice(step * SPAN, (step + 1) * SPAN)
            turned = turned_ref[at, :, span].astype(F32)
            lines = lines_ref[at * steps + step]
            for h in range(heads):
                line = jnp.concatenate(
                    [lines[8 * j + h : 8 * j + h + 1] for j in range(CHUNK)], axis=1
                )
                decayed = (turned * line).astype(BF16)
                states[h] = states[h] + dot(decayed, grads[at, span, head(h)], 1, 0)
        scatter_pieces(send, 1 - at, states)
        outs.append(sends[1 - at])
        outs[-1].start()
    wait_all(outs)


def back_chunk(heads, rows, packed, grad_of, b_ref, c_ref, state):
    current = state[...]
    for j in reversed(range(CHUNK)):
        b, c = b_ref[0, 0, block(j)], c_ref[0, 0, block(j)]
        grad = grad_of(j)
        within = weighted_back(heads, j, rows, packed, grad, b, c)
        carried = dot(b, current.astype(BF16), 1, 0) * spread(packed, TO_BLOCK, j, heads)
        yield j, (within + carried).astype(BF16)
        decayed = (grad.astype(F32) * spread(packed, FROM_BLOCK, j, heads)).astype(BF16)
        factor = spread(packed[BLOCK - 1 :], FROM_BLOCK, j, heads)
        current = current * factor + dot(c, decayed, 0, 0)
    state[...] = current


def back0_body(heads, steps, features, rows_ref, gain_ref, total_ref, gate_ref, b_ref, c_ref,
               out_grad_ref, gated_ref, partial_ref, state_grad_ref, state, packs, norms):
    step = steps - 1 - pl.program_id(0)

    @pl.when(step == steps - 1)
    def _():
        pack(rows_ref, packs)
        total = jnp.sum(total_ref[...], axis=0)
        for part in range(steps):
            norms[part] = norm_rows(total, part, 0, features).T
        state[...] = jnp.zeros_like(state)

    norm = norms[step]

    def grad_of(j):
        return ssm_gradient(
            j,
            norm,
            gain_ref[...],
            gate_ref[0, 0, block(j)],
            out_grad_ref[0, 0, block(j)],
            gated_ref[0, block(j)],
        )

    for j, part in back_chunk(heads, rows_ref[step], packs[step], grad_of, b_ref, c_ref, state):
        partial_ref[0, 0, block(j)] = part

    @pl.when(step == 0)
    def _():
        for h in range(heads):
            state_grad_ref[0, 0, h] = state[:, head(h)].T


def back_body(heads, steps, rows_ref, grad_ref, b_ref, c_ref, b_hbm, rows_hbm, given_in,
              given_state, partial_ref, state_grad_ref, near_ref, near_state_ref, b_out, rows_out,
              state, packs, sems):
    level, step = 2 - pl.program_id(0), steps - 1 - pl.program_id(1)
    copies = [
        pltpu.make_async_copy(b_hbm.at[1, 0, pl.ds(0, SPAN)], b_out, sems.at[0]),
        pltpu.make_async_copy(rows_hbm.at[pl.ds(0, 2 * steps)], rows_out, sems.at[1]),
    ]

    @pl.when((level == 2) & (step == steps - 1))
    def _():
        start_all(copies)

    @pl.when(step == steps - 1)
    def _():
        pack(rows_ref, packs)
        state[...] = jnp.zeros_like(state)

    def grad_of(j):
        return grad_ref[0, block(j)]

    for j, part in back_chunk(heads, rows_ref[step], packs[step], grad_of, b_ref, c_ref, state):
        partial_ref[0, 0, block(j)] = part

    @pl.when(step == 0)
    def _():
        for h in range(heads):
            state_grad_ref[0, 0, h] = state[:, head(h)].T

    @pl.when((level == 1) & (step == 0))
    def _():
        near_ref[...] = partial_ref[0, 0]
        near_state_ref[...] = state_grad_ref[0, 0]
        wait_all(copies)


def inputs_body(heads, steps, b_hbm, partial_hbm, local_hbm, b_ref, partial_ref, local_ref,
                rows_ref, end_ref, input_grad_out, state_grad_out, b, partial, grads, states, sems,
                local_sem, out_sems, state_sems):
    chunks = [(level, step) for level in (1, 0) for step in range(steps)]
    pieces = [(level, step * CHUNK, CHUNK) for level, step in chunks[1:]]
    copies = piece_copies(
        [lambda at, span: b_hbm.at[at, 0, span], lambda at, span: partial_hbm.at[at, 0, span]],
        [b, partial],
        sems,
        pieces,
    )
    local_copy = pltpu.make_async_copy(local_hbm.at[0, 0], states.at[0], local_sem)
    start_all(copies[0])
    local_copy.start()
    for some in copies[1:]:
        start_all(some)
    outs = []
    for i, (level, step) in enumerate(chunks):
        if step == 0:
            ends = [gather_pieces(end_ref, 1 - level, h, heads) for h in range(heads)]
            rounded = jnp.concatenate(ends, axis=1).astype(BF16)
            level_rows = rows_ref.at[pl.ds(level * steps, steps)]
            decays = level_decays(level_rows, True)
            total = level_decays(level_rows, False)[-1][8 * (CHUNK - 1) :, BLOCK - 1 :]
            if level == 0:
                local_copy.wait()
            for h in range(heads):
                local = local_ref[h] if level == 1 else states[0, h]
                states[level, h] = local + (ends[h] * total[h : h + 1]).T
            outs.append(
                pltpu.make_async_copy(
                    states.at[level], state_grad_out.at[level, 0], state_sems.at[level]
                )
            )
            outs[-1].start()
        span = slice(step * SPAN, (step + 1) * SPAN)
        if i == 0:
            some_b, some_partial = b_ref, partial_ref
        else:
            wait_all(copies[i - 1])
            some_b, some_partial = b.at[level, span], partial.at[level, span]
        piece = dot(some_b[...], rounded, 1, 0)
        for j in range(CHUNK):
            line = decays[step][8 * j : 8 * j + 8]
            extra = piece[block(j)] * spread_rows(line, heads * HDIM)
            grads[level, block(step * CHUNK + j)] = (
                some_partial[block(j)].astype(F32) + extra
            ).astype(BF16)
        span = pl.ds(step * SPAN, SPAN)
        outs.append(
            pltpu.make_async_copy(
                grads.at[level, span], input_grad_out.at[level, 0, span], out_sems.at[i]
            )
        )
        outs[-1].start()
    wait_all(outs)


def shards(features, head_devices, ssm_input, gate_input, b_input, c_output, log_decay,
           root_state, norm_gain, out_grad, parent_ids):
    levels, _, length, columns = ssm_input.shape
    heads = columns // HDIM
    blocks = length // BLOCK
    steps = blocks // CHUNK
    segments = parent_ids.shape[1]
    rows = STATE // segments
    gain = norm_gain.reshape(1, columns)
    decay = jnp.transpose(log_decay, (0, 2, 1, 3))

    smem = pl.BlockSpec(memory_space=pltpu.SMEM)
    vmem = pl.BlockSpec(memory_space=pltpu.VMEM)
    anywhere = pl.BlockSpec(memory_space=pl.ANY)
    rows_shape = (levels * steps, WIDTH, BLOCK)
    pair_shape = (segments, 2 * heads * rows, HDIM)
    first_shape = (segments, 2 * heads * rows + 8, HDIM)
    sums_shape = (head_devices, 8, levels * FOLD)
    state_shape = (levels, 1, heads, HDIM, STATE)
    state_scratch = pltpu.VMEM((STATE, columns), F32)
    packs_scratch = pltpu.VMEM((steps, BLOCK, 128), F32)
    dma = pltpu.SemaphoreType.DMA

    far = lambda array: pin(array, pltpu.HBM)
    near = lambda array: pin(array, pltpu.VMEM)
    x, gate, out_grad = far(ssm_input), far(gate_input), far(out_grad)
    decay = far(decay)
    b, c, root = far(b_input), far(c_output), far(root_state)

    def pair_of_levels(width):
        return pltpu.VMEM((2, length, width), BF16)

    def tokens(width, place):
        return pl.BlockSpec((1, 1, SPAN, width), lambda *g: (place(*g)[0], 0, place(*g)[1], 0))

    def flat(width, place):
        return pl.BlockSpec((1, SPAN, width), lambda *g: (*place(*g), 0))

    def level_rows(place):
        return pl.BlockSpec((steps,) + rows_shape[1:], lambda *g: (place(*g)[0], 0, 0))

    def state_grads(place):
        return pl.BlockSpec((1, 1, heads, HDIM, STATE), lambda *g: (place(*g)[0], 0, 0, 0, 0))

    exchange = functools.partial(
        lax.all_to_all, axis_name="seg", split_axis=0, concat_axis=0, tiled=True
    )

    send, cum_rows = call(
        functools.partial(states_body, heads, steps),
        "states",
        6,
        in_specs=[anywhere] * 4,
        out_specs=[anywhere, anywhere],
        out_shape=[pltpu.HBM(first_shape, F32), pltpu.HBM(rows_shape, F32)],
        scratch_shapes=[
            pltpu.VMEM((levels * blocks * 8, BLOCK), F32),
            pltpu.VMEM(rows_shape, F32),
            pltpu.VMEM(decay.shape, F32),
            pltpu.VMEM(first_shape, F32),
            pltpu.VMEM(root_state.shape[1:], F32),
            pair_of_levels(columns),
            pair_of_levels(STATE),
            dma,
            dma,
            dma((4, 2)),
            dma,
            dma((2,)),
        ],
    )(decay, root, x, b)
    got = exchange(send)

    own = lambda k: (0, k)
    gated0, sums0 = call(
        functools.partial(forward0_body, heads, steps),
        "forward0",
        6,
        grid=(steps,),
        in_specs=[
            level_rows(own),
            whole(root_state),
            whole(gain),
            tokens(columns, own),
            tokens(columns, own),
            tokens(STATE, own),
            tokens(STATE, own),
            tokens(columns, own),
        ],
        out_specs=[flat(columns, own), pl.BlockSpec((8, FOLD), lambda _: (0, 0))],
        out_shape=[pltpu.HBM((1, length, columns), BF16), pltpu.HBM((8, FOLD), F32)],
        scratch_shapes=[state_scratch, packs_scratch],
    )(far(cum_rows), root, gain, x, gate, b, c, out_grad)

    both = lambda l, k: (l, k)
    later = lambda l, k: (l + 1, k)
    scaled = call(
        functools.partial(scale_body, heads, steps),
        "scale",
        3,
        grid=(2, steps),
        in_specs=[level_rows(later), tokens(STATE, later)],
        out_specs=pl.BlockSpec((1, heads, SPAN, STATE), lambda l, k: (l, 0, k, 0)),
        out_shape=pltpu.HBM((2, heads, length, STATE), BF16),
        scratch_shapes=[pltpu.VMEM((steps,) + rows_shape[1:], F32)],
    )(far(cum_rows), c)

    got, sums0, scaled = lax.optimization_barrier((got, sums0, scaled))
    picked, decays = call(
        functools.partial(pick_body, heads),
        "pick",
        1,
        in_specs=[smem, vmem],
        out_specs=[anywhere, vmem],
        out_shape=[pltpu.HBM(pair_shape, F32), pltpu.VMEM((segments, 8, HDIM), F32)],
        scratch_shapes=[pltpu.VMEM(pair_shape, F32), dma((4,))],
    )(parent_ids, near(got))

    picked, late_rows = lax.optimization_barrier((picked, cum_rows))
    starts = exchange(picked)
    local, turned, *first = call(
        functools.partial(local_body, heads, steps),
        "local",
        7,
        grid=(2, steps),
        in_specs=[
            level_rows(later),
            tokens(columns, later),
            tokens(STATE, later),
            tokens(STATE, later),
        ]
        + [anywhere] * 4,
        out_specs=[
            flat(columns, both),
            pl.BlockSpec((1, STATE, SPAN), lambda l, k: (l, 0, k)),
            pl.BlockSpec((FIRST, columns), lambda l, k: (0, 0)),
        ]
        + [anywhere] * 4,
        out_shape=[
            pltpu.HBM((2, length, columns), BF16),
            pltpu.HBM((2, STATE, length), BF16),
            pltpu.VMEM((FIRST, columns), BF16),
            pltpu.VMEM((FIRST, columns), BF16),
            pltpu.VMEM((heads, FIRST, STATE), BF16),
            pltpu.VMEM((FIRST, columns), BF16),
            pltpu.VMEM((2 * steps,) + rows_shape[1:], F32),
        ],
        scratch_shapes=[state_scratch, packs_scratch, dma((4,))],
    )(far(late_rows), x, b, c, gate, far(scaled), out_grad, far(late_rows))

    scaled_act, gated_act, turned, lines, sums = call(
        functools.partial(readout_body, heads, steps),
        "readout",
        5,
        in_specs=[anywhere] * 5 + [vmem] * 8,
        out_specs=[vmem] * 5,
        out_shape=[
            pltpu.VMEM((2, length, columns), F32),
            pltpu.VMEM((2, length, columns), F32),
            pltpu.VMEM((2, STATE, length), BF16),
            pltpu.VMEM((2 * steps,) + rows_shape[1:], F32),
            pltpu.VMEM(sums_shape, F32),
        ],
        scratch_shapes=[
            pair_of_levels(columns),
            pair_of_levels(columns),
            pair_of_levels(columns),
            pltpu.VMEM((heads, 2, length, STATE), BF16),
            dma((2 * steps, 3 + heads)),
            dma,
        ],
    )(
        far(local),
        gate,
        far(scaled),
        out_grad,
        far(turned),
        near(first[0]),
        near(first[1]),
        near(first[2]),
        near(first[3]),
        near(first[4]),
        near(starts),
        gain,
        sums0,
    )
    totals = lax.all_to_all(sums, "head", split_axis=0, concat_axis=0, tiled=True)

    grads, send_back = call(
        functools.partial(grads_body, heads, steps, features),
        "grads",
        4,
        in_specs=[vmem] * 5,
        out_specs=[anywhere, anywhere],
        out_shape=[pltpu.HBM((2, length, columns), BF16), pltpu.HBM(pair_shape, F32)],
        scratch_shapes=[
            pair_of_levels(columns),
            pltpu.VMEM(pair_shape, F32),
            dma((2 * steps,)),
            dma((2,)),
        ],
    )(near(lines), near(turned), near(scaled_act), near(gated_act), near(totals))
    got_back = exchange(send_back)

    own_back = lambda k: (0, steps - 1 - k)
    given = call(
        functools.partial(back0_body, heads, steps, features),
        "back0",
        6,
        grid=(steps,),
        in_specs=[
            level_rows(own_back),
            whole(gain),
            pl.BlockSpec(sums_shape, lambda _: (0, 0, 0)),
            tokens(columns, own_back),
            tokens(STATE, own_back),
            tokens(STATE, own_back),
            tokens(columns, own_back),
            flat(columns, own_back),
        ],
        out_specs=[tokens(columns, own_back), state_grads(own_back)],
        out_shape=[pltpu.HBM(ssm_input.shape, BF16), pltpu.HBM(state_shape, F32)],
        scratch_shapes=[state_scratch, packs_scratch, pltpu.VMEM((steps, SPAN, 8), F32)],
    )(far(cum_rows), gain, totals, gate, b, c, out_grad, far(gated0))

    got_back, *given = lax.optimization_barrier((got_back, *given))
    folded = call(
        functools.partial(fold_body, heads),
        "fold",
        1,
        in_specs=[smem, vmem, vmem],
        out_specs=anywhere,
        out_shape=pltpu.HBM(pair_shape, F32),
        scratch_shapes=[pltpu.VMEM(pair_shape, F32), dma((2,))],
    )(parent_ids, near(decays), near(got_back))

    folded, late_rows = lax.optimization_barrier((folded, cum_rows))
    ends = exchange(folded)
    down_back = lambda l, k: (2 - l, steps - 1 - k)
    both_down_back = lambda l, k: (1 - l, steps - 1 - k)
    *given, near_partial, near_state, near_b, near_rows = call(
        functools.partial(back_body, heads, steps),
        "back",
        8,
        grid=(2, steps),
        in_specs=[
            level_rows(down_back),
            flat(columns, both_down_back),
            tokens(STATE, down_back),
            tokens(STATE, down_back),
        ]
        + [anywhere] * 4,
        out_specs=[
            tokens(columns, down_back),
            state_grads(down_back),
            pl.BlockSpec((SPAN, columns), lambda *g: (0, 0)),
            pl.BlockSpec((heads, HDIM, STATE), lambda *g: (0, 0, 0)),
            anywhere,
            anywhere,
        ],
        out_shape=[
            pltpu.HBM(ssm_input.shape, BF16),
            pltpu.HBM(state_shape, F32),
            pltpu.VMEM((SPAN, columns), BF16),
            pltpu.VMEM(state_shape[2:], F32),
            pltpu.VMEM((SPAN, STATE), BF16),
            pltpu.VMEM((2 * steps,) + rows_shape[1:], F32),
        ],
        input_output_aliases={6: 0, 7: 1},
        scratch_shapes=[state_scratch, packs_scratch, dma((2,))],
    )(far(late_rows), far(grads), b, c, b, far(late_rows), *given)

    return call(
        functools.partial(inputs_body, heads, steps),
        "inputs",
        4,
        in_specs=[anywhere] * 3 + [vmem] * 5,
        out_specs=[anywhere, anywhere],
        out_shape=[pltpu.HBM(ssm_input.shape, BF16), pltpu.HBM(state_shape, F32)],
        input_output_aliases={1: 0, 2: 1},
        scratch_shapes=[
            pair_of_levels(STATE),
            pair_of_levels(columns),
            pair_of_levels(columns),
            pltpu.VMEM((2,) + state_shape[2:], F32),
            dma((2 * steps - 1, 2)),
            dma,
            dma((2 * steps,)),
            dma((2,)),
        ],
    )(b, *given, near(near_b), near(near_partial), near(near_state), near(near_rows), near(ends))


def solution(mesh):
    in_specs = (
        P(None, "seg", None, "head"),
        P(None, "seg", None, "head"),
        P(None, "seg", None, None),
        P(None, "seg", None, None),
        P(None, "seg", "head", None),
        P("seg", "head", None, None),
        P("head"),
        P(None, "seg", None, "head"),
        P(),
    )
    out_specs = (P(None, "seg", None, "head"), P(None, "seg", "head", None, None))

    def run(*arrays):
        body = functools.partial(shards, arrays[0].shape[3], mesh.shape["head"])
        return tuple(
            jax.shard_map(
                body, mesh=mesh, in_specs=in_specs, out_specs=out_specs, check_vma=False
            )(*arrays)
        )

    return run
```

```python
import functools
import math

import jax
import jax.numpy as jnp
from jax import lax
from jax.experimental import pallas as pl
from jax.experimental.pallas import tpu as pltpu
from jax.sharding import PartitionSpec as P

BLOCK = 256
HALF = BLOCK // 2
HEADS = 24
HDIM = 128
STATE = 256
CHUNK = 3
SPAN = CHUNK * BLOCK
FIRST = 2 * BLOCK
FOLD = SPAN // 2
EPSILON = 1e-05
VMEM_LIMIT = 24 * 1024 * 1024
LOG2E = math.log2(math.e)

WIDTH = 8 * CHUNK
CUM = 0
FROM_BLOCK = WIDTH
TO_BLOCK = 2 * WIDTH

F32 = jnp.float32
BF16 = jnp.bfloat16
shaped = jax.ShapeDtypeStruct
pin = pltpu.with_memory_space_constraint


def call(body, name, micros, **kwargs):
    return pl.pallas_call(
        body,
        name=name,
        compiler_params=pltpu.CompilerParams(vmem_limit_bytes=VMEM_LIMIT),
        cost_estimate=pl.CostEstimate(
            flops=int(micros * 1e9), bytes_accessed=int(micros * 3e6), transcendentals=0
        ),
        **kwargs,
    )


def whole(array):
    rank = len(array.shape)
    return pl.BlockSpec(array.shape, lambda *_: (0,) * rank)


def dot(left, right, left_dim, right_dim, precision=None):
    return lax.dot_general(
        left,
        right,
        (((left_dim,), (right_dim,)), ((), ())),
        precision=precision,
        preferred_element_type=F32,
    )


def spread(packed, group, j, heads):
    at = group + 8 * j
    return jnp.concatenate(
        [
            jnp.broadcast_to(packed[:, at + h : at + h + 1], (packed.shape[0], HDIM))
            for h in range(heads)
        ],
        axis=1,
    )


def spread_rows(lines, width):
    high = lines.astype(BF16)
    low = (lines - high.astype(F32)).astype(BF16)
    row = lax.broadcasted_iota(jnp.int32, (16, width), 0)
    lane = lax.broadcasted_iota(jnp.int32, (16, width), 1)
    chosen = jnp.where((row & 7) == (lane >> 7), 1.0, 0.0).astype(BF16)
    return dot(jnp.concatenate([high, low], axis=0), chosen, 0, 0)


def block(j):
    return slice(j * BLOCK, (j + 1) * BLOCK)


def head(h):
    return slice(h * HDIM, (h + 1) * HDIM)


def turn(values):
    size = values.shape[0]
    unit = lax.broadcasted_iota(jnp.int32, (size, size), 0) == lax.broadcasted_iota(
        jnp.int32, (size, size), 1
    )
    return dot(jnp.where(unit, 1.0, 0.0).astype(BF16), values, 1, 1)


def silu(values):
    half = 0.5 * values
    return half + half * jnp.tanh(half)


def scatter_pieces(send, number, states):
    rows = STATE // send.shape[0]
    for piece in range(send.shape[0]):
        for h, state in enumerate(states):
            at = (number * len(states) + h) * rows
            send[piece, at : at + rows] = state[piece * rows : (piece + 1) * rows]


def gather_pieces(got, number, h, heads):
    rows = STATE // got.shape[0]
    at = (number * heads + h) * rows
    return got[:, at : at + rows].reshape(STATE, HDIM)


def start_all(copies):
    for copy in copies:
        copy.start()


def wait_all(copies):
    for copy in copies:
        copy.wait()


def part_copies(send, send_out, sems):
    half = send.shape[1] // 16 * 8
    parts = [pl.ds(0, half), pl.ds(half, send.shape[1] - half)]
    return [
        pltpu.make_async_copy(send.at[:, part], send_out.at[:, part], sems.at[i])
        for i, part in enumerate(parts)
    ]


def piece_copies(sources, targets, sems, pieces):
    result = []
    for i, (at, first, count) in enumerate(pieces):
        rows = pl.ds(first * BLOCK, count * BLOCK)
        result.append(
            [
                pltpu.make_async_copy(source(at, rows), target.at[at, rows], sems.at[i, a])
                for a, (source, target) in enumerate(zip(sources, targets))
            ]
        )
    return result


def block_ends(parts):
    lasts = [part[:, BLOCK - 1 :] for part in parts]
    before = [jnp.zeros((8, 1), F32)]
    for last in lasts[:-1]:
        before.append(before[-1] + last)
    after = [jnp.zeros((8, 1), F32)]
    for last in lasts[:0:-1]:
        after.insert(0, after[0] + last)
    return lasts, before, after


def states_body(heads, steps, decay_hbm, root_hbm, x_hbm, b_hbm, send_out, rows_out, rates, rows,
                decay, send, root, x, b, decay_sem, root_sem, sems, out_sem, send_sems):
    blocks = steps * CHUNK
    decay_copy = pltpu.make_async_copy(decay_hbm, decay, decay_sem)
    decay_copy.start()
    pieces = [(0, 0, CHUNK), (0, CHUNK, CHUNK), (1, 0, CHUNK), (1, CHUNK, CHUNK)]
    copies = piece_copies(
        [lambda at, span: x_hbm.at[at, 0, span], lambda at, span: b_hbm.at[at, 0, span]],
        [x, b],
        sems,
        pieces,
    )
    root_copy = pltpu.make_async_copy(root_hbm.at[0], root, root_sem)
    start_all(copies[0])
    root_copy.start()

    rates[...] = jnp.zeros_like(rates)
    upper = (
        lax.broadcasted_iota(jnp.int32, (BLOCK, BLOCK), 0)
        <= lax.broadcasted_iota(jnp.int32, (BLOCK, BLOCK), 1)
    )
    upper = jnp.where(upper, 1.0, 0.0).astype(BF16)
    decay_copy.wait()
    start_all(copies[1])
    for level in range(decay.shape[0]):
        for number in range(blocks):
            for h in range(heads):
                row = 8 * (level * blocks + number) + h
                rates[row : row + 1] = decay[level, h, :, block(number)]
    rest = rates[...]
    sums = jnp.zeros_like(rest)
    for _ in range(3):
        part = rest.astype(BF16)
        rest = rest - part.astype(F32)
        sums = sums + dot(part, upper, 1, 0)
    sums = sums * -LOG2E
    for chunk in range(rows.shape[0]):
        rows[chunk] = sums[WIDTH * chunk : WIDTH * (chunk + 1)]
    rows_copy = pltpu.make_async_copy(rows, rows_out, out_sem)
    rows_copy.start()

    to_level = []
    totals = []
    for level in range(2):
        numbers = range(level * blocks, (level + 1) * blocks)
        parts = [sums[8 * number : 8 * number + 8] for number in numbers]
        lasts, _, after = block_ends(parts)
        for part, last, suffix in zip(parts, lasts, after):
            to_level.append(jnp.exp2(last - part + suffix))
        totals.append(jnp.exp2(after[0] + lasts[0]))

    root_copy.wait()
    states = [(root[h] * totals[0][h : h + 1]).T for h in range(heads)]
    outs = part_copies(send, send_out, send_sems)
    for i, (level, first, count) in enumerate(pieces):
        if (level, first) == (1, 0):
            scatter_pieces(send, 0, states)
            outs[0].start()
            states = [jnp.zeros((STATE, HDIM), F32)] * heads
        wait_all(copies[i])
        if i > 0:
            start_all(sum(copies[i + 1 : i + 2], []))
        numbers = range(first, first + count)
        turned = [turn(b[level, block(number)]) for number in numbers]
        span = slice(first * BLOCK, (first + count) * BLOCK)
        for h in range(heads):
            decayed = [
                (values * to_level[level * blocks + number][h : h + 1]).astype(BF16)
                for number, values in zip(numbers, turned)
            ]
            states[h] = states[h] + dot(
                jnp.concatenate(decayed, axis=1), x[level, span, head(h)], 1, 0
            )
    scatter_pieces(send, 1, states)
    decays = jnp.broadcast_to(totals[1], (8, HDIM))
    for piece in range(send.shape[0]):
        send[piece, send.shape[1] - 8 :] = decays
    outs[1].start()
    wait_all(outs + [rows_copy])


def level_decays(rows, to_end):
    steps = rows.shape[0]
    parts = [rows[step, 8 * j : 8 * j + 8] for step in range(steps) for j in range(CHUNK)]
    lasts, before, after = block_ends(parts)
    if to_end:
        lines = [last - part + end for part, last, end in zip(parts, lasts, after)]
    else:
        lines = [start + part for part, start in zip(parts, before)]
    return [
        jnp.exp2(jnp.concatenate(lines[step * CHUNK : (step + 1) * CHUNK], axis=0))
        for step in range(steps)
    ]


def pack(rows, packed):
    for step in range(packed.shape[0]):
        part = rows[step]
        last = jnp.concatenate(
            [
                jnp.broadcast_to(part[8 * j : 8 * j + 8, BLOCK - 1 :], (8, BLOCK))
                for j in range(CHUNK)
            ],
            axis=0,
        )
        packed[step] = jnp.concatenate(
            [
                part,
                jnp.exp2(part),
                jnp.exp2(last - part),
                jnp.zeros((128 - 3 * WIDTH, BLOCK), F32),
            ],
            axis=0,
        ).T


def pick_body(heads, parent_ref, got_ref, send_out, decay_out, send, sems):
    segments = got_ref.shape[0]
    rows = STATE // segments
    pair = send.shape[1]
    half = pair // 2
    quarter = segments // 4
    copies = []
    for seg in range(segments):
        first = parent_ref[0, seg]
        second = parent_ref[1, seg]
        root = parent_ref[0, second]
        send[seg, :half] = got_ref[first, :half]
        decay = got_ref[second, pair : pair + 8]
        decay_out[seg] = got_ref[seg, pair : pair + 8]
        for h in range(heads):
            a = slice(h * rows, (h + 1) * rows)
            b = slice(half + h * rows, half + (h + 1) * rows)
            send[seg, b] = decay[h : h + 1] * got_ref[root, a] + got_ref[second, b]
        if (seg + 1) % quarter == 0:
            part = pl.ds(seg + 1 - quarter, quarter)
            copies.append(
                pltpu.make_async_copy(send.at[part], send_out.at[part], sems.at[len(copies)])
            )
            copies[-1].start()
    wait_all(copies)


def fold_body(heads, parent_ref, decay_ref, got_ref, send_out, send, sems):
    rows = STATE // got_ref.shape[0]
    half = send.shape[1] // 2
    send[...] = jnp.zeros_like(send)
    for seg in range(got_ref.shape[0]):
        second = parent_ref[1, seg]
        send[second, :half] += got_ref[seg, :half]
    copies = part_copies(send, send_out, sems)
    copies[0].start()
    for seg in range(got_ref.shape[0]):
        first = parent_ref[0, seg]
        decay = decay_ref[seg]
        for h in range(heads):
            a = slice(h * rows, (h + 1) * rows)
            b = slice(half + h * rows, half + (h + 1) * rows)
            send[first, b] += decay[h : h + 1] * send[seg, a] + got_ref[seg, b]
    copies[1].start()
    wait_all(copies)


def causal_mask(transposed):
    first = lax.broadcasted_iota(jnp.int32, (HALF, HALF), 0)
    second = lax.broadcasted_iota(jnp.int32, (HALF, HALF), 1)
    return first <= second if transposed else first >= second


def weighted(heads, j, rows, packed, x, b, c):
    scores = dot(c, b, 1, 1)
    causal = causal_mask(False)
    results = []
    for h in range(heads):
        row = rows[8 * j + h : 8 * j + h + 1]
        col = packed[:, CUM + 8 * j + h : CUM + 8 * j + h + 1]
        first = jnp.where(causal, col[:HALF] - row[:, :HALF], -jnp.inf)
        last = jnp.where(causal, col[HALF:] - row[:, HALF:], -jnp.inf)
        across = col[HALF:] - row[:, :HALF]
        top = jnp.concatenate(
            [(scores[:HALF, :HALF] * jnp.exp2(first)).astype(BF16), jnp.zeros((HALF, HALF), BF16)],
            axis=1,
        )
        bottom = jnp.concatenate(
            [
                (scores[HALF:, :HALF] * jnp.exp2(across)).astype(BF16),
                (scores[HALF:, HALF:] * jnp.exp2(last)).astype(BF16),
            ],
            axis=1,
        )
        results.append(dot(jnp.concatenate([top, bottom], axis=0), x[:, head(h)], 1, 0))
    return jnp.concatenate(results, axis=1)


def weighted_back(heads, j, rows, packed, grad, b, c):
    scores = dot(b, c, 1, 1)
    causal = causal_mask(True)
    results = []
    for h in range(heads):
        row = rows[8 * j + h : 8 * j + h + 1]
        col = packed[:, CUM + 8 * j + h : CUM + 8 * j + h + 1]
        first = jnp.where(causal, row[:, :HALF] - col[:HALF], -jnp.inf)
        last = jnp.where(causal, row[:, HALF:] - col[HALF:], -jnp.inf)
        across = row[:, HALF:] - col[:HALF]
        top = jnp.concatenate(
            [
                (scores[:HALF, :HALF] * jnp.exp2(first)).astype(BF16),
                (scores[:HALF, HALF:] * jnp.exp2(across)).astype(BF16),
            ],
            axis=1,
        )
        bottom = jnp.concatenate(
            [jnp.zeros((HALF, HALF), BF16), (scores[HALF:, HALF:] * jnp.exp2(last)).astype(BF16)],
            axis=1,
        )
        results.append(dot(jnp.concatenate([top, bottom], axis=0), grad[:, head(h)], 1, 0))
    return jnp.concatenate(results, axis=1)


def gated_sums(ssm_out, gate, out_grad, gain):
    act = silu(gate.astype(F32))
    gated = ssm_out * act
    scaled = out_grad.astype(F32) * gain
    ones = jnp.ones((8, gated.shape[1]), BF16)
    squares = dot(ones, (gated * gated).astype(BF16), 1, 1)
    products = dot(ones, (scaled * gated).astype(BF16), 1, 1)
    return gated, scaled * act, gated * act, (squares[:1], products[:1])


def store_sums(sums, step, at, pairs):
    for q in range(2):
        line = jnp.concatenate([pair[q] for pair in pairs], axis=1)
        for half in range(2):
            sums[4 * step + 2 * q + half : 4 * step + 2 * q + half + 1, at : at + FOLD] = line[
                :, half * FOLD : (half + 1) * FOLD
            ]


def norm_rows(total, step, at, features):
    lines = [total[4 * step + i : 4 * step + i + 1, at : at + FOLD] for i in range(4)]
    squares = jnp.concatenate(lines[:2], axis=1) / features
    dots = jnp.concatenate(lines[2:], axis=1) / features
    inv_rms = lax.rsqrt(squares + EPSILON)
    back = inv_rms * inv_rms * inv_rms * dots
    return jnp.concatenate([inv_rms, back, jnp.zeros((6, SPAN), F32)], axis=0)


def ssm_gradient(j, norm, gain, gate, out_grad, gated):
    inv_rms, back = norm[block(j), 0:1], norm[block(j), 1:2]
    grad = inv_rms * (out_grad.astype(F32) * gain) - gated.astype(F32) * back
    return (grad * silu(gate.astype(F32))).astype(BF16)


def forward0_body(heads, steps, rows_ref, root_ref, gain_ref, x_ref, gate_ref, b_ref, c_ref,
                  out_grad_ref, gated_ref, sums_ref, state, packs):
    step = pl.program_id(0)

    @pl.when(step == 0)
    def _():
        pack(rows_ref, packs)
        for h in range(heads):
            state[:, head(h)] = root_ref[0, h].T

    rows, packed = rows_ref[step], packs[step]
    current = state[...]
    pairs = []
    for j in range(CHUNK):
        x, b, c = x_ref[0, 0, block(j)], b_ref[0, 0, block(j)], c_ref[0, 0, block(j)]
        within = weighted(heads, j, rows, packed, x, b, c)
        carried = dot(c, current.astype(BF16), 1, 0) * spread(packed, FROM_BLOCK, j, heads)
        gated, _, _, pair = gated_sums(
            within + carried, gate_ref[0, 0, block(j)], out_grad_ref[0, 0, block(j)], gain_ref[...]
        )
        gated_ref[0, block(j)] = gated.astype(BF16)
        pairs.append(pair)
        decayed = (x.astype(F32) * spread(packed, TO_BLOCK, j, heads)).astype(BF16)
        factor = spread(packed[BLOCK - 1 :], FROM_BLOCK, j, heads)
        current = current * factor + dot(b, decayed, 0, 0)
    state[...] = current
    for part in range(steps):

        @pl.when(step == part)
        def _():
            store_sums(sums_ref, part, 0, pairs)


def local_body(heads, steps, rows_ref, x_ref, b_ref, c_ref, gate_hbm, c_hbm, out_grad_hbm,
               rows_hbm, out_ref, turned_ref, first_ref, gate_out, c_out, out_grad_out, rows_out,
               state, packs, sems):
    level, step = pl.program_id(0), pl.program_id(1)
    span = pl.ds(0, FIRST)
    copies = [
        pltpu.make_async_copy(source, target, sems.at[i])
        for i, (source, target) in enumerate(
            [
                (gate_hbm.at[1, 0, span], gate_out),
                (c_hbm.at[1, 0, span], c_out),
                (out_grad_hbm.at[1, 0, span], out_grad_out),
                (rows_hbm.at[pl.ds(steps, 2 * steps)], rows_out),
            ]
        )
    ]

    @pl.when((level == 0) & (step == 0))
    def _():
        start_all(copies)

    @pl.when(step == 0)
    def _():
        pack(rows_ref, packs)
        state[...] = jnp.zeros_like(state)

    rows, packed = rows_ref[step], packs[step]
    current = state[...]
    for j in range(CHUNK):
        x, b, c = x_ref[0, 0, block(j)], b_ref[0, 0, block(j)], c_ref[0, 0, block(j)]
        within = weighted(heads, j, rows, packed, x, b, c)
        carried = dot(c, current.astype(BF16), 1, 0) * spread(packed, FROM_BLOCK, j, heads)
        out_ref[0, block(j)] = (within + carried).astype(BF16)
        turned_ref[0, :, block(j)] = turn(c).astype(BF16)
        decayed = (x.astype(F32) * spread(packed, TO_BLOCK, j, heads)).astype(BF16)
        factor = spread(packed[BLOCK - 1 :], FROM_BLOCK, j, heads)
        current = current * factor + dot(b, decayed, 0, 0)
    state[...] = current

    @pl.when((level == 0) & (step == 0))
    def _():
        first_ref[...] = out_ref[0, :FIRST]

    @pl.when((level == 1) & (step == steps - 1))
    def _():
        wait_all(copies)


def readout_body(heads, steps, local_hbm, gate_hbm, c_hbm, out_grad_hbm, turned_hbm, local_ref,
                 gate_ref, c_ref, out_grad_ref, rows_ref, start_ref, gain_ref, first_sums_ref,
                 scaled_act, gated_act, turned, lines, sums, local, gate, out_grad, c, sems,
                 turned_sem):
    early = FIRST // BLOCK
    pieces = [(0, early, CHUNK - early)]
    pieces += [(at, step * CHUNK, CHUNK) for at in range(2) for step in range(steps)][1:]
    copies = piece_copies(
        [
            lambda at, span: c_hbm.at[at + 1, 0, span],
            lambda at, span: local_hbm.at[at, span],
            lambda at, span: gate_hbm.at[at + 1, 0, span],
            lambda at, span: out_grad_hbm.at[at + 1, 0, span],
        ],
        [c, local, gate, out_grad],
        sems,
        pieces,
    )
    turned_copy = pltpu.make_async_copy(turned_hbm, turned, turned_sem)
    copies.append([turned_copy])
    start_all(copies[0] + copies[1])
    sums[0, :, :FOLD] = first_sums_ref[...]
    decays = []
    for at in range(2):
        decays += level_decays(rows_ref.at[pl.ds(at * steps, steps)], False)
    columns = []
    for chunk, line in enumerate(decays):
        lines[chunk] = line
        columns.append(line.T)
    pairs = []
    for i, (at, first, count) in enumerate([(0, 0, early)] + pieces):
        if first == 0:
            start = jnp.concatenate(
                [gather_pieces(start_ref, at, h, heads) for h in range(heads)], axis=1
            ).astype(BF16)
        if i == 0:
            refs = [c_ref, local_ref, gate_ref, out_grad_ref]
        else:
            wait_all(copies[i - 1])
            start_all(sum(copies[i + 1 : i + 2], []))
            span = slice(first * BLOCK, (first + count) * BLOCK)
            refs = [buffer.at[at, span] for buffer in (c, local, gate, out_grad)]
        piece = dot(refs[0][...], start, 1, 0)
        for number in range(first, first + count):
            step, j = number // CHUNK, number % CHUNK
            mine = block(number - first)
            carried = piece[mine] * spread(columns[at * steps + step], 0, j, heads)
            place = block(number)
            _, scaled_act[at, place], gated_act[at, place], pair = gated_sums(
                carried + refs[1][mine].astype(F32), refs[2][mine], refs[3][mine], gain_ref[...]
            )
            pairs.append(pair)
            if j == CHUNK - 1:
                store_sums(sums.at[0], step, (at + 1) * FOLD, pairs)
                pairs = []
    for copy in range(1, sums.shape[0]):
        sums[copy] = sums[0]
    turned_copy.wait()


def grads_body(heads, steps, features, lines_ref, turned_ref, scaled_act_ref, gated_act_ref,
               total_ref, grad_out, send_out, grads, send, grad_sems, sems):
    total = jnp.sum(total_ref[...], axis=0)
    sends = part_copies(send, send_out, sems)
    outs = []
    for at in (1, 0):
        for step in range(steps):
            norm = norm_rows(total, step, (at + 1) * FOLD, features)
            for j in range(CHUNK):
                place = block(step * CHUNK + j)
                factors = spread_rows(norm[:, block(j)], 2 * HDIM)
                inv_rms, back = factors[:, :HDIM], factors[:, HDIM:]
                for h in range(heads):
                    grad = inv_rms * scaled_act_ref[at, place, head(h)]
                    grad = grad - back * gated_act_ref[at, place, head(h)]
                    grads[at, place, head(h)] = grad.astype(BF16)
            span = pl.ds(step * SPAN, SPAN)
            outs.append(
                pltpu.make_async_copy(
                    grads.at[at, span], grad_out.at[at, span], grad_sems.at[at * steps + step]
                )
            )
            outs[-1].start()
    for at in (1, 0):
        states = [jnp.zeros((STATE, HDIM), F32)] * heads
        for step in range(steps):
            span = slice(step * SPAN, (step + 1) * SPAN)
            turned = turned_ref[at, :, span].astype(F32)
            lines = lines_ref[at * steps + step]
            for h in range(heads):
                line = jnp.concatenate(
                    [lines[8 * j + h : 8 * j + h + 1] for j in range(CHUNK)], axis=1
                )
                decayed = (turned * line).astype(BF16)
                states[h] = states[h] + dot(decayed, grads[at, span, head(h)], 1, 0)
        scatter_pieces(send, 1 - at, states)
        outs.append(sends[1 - at])
        outs[-1].start()
    wait_all(outs)


def back_chunk(heads, rows, packed, grad_of, b_ref, c_ref, state):
    current = state[...]
    for j in reversed(range(CHUNK)):
        b, c = b_ref[0, 0, block(j)], c_ref[0, 0, block(j)]
        grad = grad_of(j)
        within = weighted_back(heads, j, rows, packed, grad, b, c)
        carried = dot(b, current.astype(BF16), 1, 0) * spread(packed, TO_BLOCK, j, heads)
        yield j, (within + carried).astype(BF16)
        decayed = (grad.astype(F32) * spread(packed, FROM_BLOCK, j, heads)).astype(BF16)
        factor = spread(packed[BLOCK - 1 :], FROM_BLOCK, j, heads)
        current = current * factor + dot(c, decayed, 0, 0)
    state[...] = current


def back0_body(heads, steps, features, rows_ref, gain_ref, total_ref, gate_ref, b_ref, c_ref,
               out_grad_ref, gated_ref, partial_ref, state_grad_ref, state, packs, norms):
    step = steps - 1 - pl.program_id(0)

    @pl.when(step == steps - 1)
    def _():
        pack(rows_ref, packs)
        total = jnp.sum(total_ref[...], axis=0)
        for part in range(steps):
            norms[part] = norm_rows(total, part, 0, features).T
        state[...] = jnp.zeros_like(state)

    norm = norms[step]

    def grad_of(j):
        return ssm_gradient(
            j,
            norm,
            gain_ref[...],
            gate_ref[0, 0, block(j)],
            out_grad_ref[0, 0, block(j)],
            gated_ref[0, block(j)],
        )

    for j, part in back_chunk(heads, rows_ref[step], packs[step], grad_of, b_ref, c_ref, state):
        partial_ref[0, 0, block(j)] = part

    @pl.when(step == 0)
    def _():
        for h in range(heads):
            state_grad_ref[0, 0, h] = state[:, head(h)].T


def back_body(heads, steps, rows_ref, grad_ref, b_ref, c_ref, b_hbm, rows_hbm, given_in,
              given_state, partial_ref, state_grad_ref, near_ref, near_state_ref, b_out, rows_out,
              state, packs, sems):
    level, step = 2 - pl.program_id(0), steps - 1 - pl.program_id(1)
    copies = [
        pltpu.make_async_copy(b_hbm.at[1, 0, pl.ds(0, SPAN)], b_out, sems.at[0]),
        pltpu.make_async_copy(rows_hbm.at[pl.ds(0, 2 * steps)], rows_out, sems.at[1]),
    ]

    @pl.when((level == 2) & (step == steps - 1))
    def _():
        start_all(copies)

    @pl.when(step == steps - 1)
    def _():
        pack(rows_ref, packs)
        state[...] = jnp.zeros_like(state)

    def grad_of(j):
        return grad_ref[0, block(j)]

    for j, part in back_chunk(heads, rows_ref[step], packs[step], grad_of, b_ref, c_ref, state):
        partial_ref[0, 0, block(j)] = part

    @pl.when(step == 0)
    def _():
        for h in range(heads):
            state_grad_ref[0, 0, h] = state[:, head(h)].T

    @pl.when((level == 1) & (step == 0))
    def _():
        near_ref[...] = partial_ref[0, 0]
        near_state_ref[...] = state_grad_ref[0, 0]
        wait_all(copies)


def inputs_body(heads, steps, b_hbm, partial_hbm, local_hbm, b_ref, partial_ref, local_ref,
                rows_ref, end_ref, input_grad_out, state_grad_out, b, partial, grads, states, sems,
                local_sem, out_sems, state_sems):
    chunks = [(level, step) for level in (1, 0) for step in range(steps)]
    pieces = [(level, step * CHUNK, CHUNK) for level, step in chunks[1:]]
    copies = piece_copies(
        [lambda at, span: b_hbm.at[at, 0, span], lambda at, span: partial_hbm.at[at, 0, span]],
        [b, partial],
        sems,
        pieces,
    )
    local_copy = pltpu.make_async_copy(local_hbm.at[0, 0], states.at[0], local_sem)
    start_all(copies[0])
    local_copy.start()
    for some in copies[1:]:
        start_all(some)
    outs = []
    for i, (level, step) in enumerate(chunks):
        if step == 0:
            ends = [gather_pieces(end_ref, 1 - level, h, heads) for h in range(heads)]
            rounded = jnp.concatenate(ends, axis=1).astype(BF16)
            level_rows = rows_ref.at[pl.ds(level * steps, steps)]
            decays = level_decays(level_rows, True)
            total = level_decays(level_rows, False)[-1][8 * (CHUNK - 1) :, BLOCK - 1 :]
            if level == 0:
                local_copy.wait()
            for h in range(heads):
                local = local_ref[h] if level == 1 else states[0, h]
                states[level, h] = local + (ends[h] * total[h : h + 1]).T
            outs.append(
                pltpu.make_async_copy(
                    states.at[level], state_grad_out.at[level, 0], state_sems.at[level]
                )
            )
            outs[-1].start()
        span = slice(step * SPAN, (step + 1) * SPAN)
        if i == 0:
            some_b, some_partial = b_ref, partial_ref
        else:
            wait_all(copies[i - 1])
            some_b, some_partial = b.at[level, span], partial.at[level, span]
        piece = dot(some_b[...], rounded, 1, 0)
        for j in range(CHUNK):
            line = decays[step][8 * j : 8 * j + 8]
            extra = piece[block(j)] * spread_rows(line, heads * HDIM)
            grads[level, block(step * CHUNK + j)] = (
                some_partial[block(j)].astype(F32) + extra
            ).astype(BF16)
        span = pl.ds(step * SPAN, SPAN)
        outs.append(
            pltpu.make_async_copy(
                grads.at[level, span], input_grad_out.at[level, 0, span], out_sems.at[i]
            )
        )
        outs[-1].start()
    wait_all(outs)


def shards(features, head_devices, ssm_input, gate_input, b_input, c_output, log_decay,
           root_state, norm_gain, out_grad, parent_ids):
    levels, _, length, columns = ssm_input.shape
    heads = columns // HDIM
    blocks = length // BLOCK
    steps = blocks // CHUNK
    segments = parent_ids.shape[1]
    rows = STATE // segments
    gain = norm_gain.reshape(1, columns)
    decay = jnp.transpose(log_decay, (0, 2, 1, 3))

    smem = pl.BlockSpec(memory_space=pltpu.SMEM)
    vmem = pl.BlockSpec(memory_space=pltpu.VMEM)
    anywhere = pl.BlockSpec(memory_space=pl.ANY)
    rows_shape = (levels * steps, WIDTH, BLOCK)
    pair_shape = (segments, 2 * heads * rows, HDIM)
    first_shape = (segments, 2 * heads * rows + 8, HDIM)
    sums_shape = (head_devices, 8, levels * FOLD)
    state_shape = (levels, 1, heads, HDIM, STATE)
    state_scratch = pltpu.VMEM((STATE, columns), F32)
    packs_scratch = pltpu.VMEM((steps, BLOCK, 128), F32)
    dma = pltpu.SemaphoreType.DMA

    far = lambda array: pin(array, pltpu.HBM)
    near = lambda array: pin(array, pltpu.VMEM)
    x, gate, out_grad = far(ssm_input), far(gate_input), far(out_grad)
    decay = far(decay)
    b, c, root = far(b_input), far(c_output), far(root_state)

    def pair_of_levels(width):
        return pltpu.VMEM((2, length, width), BF16)

    def tokens(width, place):
        return pl.BlockSpec((1, 1, SPAN, width), lambda *g: (place(*g)[0], 0, place(*g)[1], 0))

    def flat(width, place):
        return pl.BlockSpec((1, SPAN, width), lambda *g: (*place(*g), 0))

    def level_rows(place):
        return pl.BlockSpec((steps,) + rows_shape[1:], lambda *g: (place(*g)[0], 0, 0))

    def state_grads(place):
        return pl.BlockSpec((1, 1, heads, HDIM, STATE), lambda *g: (place(*g)[0], 0, 0, 0, 0))

    exchange = functools.partial(
        lax.all_to_all, axis_name="seg", split_axis=0, concat_axis=0, tiled=True
    )

    send, cum_rows = call(
        functools.partial(states_body, heads, steps),
        "states",
        6,
        in_specs=[anywhere] * 4,
        out_specs=[anywhere, anywhere],
        out_shape=[pltpu.HBM(first_shape, F32), pltpu.HBM(rows_shape, F32)],
        scratch_shapes=[
            pltpu.VMEM((levels * blocks * 8, BLOCK), F32),
            pltpu.VMEM(rows_shape, F32),
            pltpu.VMEM(decay.shape, F32),
            pltpu.VMEM(first_shape, F32),
            pltpu.VMEM(root_state.shape[1:], F32),
            pair_of_levels(columns),
            pair_of_levels(STATE),
            dma,
            dma,
            dma((4, 2)),
            dma,
            dma((2,)),
        ],
    )(decay, root, x, b)
    got = exchange(send)

    own = lambda k: (0, k)
    gated0, sums0 = call(
        functools.partial(forward0_body, heads, steps),
        "forward0",
        6,
        grid=(steps,),
        in_specs=[
            level_rows(own),
            whole(root_state),
            whole(gain),
            tokens(columns, own),
            tokens(columns, own),
            tokens(STATE, own),
            tokens(STATE, own),
            tokens(columns, own),
        ],
        out_specs=[flat(columns, own), pl.BlockSpec((8, FOLD), lambda _: (0, 0))],
        out_shape=[pltpu.HBM((1, length, columns), BF16), pltpu.HBM((8, FOLD), F32)],
        scratch_shapes=[state_scratch, packs_scratch],
    )(far(cum_rows), root, gain, x, gate, b, c, out_grad)

    got, sums0 = lax.optimization_barrier((got, sums0))
    picked, decays = call(
        functools.partial(pick_body, heads),
        "pick",
        1,
        in_specs=[smem, vmem],
        out_specs=[anywhere, vmem],
        out_shape=[pltpu.HBM(pair_shape, F32), pltpu.VMEM((segments, 8, HDIM), F32)],
        scratch_shapes=[pltpu.VMEM(pair_shape, F32), dma((4,))],
    )(parent_ids, near(got))

    picked, late_rows = lax.optimization_barrier((picked, cum_rows))
    starts = exchange(picked)
    both = lambda l, k: (l, k)
    later = lambda l, k: (l + 1, k)
    local, turned, *first = call(
        functools.partial(local_body, heads, steps),
        "local",
        7,
        grid=(2, steps),
        in_specs=[
            level_rows(later),
            tokens(columns, later),
            tokens(STATE, later),
            tokens(STATE, later),
        ]
        + [anywhere] * 4,
        out_specs=[
            flat(columns, both),
            pl.BlockSpec((1, STATE, SPAN), lambda l, k: (l, 0, k)),
            pl.BlockSpec((FIRST, columns), lambda l, k: (0, 0)),
        ]
        + [anywhere] * 4,
        out_shape=[
            pltpu.HBM((2, length, columns), BF16),
            pltpu.HBM((2, STATE, length), BF16),
            pltpu.VMEM((FIRST, columns), BF16),
            pltpu.VMEM((FIRST, columns), BF16),
            pltpu.VMEM((FIRST, STATE), BF16),
            pltpu.VMEM((FIRST, columns), BF16),
            pltpu.VMEM((2 * steps,) + rows_shape[1:], F32),
        ],
        scratch_shapes=[state_scratch, packs_scratch, dma((4,))],
    )(far(late_rows), x, b, c, gate, c, out_grad, far(late_rows))

    scaled_act, gated_act, turned, lines, sums = call(
        functools.partial(readout_body, heads, steps),
        "readout",
        5,
        in_specs=[anywhere] * 5 + [vmem] * 8,
        out_specs=[vmem] * 5,
        out_shape=[
            pltpu.VMEM((2, length, columns), F32),
            pltpu.VMEM((2, length, columns), F32),
            pltpu.VMEM((2, STATE, length), BF16),
            pltpu.VMEM((2 * steps,) + rows_shape[1:], F32),
            pltpu.VMEM(sums_shape, F32),
        ],
        scratch_shapes=[
            pair_of_levels(columns),
            pair_of_levels(columns),
            pair_of_levels(columns),
            pair_of_levels(STATE),
            dma((2 * steps, 4)),
            dma,
        ],
    )(
        far(local),
        gate,
        c,
        out_grad,
        far(turned),
        near(first[0]),
        near(first[1]),
        near(first[2]),
        near(first[3]),
        near(first[4]),
        near(starts),
        gain,
        sums0,
    )
    totals = lax.all_to_all(sums, "head", split_axis=0, concat_axis=0, tiled=True)

    grads, send_back = call(
        functools.partial(grads_body, heads, steps, features),
        "grads",
        4,
        in_specs=[vmem] * 5,
        out_specs=[anywhere, anywhere],
        out_shape=[pltpu.HBM((2, length, columns), BF16), pltpu.HBM(pair_shape, F32)],
        scratch_shapes=[
            pair_of_levels(columns),
            pltpu.VMEM(pair_shape, F32),
            dma((2 * steps,)),
            dma((2,)),
        ],
    )(near(lines), near(turned), near(scaled_act), near(gated_act), near(totals))
    got_back = exchange(send_back)

    own_back = lambda k: (0, steps - 1 - k)
    given = call(
        functools.partial(back0_body, heads, steps, features),
        "back0",
        6,
        grid=(steps,),
        in_specs=[
            level_rows(own_back),
            whole(gain),
            pl.BlockSpec(sums_shape, lambda _: (0, 0, 0)),
            tokens(columns, own_back),
            tokens(STATE, own_back),
            tokens(STATE, own_back),
            tokens(columns, own_back),
            flat(columns, own_back),
        ],
        out_specs=[tokens(columns, own_back), state_grads(own_back)],
        out_shape=[pltpu.HBM(ssm_input.shape, BF16), pltpu.HBM(state_shape, F32)],
        scratch_shapes=[state_scratch, packs_scratch, pltpu.VMEM((steps, SPAN, 8), F32)],
    )(far(cum_rows), gain, totals, gate, b, c, out_grad, far(gated0))

    got_back, *given = lax.optimization_barrier((got_back, *given))
    folded = call(
        functools.partial(fold_body, heads),
        "fold",
        1,
        in_specs=[smem, vmem, vmem],
        out_specs=anywhere,
        out_shape=pltpu.HBM(pair_shape, F32),
        scratch_shapes=[pltpu.VMEM(pair_shape, F32), dma((2,))],
    )(parent_ids, near(decays), near(got_back))

    folded, late_rows = lax.optimization_barrier((folded, cum_rows))
    ends = exchange(folded)
    down_back = lambda l, k: (2 - l, steps - 1 - k)
    both_down_back = lambda l, k: (1 - l, steps - 1 - k)
    *given, near_partial, near_state, near_b, near_rows = call(
        functools.partial(back_body, heads, steps),
        "back",
        8,
        grid=(2, steps),
        in_specs=[
            level_rows(down_back),
            flat(columns, both_down_back),
            tokens(STATE, down_back),
            tokens(STATE, down_back),
        ]
        + [anywhere] * 4,
        out_specs=[
            tokens(columns, down_back),
            state_grads(down_back),
            pl.BlockSpec((SPAN, columns), lambda *g: (0, 0)),
            pl.BlockSpec((heads, HDIM, STATE), lambda *g: (0, 0, 0)),
            anywhere,
            anywhere,
        ],
        out_shape=[
            pltpu.HBM(ssm_input.shape, BF16),
            pltpu.HBM(state_shape, F32),
            pltpu.VMEM((SPAN, columns), BF16),
            pltpu.VMEM(state_shape[2:], F32),
            pltpu.VMEM((SPAN, STATE), BF16),
            pltpu.VMEM((2 * steps,) + rows_shape[1:], F32),
        ],
        input_output_aliases={6: 0, 7: 1},
        scratch_shapes=[state_scratch, packs_scratch, dma((2,))],
    )(far(late_rows), far(grads), b, c, b, far(late_rows), *given)

    return call(
        functools.partial(inputs_body, heads, steps),
        "inputs",
        4,
        in_specs=[anywhere] * 3 + [vmem] * 5,
        out_specs=[anywhere, anywhere],
        out_shape=[pltpu.HBM(ssm_input.shape, BF16), pltpu.HBM(state_shape, F32)],
        input_output_aliases={1: 0, 2: 1},
        scratch_shapes=[
            pair_of_levels(STATE),
            pair_of_levels(columns),
            pair_of_levels(columns),
            pltpu.VMEM((2,) + state_shape[2:], F32),
            dma((2 * steps - 1, 2)),
            dma,
            dma((2 * steps,)),
            dma((2,)),
        ],
    )(b, *given, near(near_b), near(near_partial), near(near_state), near(near_rows), near(ends))


def solution(mesh):
    in_specs = (
        P(None, "seg", None, "head"),
        P(None, "seg", None, "head"),
        P(None, "seg", None, None),
        P(None, "seg", None, None),
        P(None, "seg", "head", None),
        P("seg", "head", None, None),
        P("head"),
        P(None, "seg", None, "head"),
        P(),
    )
    out_specs = (P(None, "seg", None, "head"), P(None, "seg", "head", None, None))

    def run(*arrays):
        body = functools.partial(shards, arrays[0].shape[3], mesh.shape["head"])
        return tuple(
            jax.shard_map(
                body, mesh=mesh, in_specs=in_specs, out_specs=out_specs, check_vma=False
            )(*arrays)
        )

    return run
```

```python
import functools
import math

import jax
import jax.numpy as jnp
from jax import lax
from jax.experimental import pallas as pl
from jax.experimental.pallas import tpu as pltpu
from jax.sharding import PartitionSpec as P

BLOCK = 256
HALF = BLOCK // 2
HEADS = 24
HDIM = 128
STATE = 256
CHUNK = 3
SPAN = CHUNK * BLOCK
FIRST = 2 * BLOCK
FOLD = SPAN // 2
EPSILON = 1e-05
VMEM_LIMIT = 24 * 1024 * 1024
LOG2E = math.log2(math.e)

WIDTH = 8 * CHUNK
CUM = 0
FROM_BLOCK = WIDTH
TO_BLOCK = 2 * WIDTH

F32 = jnp.float32
BF16 = jnp.bfloat16
shaped = jax.ShapeDtypeStruct
pin = pltpu.with_memory_space_constraint


def call(body, name, micros, **kwargs):
    return pl.pallas_call(
        body,
        name=name,
        compiler_params=pltpu.CompilerParams(vmem_limit_bytes=VMEM_LIMIT),
        cost_estimate=pl.CostEstimate(
            flops=int(micros * 1e9), bytes_accessed=int(micros * 3e6), transcendentals=0
        ),
        **kwargs,
    )


def whole(array):
    rank = len(array.shape)
    return pl.BlockSpec(array.shape, lambda *_: (0,) * rank)


def dot(left, right, left_dim, right_dim, precision=None):
    return lax.dot_general(
        left,
        right,
        (((left_dim,), (right_dim,)), ((), ())),
        precision=precision,
        preferred_element_type=F32,
    )


def spread(packed, group, j, heads):
    at = group + 8 * j
    return jnp.concatenate(
        [
            jnp.broadcast_to(packed[:, at + h : at + h + 1], (packed.shape[0], HDIM))
            for h in range(heads)
        ],
        axis=1,
    )


def spread_rows(lines, width):
    high = lines.astype(BF16)
    low = (lines - high.astype(F32)).astype(BF16)
    row = lax.broadcasted_iota(jnp.int32, (16, width), 0)
    lane = lax.broadcasted_iota(jnp.int32, (16, width), 1)
    chosen = jnp.where((row & 7) == (lane >> 7), 1.0, 0.0).astype(BF16)
    return dot(jnp.concatenate([high, low], axis=0), chosen, 0, 0)


def block(j):
    return slice(j * BLOCK, (j + 1) * BLOCK)


def head(h):
    return slice(h * HDIM, (h + 1) * HDIM)


def turn(values):
    size = values.shape[0]
    unit = lax.broadcasted_iota(jnp.int32, (size, size), 0) == lax.broadcasted_iota(
        jnp.int32, (size, size), 1
    )
    return dot(jnp.where(unit, 1.0, 0.0).astype(BF16), values, 1, 1)


def silu(values):
    half = 0.5 * values
    return half + half * jnp.tanh(half)


def scatter_pieces(send, number, states):
    rows = STATE // send.shape[0]
    for piece in range(send.shape[0]):
        for h, state in enumerate(states):
            at = (number * len(states) + h) * rows
            send[piece, at : at + rows] = state[piece * rows : (piece + 1) * rows]


def gather_pieces(got, number, h, heads):
    rows = STATE // got.shape[0]
    at = (number * heads + h) * rows
    return got[:, at : at + rows].reshape(STATE, HDIM)


def start_all(copies):
    for copy in copies:
        copy.start()


def wait_all(copies):
    for copy in copies:
        copy.wait()


def part_copies(send, send_out, sems):
    half = send.shape[1] // 16 * 8
    parts = [pl.ds(0, half), pl.ds(half, send.shape[1] - half)]
    return [
        pltpu.make_async_copy(send.at[:, part], send_out.at[:, part], sems.at[i])
        for i, part in enumerate(parts)
    ]


def piece_copies(sources, targets, sems, pieces):
    result = []
    for i, (at, first, count) in enumerate(pieces):
        rows = pl.ds(first * BLOCK, count * BLOCK)
        result.append(
            [
                pltpu.make_async_copy(source(at, rows), target.at[at, rows], sems.at[i, a])
                for a, (source, target) in enumerate(zip(sources, targets))
            ]
        )
    return result


def block_ends(parts):
    lasts = [part[:, BLOCK - 1 :] for part in parts]
    before = [jnp.zeros((8, 1), F32)]
    for last in lasts[:-1]:
        before.append(before[-1] + last)
    after = [jnp.zeros((8, 1), F32)]
    for last in lasts[:0:-1]:
        after.insert(0, after[0] + last)
    return lasts, before, after


def states_body(heads, steps, decay_hbm, root_hbm, x_hbm, b_hbm, send_out, rows_out, rates, rows,
                decay, send, root, x, b, decay_sem, root_sem, sems, out_sem, send_sems):
    blocks = steps * CHUNK
    decay_copy = pltpu.make_async_copy(decay_hbm, decay, decay_sem)
    decay_copy.start()
    pieces = [(0, 0, CHUNK), (0, CHUNK, CHUNK), (1, 0, CHUNK), (1, CHUNK, CHUNK)]
    copies = piece_copies(
        [lambda at, span: x_hbm.at[at, 0, span], lambda at, span: b_hbm.at[at, 0, span]],
        [x, b],
        sems,
        pieces,
    )
    root_copy = pltpu.make_async_copy(root_hbm.at[0], root, root_sem)
    start_all(copies[0])
    root_copy.start()

    rates[...] = jnp.zeros_like(rates)
    upper = (
        lax.broadcasted_iota(jnp.int32, (BLOCK, BLOCK), 0)
        <= lax.broadcasted_iota(jnp.int32, (BLOCK, BLOCK), 1)
    )
    upper = jnp.where(upper, 1.0, 0.0).astype(BF16)
    decay_copy.wait()
    start_all(copies[1])
    for level in range(decay.shape[0]):
        for number in range(blocks):
            for h in range(heads):
                row = 8 * (level * blocks + number) + h
                rates[row : row + 1] = decay[level, h, :, block(number)]
    rest = rates[...]
    sums = jnp.zeros_like(rest)
    for _ in range(3):
        part = rest.astype(BF16)
        rest = rest - part.astype(F32)
        sums = sums + dot(part, upper, 1, 0)
    sums = sums * -LOG2E
    for chunk in range(rows.shape[0]):
        rows[chunk] = sums[WIDTH * chunk : WIDTH * (chunk + 1)]
    rows_copy = pltpu.make_async_copy(rows, rows_out, out_sem)
    rows_copy.start()

    to_level = []
    totals = []
    for level in range(2):
        numbers = range(level * blocks, (level + 1) * blocks)
        parts = [sums[8 * number : 8 * number + 8] for number in numbers]
        lasts, _, after = block_ends(parts)
        for part, last, suffix in zip(parts, lasts, after):
            to_level.append(jnp.exp2(last - part + suffix))
        totals.append(jnp.exp2(after[0] + lasts[0]))

    root_copy.wait()
    states = [(root[h] * totals[0][h : h + 1]).T for h in range(heads)]
    outs = part_copies(send, send_out, send_sems)
    for i, (level, first, count) in enumerate(pieces):
        if (level, first) == (1, 0):
            scatter_pieces(send, 0, states)
            outs[0].start()
            states = [jnp.zeros((STATE, HDIM), F32)] * heads
        wait_all(copies[i])
        if i > 0:
            start_all(sum(copies[i + 1 : i + 2], []))
        numbers = range(first, first + count)
        turned = [turn(b[level, block(number)]) for number in numbers]
        span = slice(first * BLOCK, (first + count) * BLOCK)
        for h in range(heads):
            decayed = [
                (values * to_level[level * blocks + number][h : h + 1]).astype(BF16)
                for number, values in zip(numbers, turned)
            ]
            states[h] = states[h] + dot(
                jnp.concatenate(decayed, axis=1), x[level, span, head(h)], 1, 0
            )
    scatter_pieces(send, 1, states)
    decays = jnp.broadcast_to(totals[1], (8, HDIM))
    for piece in range(send.shape[0]):
        send[piece, send.shape[1] - 8 :] = decays
    outs[1].start()
    wait_all(outs + [rows_copy])


def level_decays(rows, to_end):
    steps = rows.shape[0]
    parts = [rows[step, 8 * j : 8 * j + 8] for step in range(steps) for j in range(CHUNK)]
    lasts, before, after = block_ends(parts)
    if to_end:
        lines = [last - part + end for part, last, end in zip(parts, lasts, after)]
    else:
        lines = [start + part for part, start in zip(parts, before)]
    return [
        jnp.exp2(jnp.concatenate(lines[step * CHUNK : (step + 1) * CHUNK], axis=0))
        for step in range(steps)
    ]


def pack(rows, packed):
    for step in range(packed.shape[0]):
        part = rows[step]
        last = jnp.concatenate(
            [
                jnp.broadcast_to(part[8 * j : 8 * j + 8, BLOCK - 1 :], (8, BLOCK))
                for j in range(CHUNK)
            ],
            axis=0,
        )
        packed[step] = jnp.concatenate(
            [
                part,
                jnp.exp2(part),
                jnp.exp2(last - part),
                jnp.zeros((128 - 3 * WIDTH, BLOCK), F32),
            ],
            axis=0,
        ).T


def pick_body(heads, parent_ref, got_ref, send_out, decay_out, send, sems):
    segments = got_ref.shape[0]
    rows = STATE // segments
    pair = send.shape[1]
    half = pair // 2
    quarter = segments // 4
    copies = []
    for seg in range(segments):
        first = parent_ref[0, seg]
        second = parent_ref[1, seg]
        root = parent_ref[0, second]
        send[seg, :half] = got_ref[first, :half]
        decay = got_ref[second, pair : pair + 8]
        decay_out[seg] = got_ref[seg, pair : pair + 8]
        for h in range(heads):
            a = slice(h * rows, (h + 1) * rows)
            b = slice(half + h * rows, half + (h + 1) * rows)
            send[seg, b] = decay[h : h + 1] * got_ref[root, a] + got_ref[second, b]
        if (seg + 1) % quarter == 0:
            part = pl.ds(seg + 1 - quarter, quarter)
            copies.append(
                pltpu.make_async_copy(send.at[part], send_out.at[part], sems.at[len(copies)])
            )
            copies[-1].start()
    wait_all(copies)


def fold_body(heads, parent_ref, decay_ref, got_ref, send_out, send, sems):
    rows = STATE // got_ref.shape[0]
    half = send.shape[1] // 2
    send[...] = jnp.zeros_like(send)
    for seg in range(got_ref.shape[0]):
        second = parent_ref[1, seg]
        send[second, :half] += got_ref[seg, :half]
    copies = part_copies(send, send_out, sems)
    copies[0].start()
    for seg in range(got_ref.shape[0]):
        first = parent_ref[0, seg]
        decay = decay_ref[seg]
        for h in range(heads):
            a = slice(h * rows, (h + 1) * rows)
            b = slice(half + h * rows, half + (h + 1) * rows)
            send[first, b] += decay[h : h + 1] * send[seg, a] + got_ref[seg, b]
    copies[1].start()
    wait_all(copies)


def causal_mask(transposed):
    first = lax.broadcasted_iota(jnp.int32, (HALF, HALF), 0)
    second = lax.broadcasted_iota(jnp.int32, (HALF, HALF), 1)
    return first <= second if transposed else first >= second


def weighted(heads, j, rows, packed, x, b, c):
    scores = dot(c, b, 1, 1)
    causal = causal_mask(False)
    results = []
    for h in range(heads):
        row = rows[8 * j + h : 8 * j + h + 1]
        col = packed[:, CUM + 8 * j + h : CUM + 8 * j + h + 1]
        first = jnp.where(causal, col[:HALF] - row[:, :HALF], -jnp.inf)
        last = jnp.where(causal, col[HALF:] - row[:, HALF:], -jnp.inf)
        across = col[HALF:] - row[:, :HALF]
        top = jnp.concatenate(
            [(scores[:HALF, :HALF] * jnp.exp2(first)).astype(BF16), jnp.zeros((HALF, HALF), BF16)],
            axis=1,
        )
        bottom = jnp.concatenate(
            [
                (scores[HALF:, :HALF] * jnp.exp2(across)).astype(BF16),
                (scores[HALF:, HALF:] * jnp.exp2(last)).astype(BF16),
            ],
            axis=1,
        )
        results.append(dot(jnp.concatenate([top, bottom], axis=0), x[:, head(h)], 1, 0))
    return jnp.concatenate(results, axis=1)


def weighted_back(heads, j, rows, packed, grad, b, c):
    scores = dot(b, c, 1, 1)
    causal = causal_mask(True)
    results = []
    for h in range(heads):
        row = rows[8 * j + h : 8 * j + h + 1]
        col = packed[:, CUM + 8 * j + h : CUM + 8 * j + h + 1]
        first = jnp.where(causal, row[:, :HALF] - col[:HALF], -jnp.inf)
        last = jnp.where(causal, row[:, HALF:] - col[HALF:], -jnp.inf)
        across = row[:, HALF:] - col[:HALF]
        top = jnp.concatenate(
            [
                (scores[:HALF, :HALF] * jnp.exp2(first)).astype(BF16),
                (scores[:HALF, HALF:] * jnp.exp2(across)).astype(BF16),
            ],
            axis=1,
        )
        bottom = jnp.concatenate(
            [jnp.zeros((HALF, HALF), BF16), (scores[HALF:, HALF:] * jnp.exp2(last)).astype(BF16)],
            axis=1,
        )
        results.append(dot(jnp.concatenate([top, bottom], axis=0), grad[:, head(h)], 1, 0))
    return jnp.concatenate(results, axis=1)


def gated_sums(ssm_out, gate, out_grad, gain):
    act = silu(gate.astype(F32))
    gated = ssm_out * act
    scaled = out_grad.astype(F32) * gain
    ones = jnp.ones((8, gated.shape[1]), BF16)
    squares = dot(ones, (gated * gated).astype(BF16), 1, 1)
    products = dot(ones, (scaled * gated).astype(BF16), 1, 1)
    return gated, scaled * act, gated * act, (squares[:1], products[:1])


def store_sums(sums, step, at, pairs):
    for q in range(2):
        line = jnp.concatenate([pair[q] for pair in pairs], axis=1)
        for half in range(2):
            sums[4 * step + 2 * q + half : 4 * step + 2 * q + half + 1, at : at + FOLD] = line[
                :, half * FOLD : (half + 1) * FOLD
            ]


def norm_rows(total, step, at, features):
    lines = [total[4 * step + i : 4 * step + i + 1, at : at + FOLD] for i in range(4)]
    squares = jnp.concatenate(lines[:2], axis=1) / features
    dots = jnp.concatenate(lines[2:], axis=1) / features
    inv_rms = lax.rsqrt(squares + EPSILON)
    back = inv_rms * inv_rms * inv_rms * dots
    return jnp.concatenate([inv_rms, back, jnp.zeros((6, SPAN), F32)], axis=0)


def ssm_gradient(j, norm, gain, gate, out_grad, gated):
    inv_rms, back = norm[block(j), 0:1], norm[block(j), 1:2]
    grad = inv_rms * (out_grad.astype(F32) * gain) - gated.astype(F32) * back
    return (grad * silu(gate.astype(F32))).astype(BF16)


def forward0_body(heads, steps, rows_ref, root_ref, gain_ref, x_ref, gate_ref, b_ref, c_ref,
                  out_grad_ref, gated_ref, sums_ref, state, packs):
    step = pl.program_id(0)

    @pl.when(step == 0)
    def _():
        pack(rows_ref, packs)
        for h in range(heads):
            state[:, head(h)] = root_ref[0, h].T

    rows, packed = rows_ref[step], packs[step]
    current = state[...]
    pairs = []
    for j in range(CHUNK):
        x, b, c = x_ref[0, 0, block(j)], b_ref[0, 0, block(j)], c_ref[0, 0, block(j)]
        within = weighted(heads, j, rows, packed, x, b, c)
        carried = dot(c, current.astype(BF16), 1, 0) * spread(packed, FROM_BLOCK, j, heads)
        gated, _, _, pair = gated_sums(
            within + carried, gate_ref[0, 0, block(j)], out_grad_ref[0, 0, block(j)], gain_ref[...]
        )
        gated_ref[0, block(j)] = gated.astype(BF16)
        pairs.append(pair)
        decayed = (x.astype(F32) * spread(packed, TO_BLOCK, j, heads)).astype(BF16)
        factor = spread(packed[BLOCK - 1 :], FROM_BLOCK, j, heads)
        current = current * factor + dot(b, decayed, 0, 0)
    state[...] = current
    for part in range(steps):

        @pl.when(step == part)
        def _():
            store_sums(sums_ref, part, 0, pairs)


def local_body(heads, steps, rows_ref, x_ref, b_ref, c_ref, gate_hbm, c_hbm, out_grad_hbm,
               rows_hbm, out_ref, turned_ref, first_ref, gate_out, c_out, out_grad_out, rows_out,
               state, packs, sems):
    level, step = pl.program_id(0), pl.program_id(1)
    span = pl.ds(0, FIRST)
    copies = [
        pltpu.make_async_copy(source, target, sems.at[i])
        for i, (source, target) in enumerate(
            [
                (gate_hbm.at[1, 0, span], gate_out),
                (c_hbm.at[1, 0, span], c_out),
                (out_grad_hbm.at[1, 0, span], out_grad_out),
                (rows_hbm.at[pl.ds(steps, 2 * steps)], rows_out),
            ]
        )
    ]

    @pl.when((level == 0) & (step == 0))
    def _():
        start_all(copies)

    @pl.when(step == 0)
    def _():
        pack(rows_ref, packs)
        state[...] = jnp.zeros_like(state)

    rows, packed = rows_ref[step], packs[step]
    current = state[...]
    for j in range(CHUNK):
        x, b, c = x_ref[0, 0, block(j)], b_ref[0, 0, block(j)], c_ref[0, 0, block(j)]
        within = weighted(heads, j, rows, packed, x, b, c)
        carried = dot(c, current.astype(BF16), 1, 0) * spread(packed, FROM_BLOCK, j, heads)
        out_ref[0, block(j)] = (within + carried).astype(BF16)
        turned_ref[0, :, block(j)] = turn(c).astype(BF16)
        decayed = (x.astype(F32) * spread(packed, TO_BLOCK, j, heads)).astype(BF16)
        factor = spread(packed[BLOCK - 1 :], FROM_BLOCK, j, heads)
        current = current * factor + dot(b, decayed, 0, 0)
    state[...] = current

    @pl.when((level == 0) & (step == 0))
    def _():
        first_ref[...] = out_ref[0, :FIRST]

    @pl.when((level == 1) & (step == steps - 1))
    def _():
        wait_all(copies)


def readout_body(heads, steps, local_hbm, gate_hbm, c_hbm, out_grad_hbm, turned_hbm, local_ref,
                 gate_ref, c_ref, out_grad_ref, rows_ref, start_ref, gain_ref, first_sums_ref,
                 scaled_act, gated_act, turned, lines, sums, local, gate, out_grad, c, sems,
                 turned_sem):
    early = FIRST // BLOCK
    pieces = [(0, early, CHUNK - early)]
    pieces += [(at, step * CHUNK, CHUNK) for at in range(2) for step in range(steps)][1:]
    copies = piece_copies(
        [
            lambda at, span: c_hbm.at[at + 1, 0, span],
            lambda at, span: local_hbm.at[at, span],
            lambda at, span: gate_hbm.at[at + 1, 0, span],
            lambda at, span: out_grad_hbm.at[at + 1, 0, span],
        ],
        [c, local, gate, out_grad],
        sems,
        pieces,
    )
    turned_copy = pltpu.make_async_copy(turned_hbm, turned, turned_sem)
    copies.append([turned_copy])
    start_all(copies[0] + copies[1])
    sums[0, :, :FOLD] = first_sums_ref[...]
    decays = []
    for at in range(2):
        decays += level_decays(rows_ref.at[pl.ds(at * steps, steps)], False)
    columns = []
    for chunk, line in enumerate(decays):
        lines[chunk] = line
        columns.append(line.T)
    pairs = []
    for i, (at, first, count) in enumerate([(0, 0, early)] + pieces):
        if first == 0:
            start = jnp.concatenate(
                [gather_pieces(start_ref, at, h, heads) for h in range(heads)], axis=1
            ).astype(BF16)
        if i == 0:
            refs = [c_ref, local_ref, gate_ref, out_grad_ref]
        else:
            wait_all(copies[i - 1])
            start_all(sum(copies[i + 1 : i + 2], []))
            span = slice(first * BLOCK, (first + count) * BLOCK)
            refs = [buffer.at[at, span] for buffer in (c, local, gate, out_grad)]
        piece = dot(refs[0][...], start, 1, 0)
        for number in range(first, first + count):
            step, j = number // CHUNK, number % CHUNK
            mine = block(number - first)
            carried = piece[mine] * spread(columns[at * steps + step], 0, j, heads)
            place = block(number)
            _, scaled_act[at, place], gated_act[at, place], pair = gated_sums(
                carried + refs[1][mine].astype(F32), refs[2][mine], refs[3][mine], gain_ref[...]
            )
            pairs.append(pair)
            if j == CHUNK - 1:
                store_sums(sums.at[0], step, (at + 1) * FOLD, pairs)
                pairs = []
    for copy in range(1, sums.shape[0]):
        sums[copy] = sums[0]
    turned_copy.wait()


def grads_body(heads, steps, features, lines_ref, turned_ref, scaled_act_ref, gated_act_ref,
               total_ref, grad_out, send_out, grads, send, grad_sems, sems):
    total = jnp.sum(total_ref[...], axis=0)
    sends = part_copies(send, send_out, sems)
    outs = []
    for at in (1, 0):
        for step in range(steps):
            norm = norm_rows(total, step, (at + 1) * FOLD, features)
            for j in range(CHUNK):
                place = block(step * CHUNK + j)
                factors = spread_rows(norm[:, block(j)], 2 * HDIM)
                inv_rms, back = factors[:, :HDIM], factors[:, HDIM:]
                for h in range(heads):
                    grad = inv_rms * scaled_act_ref[at, place, head(h)]
                    grad = grad - back * gated_act_ref[at, place, head(h)]
                    grads[at, place, head(h)] = grad.astype(BF16)
            span = pl.ds(step * SPAN, SPAN)
            outs.append(
                pltpu.make_async_copy(
                    grads.at[at, span], grad_out.at[at, span], grad_sems.at[at * steps + step]
                )
            )
            outs[-1].start()
    for at in (1, 0):
        states = [jnp.zeros((STATE, HDIM), F32)] * heads
        for step in range(steps):
            span = slice(step * SPAN, (step + 1) * SPAN)
            turned = turned_ref[at, :, span].astype(F32)
            lines = lines_ref[at * steps + step]
            for h in range(heads):
                line = jnp.concatenate(
                    [lines[8 * j + h : 8 * j + h + 1] for j in range(CHUNK)], axis=1
                )
                decayed = (turned * line).astype(BF16)
                states[h] = states[h] + dot(decayed, grads[at, span, head(h)], 1, 0)
        scatter_pieces(send, 1 - at, states)
        outs.append(sends[1 - at])
        outs[-1].start()
    wait_all(outs)


def back_chunk(heads, rows, packed, grad_of, b_ref, c_ref, state):
    current = state[...]
    for j in reversed(range(CHUNK)):
        b, c = b_ref[0, 0, block(j)], c_ref[0, 0, block(j)]
        grad = grad_of(j)
        within = weighted_back(heads, j, rows, packed, grad, b, c)
        carried = dot(b, current.astype(BF16), 1, 0) * spread(packed, TO_BLOCK, j, heads)
        yield j, (within + carried).astype(BF16)
        decayed = (grad.astype(F32) * spread(packed, FROM_BLOCK, j, heads)).astype(BF16)
        factor = spread(packed[BLOCK - 1 :], FROM_BLOCK, j, heads)
        current = current * factor + dot(c, decayed, 0, 0)
    state[...] = current


def back0_body(heads, steps, features, rows_ref, gain_ref, total_ref, gate_ref, b_ref, c_ref,
               out_grad_ref, gated_ref, partial_ref, state_grad_ref, state, packs, norms):
    step = steps - 1 - pl.program_id(0)

    @pl.when(step == steps - 1)
    def _():
        pack(rows_ref, packs)
        total = jnp.sum(total_ref[...], axis=0)
        for part in range(steps):
            norms[part] = norm_rows(total, part, 0, features).T
        state[...] = jnp.zeros_like(state)

    norm = norms[step]

    def grad_of(j):
        return ssm_gradient(
            j,
            norm,
            gain_ref[...],
            gate_ref[0, 0, block(j)],
            out_grad_ref[0, 0, block(j)],
            gated_ref[0, block(j)],
        )

    for j, part in back_chunk(heads, rows_ref[step], packs[step], grad_of, b_ref, c_ref, state):
        partial_ref[0, 0, block(j)] = part

    @pl.when(step == 0)
    def _():
        for h in range(heads):
            state_grad_ref[0, 0, h] = state[:, head(h)].T


def back_body(heads, steps, rows_ref, grad_ref, b_ref, c_ref, b_hbm, rows_hbm, given_in,
              given_state, partial_ref, state_grad_ref, near_ref, near_state_ref, b_out, rows_out,
              state, packs, sems):
    level, step = 2 - pl.program_id(0), steps - 1 - pl.program_id(1)
    copies = [
        pltpu.make_async_copy(b_hbm.at[1, 0, pl.ds(0, SPAN)], b_out, sems.at[0]),
        pltpu.make_async_copy(rows_hbm.at[pl.ds(0, 2 * steps)], rows_out, sems.at[1]),
    ]

    @pl.when((level == 2) & (step == steps - 1))
    def _():
        start_all(copies)

    @pl.when(step == steps - 1)
    def _():
        pack(rows_ref, packs)
        state[...] = jnp.zeros_like(state)

    def grad_of(j):
        return grad_ref[0, block(j)]

    for j, part in back_chunk(heads, rows_ref[step], packs[step], grad_of, b_ref, c_ref, state):
        partial_ref[0, 0, block(j)] = part

    @pl.when(step == 0)
    def _():
        for h in range(heads):
            state_grad_ref[0, 0, h] = state[:, head(h)].T

    @pl.when((level == 1) & (step == 0))
    def _():
        near_ref[...] = partial_ref[0, 0]
        near_state_ref[...] = state_grad_ref[0, 0]
        wait_all(copies)


def inputs_body(heads, steps, b_hbm, partial_hbm, local_hbm, b_ref, partial_ref, local_ref,
                rows_ref, end_ref, input_grad_out, state_grad_out, b, partial, grads, states, sems,
                local_sem, out_sems, state_sems):
    chunks = [(level, step) for level in (1, 0) for step in range(steps)]
    pieces = [(level, step * CHUNK, CHUNK) for level, step in chunks[1:]]
    copies = piece_copies(
        [lambda at, span: b_hbm.at[at, 0, span], lambda at, span: partial_hbm.at[at, 0, span]],
        [b, partial],
        sems,
        pieces,
    )
    local_copy = pltpu.make_async_copy(local_hbm.at[0, 0], states.at[0], local_sem)
    start_all(copies[0])
    local_copy.start()
    for some in copies[1:]:
        start_all(some)
    outs = []
    for i, (level, step) in enumerate(chunks):
        if step == 0:
            ends = [gather_pieces(end_ref, 1 - level, h, heads) for h in range(heads)]
            rounded = jnp.concatenate(ends, axis=1).astype(BF16)
            level_rows = rows_ref.at[pl.ds(level * steps, steps)]
            decays = level_decays(level_rows, True)
            total = level_decays(level_rows, False)[-1][8 * (CHUNK - 1) :, BLOCK - 1 :]
            if level == 0:
                local_copy.wait()
            for h in range(heads):
                local = local_ref[h] if level == 1 else states[0, h]
                states[level, h] = local + (ends[h] * total[h : h + 1]).T
            outs.append(
                pltpu.make_async_copy(
                    states.at[level], state_grad_out.at[level, 0], state_sems.at[level]
                )
            )
            outs[-1].start()
        span = slice(step * SPAN, (step + 1) * SPAN)
        if i == 0:
            some_b, some_partial = b_ref, partial_ref
        else:
            wait_all(copies[i - 1])
            some_b, some_partial = b.at[level, span], partial.at[level, span]
        piece = dot(some_b[...], rounded, 1, 0)
        for j in range(CHUNK):
            line = decays[step][8 * j : 8 * j + 8]
            extra = piece[block(j)] * spread_rows(line, heads * HDIM)
            grads[level, block(step * CHUNK + j)] = (
                some_partial[block(j)].astype(F32) + extra
            ).astype(BF16)
            span = pl.ds((step * CHUNK + j) * BLOCK, BLOCK)
            outs.append(
                pltpu.make_async_copy(
                    grads.at[level, span],
                    input_grad_out.at[level, 0, span],
                    out_sems.at[i * CHUNK + j],
                )
            )
            outs[-1].start()
    wait_all(outs)


def shards(features, head_devices, ssm_input, gate_input, b_input, c_output, log_decay,
           root_state, norm_gain, out_grad, parent_ids):
    levels, _, length, columns = ssm_input.shape
    heads = columns // HDIM
    blocks = length // BLOCK
    steps = blocks // CHUNK
    segments = parent_ids.shape[1]
    rows = STATE // segments
    gain = norm_gain.reshape(1, columns)
    decay = jnp.transpose(log_decay, (0, 2, 1, 3))

    smem = pl.BlockSpec(memory_space=pltpu.SMEM)
    vmem = pl.BlockSpec(memory_space=pltpu.VMEM)
    anywhere = pl.BlockSpec(memory_space=pl.ANY)
    rows_shape = (levels * steps, WIDTH, BLOCK)
    pair_shape = (segments, 2 * heads * rows, HDIM)
    first_shape = (segments, 2 * heads * rows + 8, HDIM)
    sums_shape = (head_devices, 8, levels * FOLD)
    state_shape = (levels, 1, heads, HDIM, STATE)
    state_scratch = pltpu.VMEM((STATE, columns), F32)
    packs_scratch = pltpu.VMEM((steps, BLOCK, 128), F32)
    dma = pltpu.SemaphoreType.DMA

    far = lambda array: pin(array, pltpu.HBM)
    near = lambda array: pin(array, pltpu.VMEM)
    x, gate, out_grad = far(ssm_input), far(gate_input), far(out_grad)
    decay = far(decay)
    b, c, root = far(b_input), far(c_output), far(root_state)

    def pair_of_levels(width):
        return pltpu.VMEM((2, length, width), BF16)

    def tokens(width, place):
        return pl.BlockSpec((1, 1, SPAN, width), lambda *g: (place(*g)[0], 0, place(*g)[1], 0))

    def flat(width, place):
        return pl.BlockSpec((1, SPAN, width), lambda *g: (*place(*g), 0))

    def level_rows(place):
        return pl.BlockSpec((steps,) + rows_shape[1:], lambda *g: (place(*g)[0], 0, 0))

    def state_grads(place):
        return pl.BlockSpec((1, 1, heads, HDIM, STATE), lambda *g: (place(*g)[0], 0, 0, 0, 0))

    exchange = functools.partial(
        lax.all_to_all, axis_name="seg", split_axis=0, concat_axis=0, tiled=True
    )

    send, cum_rows = call(
        functools.partial(states_body, heads, steps),
        "states",
        6,
        in_specs=[anywhere] * 4,
        out_specs=[anywhere, anywhere],
        out_shape=[pltpu.HBM(first_shape, F32), pltpu.HBM(rows_shape, F32)],
        scratch_shapes=[
            pltpu.VMEM((levels * blocks * 8, BLOCK), F32),
            pltpu.VMEM(rows_shape, F32),
            pltpu.VMEM(decay.shape, F32),
            pltpu.VMEM(first_shape, F32),
            pltpu.VMEM(root_state.shape[1:], F32),
            pair_of_levels(columns),
            pair_of_levels(STATE),
            dma,
            dma,
            dma((4, 2)),
            dma,
            dma((2,)),
        ],
    )(decay, root, x, b)
    got = exchange(send)

    own = lambda k: (0, k)
    gated0, sums0 = call(
        functools.partial(forward0_body, heads, steps),
        "forward0",
        6,
        grid=(steps,),
        in_specs=[
            level_rows(own),
            whole(root_state),
            whole(gain),
            tokens(columns, own),
            tokens(columns, own),
            tokens(STATE, own),
            tokens(STATE, own),
            tokens(columns, own),
        ],
        out_specs=[flat(columns, own), pl.BlockSpec((8, FOLD), lambda _: (0, 0))],
        out_shape=[pltpu.HBM((1, length, columns), BF16), pltpu.HBM((8, FOLD), F32)],
        scratch_shapes=[state_scratch, packs_scratch],
    )(far(cum_rows), root, gain, x, gate, b, c, out_grad)

    got, sums0 = lax.optimization_barrier((got, sums0))
    picked, decays = call(
        functools.partial(pick_body, heads),
        "pick",
        1,
        in_specs=[smem, vmem],
        out_specs=[anywhere, vmem],
        out_shape=[pltpu.HBM(pair_shape, F32), pltpu.VMEM((segments, 8, HDIM), F32)],
        scratch_shapes=[pltpu.VMEM(pair_shape, F32), dma((4,))],
    )(parent_ids, near(got))

    picked, late_rows = lax.optimization_barrier((picked, cum_rows))
    starts = exchange(picked)
    both = lambda l, k: (l, k)
    later = lambda l, k: (l + 1, k)
    local, turned, *first = call(
        functools.partial(local_body, heads, steps),
        "local",
        7,
        grid=(2, steps),
        in_specs=[
            level_rows(later),
            tokens(columns, later),
            tokens(STATE, later),
            tokens(STATE, later),
        ]
        + [anywhere] * 4,
        out_specs=[
            flat(columns, both),
            pl.BlockSpec((1, STATE, SPAN), lambda l, k: (l, 0, k)),
            pl.BlockSpec((FIRST, columns), lambda l, k: (0, 0)),
        ]
        + [anywhere] * 4,
        out_shape=[
            pltpu.HBM((2, length, columns), BF16),
            pltpu.HBM((2, STATE, length), BF16),
            pltpu.VMEM((FIRST, columns), BF16),
            pltpu.VMEM((FIRST, columns), BF16),
            pltpu.VMEM((FIRST, STATE), BF16),
            pltpu.VMEM((FIRST, columns), BF16),
            pltpu.VMEM((2 * steps,) + rows_shape[1:], F32),
        ],
        scratch_shapes=[state_scratch, packs_scratch, dma((4,))],
    )(far(late_rows), x, b, c, gate, c, out_grad, far(late_rows))

    scaled_act, gated_act, turned, lines, sums = call(
        functools.partial(readout_body, heads, steps),
        "readout",
        5,
        in_specs=[anywhere] * 5 + [vmem] * 8,
        out_specs=[vmem] * 5,
        out_shape=[
            pltpu.VMEM((2, length, columns), F32),
            pltpu.VMEM((2, length, columns), F32),
            pltpu.VMEM((2, STATE, length), BF16),
            pltpu.VMEM((2 * steps,) + rows_shape[1:], F32),
            pltpu.VMEM(sums_shape, F32),
        ],
        scratch_shapes=[
            pair_of_levels(columns),
            pair_of_levels(columns),
            pair_of_levels(columns),
            pair_of_levels(STATE),
            dma((2 * steps, 4)),
            dma,
        ],
    )(
        far(local),
        gate,
        c,
        out_grad,
        far(turned),
        near(first[0]),
        near(first[1]),
        near(first[2]),
        near(first[3]),
        near(first[4]),
        near(starts),
        gain,
        sums0,
    )
    totals = lax.all_to_all(sums, "head", split_axis=0, concat_axis=0, tiled=True)

    grads, send_back = call(
        functools.partial(grads_body, heads, steps, features),
        "grads",
        4,
        in_specs=[vmem] * 5,
        out_specs=[anywhere, anywhere],
        out_shape=[pltpu.HBM((2, length, columns), BF16), pltpu.HBM(pair_shape, F32)],
        scratch_shapes=[
            pair_of_levels(columns),
            pltpu.VMEM(pair_shape, F32),
            dma((2 * steps,)),
            dma((2,)),
        ],
    )(near(lines), near(turned), near(scaled_act), near(gated_act), near(totals))
    got_back = exchange(send_back)

    own_back = lambda k: (0, steps - 1 - k)
    given = call(
        functools.partial(back0_body, heads, steps, features),
        "back0",
        6,
        grid=(steps,),
        in_specs=[
            level_rows(own_back),
            whole(gain),
            pl.BlockSpec(sums_shape, lambda _: (0, 0, 0)),
            tokens(columns, own_back),
            tokens(STATE, own_back),
            tokens(STATE, own_back),
            tokens(columns, own_back),
            flat(columns, own_back),
        ],
        out_specs=[tokens(columns, own_back), state_grads(own_back)],
        out_shape=[pltpu.HBM(ssm_input.shape, BF16), pltpu.HBM(state_shape, F32)],
        scratch_shapes=[state_scratch, packs_scratch, pltpu.VMEM((steps, SPAN, 8), F32)],
    )(far(cum_rows), gain, totals, gate, b, c, out_grad, far(gated0))

    got_back, *given = lax.optimization_barrier((got_back, *given))
    folded = call(
        functools.partial(fold_body, heads),
        "fold",
        1,
        in_specs=[smem, vmem, vmem],
        out_specs=anywhere,
        out_shape=pltpu.HBM(pair_shape, F32),
        scratch_shapes=[pltpu.VMEM(pair_shape, F32), dma((2,))],
    )(parent_ids, near(decays), near(got_back))

    folded, late_rows = lax.optimization_barrier((folded, cum_rows))
    ends = exchange(folded)
    down_back = lambda l, k: (2 - l, steps - 1 - k)
    both_down_back = lambda l, k: (1 - l, steps - 1 - k)
    *given, near_partial, near_state, near_b, near_rows = call(
        functools.partial(back_body, heads, steps),
        "back",
        8,
        grid=(2, steps),
        in_specs=[
            level_rows(down_back),
            flat(columns, both_down_back),
            tokens(STATE, down_back),
            tokens(STATE, down_back),
        ]
        + [anywhere] * 4,
        out_specs=[
            tokens(columns, down_back),
            state_grads(down_back),
            pl.BlockSpec((SPAN, columns), lambda *g: (0, 0)),
            pl.BlockSpec((heads, HDIM, STATE), lambda *g: (0, 0, 0)),
            anywhere,
            anywhere,
        ],
        out_shape=[
            pltpu.HBM(ssm_input.shape, BF16),
            pltpu.HBM(state_shape, F32),
            pltpu.VMEM((SPAN, columns), BF16),
            pltpu.VMEM(state_shape[2:], F32),
            pltpu.VMEM((SPAN, STATE), BF16),
            pltpu.VMEM((2 * steps,) + rows_shape[1:], F32),
        ],
        input_output_aliases={6: 0, 7: 1},
        scratch_shapes=[state_scratch, packs_scratch, dma((2,))],
    )(far(late_rows), far(grads), b, c, b, far(late_rows), *given)

    return call(
        functools.partial(inputs_body, heads, steps),
        "inputs",
        4,
        in_specs=[anywhere] * 3 + [vmem] * 5,
        out_specs=[anywhere, anywhere],
        out_shape=[pltpu.HBM(ssm_input.shape, BF16), pltpu.HBM(state_shape, F32)],
        input_output_aliases={1: 0, 2: 1},
        scratch_shapes=[
            pair_of_levels(STATE),
            pair_of_levels(columns),
            pair_of_levels(columns),
            pltpu.VMEM((2,) + state_shape[2:], F32),
            dma((2 * steps - 1, 2)),
            dma,
            dma((2 * blocks,)),
            dma((2,)),
        ],
    )(b, *given, near(near_b), near(near_partial), near(near_state), near(near_rows), near(ends))


def solution(mesh):
    in_specs = (
        P(None, "seg", None, "head"),
        P(None, "seg", None, "head"),
        P(None, "seg", None, None),
        P(None, "seg", None, None),
        P(None, "seg", "head", None),
        P("seg", "head", None, None),
        P("head"),
        P(None, "seg", None, "head"),
        P(),
    )
    out_specs = (P(None, "seg", None, "head"), P(None, "seg", "head", None, None))

    def run(*arrays):
        body = functools.partial(shards, arrays[0].shape[3], mesh.shape["head"])
        return tuple(
            jax.shard_map(
                body, mesh=mesh, in_specs=in_specs, out_specs=out_specs, check_vma=False
            )(*arrays)
        )

    return run
```
